512 devices in a mesh: smp: 8 (over x, y_hi), proto: 64 (over y_lo, z, core).
Axes of the slice: x: 4, y: 8 (y_hi: 2, y_lo: 4; y = y_hi * 4 + y_lo), z: 8, core: 2. Of those that a mesh axis runs over, the one named last changes fastest.
Arguments:
- teacher_features: bfloat16 [1024, 512], P('smp', 'proto'), may hold values from -6 to 6
- student_features: bfloat16 [1024, 512], P('smp', 'proto'), may hold values from -6 to 6
- teacher_weight: bfloat16 [131072, 512], P('proto'), may hold values from -0.45 to 0.45
- student_weight: bfloat16 [131072, 512], P('proto'), may hold values from -0.19921875 to 0.19921875
Outputs:
- sample_loss: float32 [1024], P('smp')
- grad_features: float32 [1024, 512], P('smp', 'proto')
- grad_weight: float32 [131072, 512], P('proto', 'smp')
The draws below stay inside these ranges and needn't reach their ends.
All inputs are finite; a program needn't handle non-finite values.
Results may differ from the reference program's by a relative error of at most 0.0085.
Values may be sent and summed in bfloat16 or wider, within the bound.
No kernel may reach another device: no remote copies, remote signals or barrier semaphores. Data moves between devices by JAX's collectives and lax.ppermute only.
A program may use at most 64 MiB of HBM per device.

```python
import math
import jax
import jax.numpy as jnp
from jax import lax

D = 512
K = 131072
B_DEV = 128
ITERS = 3
B = 1024
N_SMP = 8


cluster_count = 4


center_gain = 0.3


noise_level = 0.07


student_gain = 0.15


student_noise = 0.05


student_bound = 0.19921875


def cluster_centers(key):
    raw = jax.random.normal(jax.random.fold_in(key, 7101), (cluster_count, D), jnp.float32)
    return raw / jnp.sqrt(jnp.sum(raw * raw, axis=1, keepdims=True))


def spread_centers(labels, centers):
    onehot = (labels[:, None] == jnp.arange(cluster_count, dtype=jnp.int32)[None, :]).astype(jnp.float32)
    return jnp.dot(onehot, centers, precision=lax.Precision.HIGHEST)


def sample_labels(key):
    blocks = B // B_DEV
    dominant = jax.random.randint(jax.random.fold_in(key, 7707), (blocks,), 0, cluster_count).astype(jnp.int32)
    ticket = jax.random.randint(jax.random.fold_in(key, 7202), (B,), 0, 20).astype(jnp.int32)
    offset = jax.random.randint(jax.random.fold_in(key, 7808), (B,), 1, cluster_count).astype(jnp.int32)
    block_of = jnp.arange(B, dtype=jnp.int32) // B_DEV
    leader = dominant[block_of]
    return jnp.where(ticket < 15, leader, (leader + offset) % cluster_count).astype(jnp.int32)


def prototype_labels(key):
    ticket = jax.random.randint(jax.random.fold_in(key, 7505), (K,), 0, 10).astype(jnp.int32)
    return (ticket >= 1).astype(jnp.int32) + (ticket >= 3).astype(jnp.int32) + (ticket >= 6).astype(jnp.int32)


def feature_rows(key, noise_fold):
    centers = cluster_centers(key)
    anchor = spread_centers(sample_labels(key), centers) * math.sqrt(D)
    noise_key = jax.random.fold_in(key, noise_fold)
    noise = jnp.clip(jax.random.normal(noise_key, (B, D), jnp.float32), -4.0, 4.0)
    mixed = math.sqrt(0.5) * anchor + math.sqrt(0.5) * noise
    return jnp.clip(mixed, -6.0, 6.0)


def draw_teacher_features(key, part):
    return feature_rows(key, 7303).astype(jnp.bfloat16)


def draw_student_features(key, part):
    return feature_rows(key, 8101).astype(jnp.bfloat16)


def draw_teacher_weight(key, part):
    centers = cluster_centers(key)
    anchor = spread_centers(prototype_labels(key), centers) * center_gain
    noise_key = jax.random.fold_in(key, 7606)
    noise = jnp.clip(noise_level * jax.random.normal(noise_key, (K, D), jnp.float32), -0.3, 0.3)
    return jnp.clip(anchor + noise, -0.45, 0.45).astype(jnp.bfloat16)


def draw_student_weight(key, part):
    centers = cluster_centers(key)
    anchor = spread_centers(prototype_labels(key), centers) * student_gain
    noise_key = jax.random.fold_in(key, 8303)
    noise = jnp.clip(student_noise * jax.random.normal(noise_key, (K, D), jnp.float32), -0.18, 0.18)
    return jnp.clip(anchor + noise, -student_bound, student_bound).astype(jnp.bfloat16)


def setup_inputs(seed: int = 0) -> dict:
    keys = jax.random.split(jax.random.key(seed), 5)
    return {
        "teacher_features": draw_teacher_features(jax.random.fold_in(keys[4], 71), 0),
        "student_features": draw_student_features(jax.random.fold_in(keys[4], 71), 0),
        "teacher_weight": draw_teacher_weight(jax.random.fold_in(keys[4], 71), 0),
        "student_weight": draw_student_weight(jax.random.fold_in(keys[4], 71), 0),
    }


TEACHER_TEMP = 0.07
STUDENT_TEMP = 0.1

def unit_rows(features):
    values = features.astype(jnp.float32)
    scale = lax.rsqrt(lax.optimization_barrier(jnp.sum(values * values, axis=1)) + 1e-06)
    return ((values * scale[:, None]).astype(jnp.bfloat16), scale)

def project(rows, weight):
    return lax.dot_general(rows, weight, (((1,), (1,)), ((), ())), preferred_element_type=jnp.float32)

def reference(teacher_features, student_features, teacher_weight, student_weight):
    samples = teacher_features.shape[0]
    protos = teacher_weight.shape[0]
    teacher_unit, unused = unit_rows(teacher_features)
    student_unit, student_scale = unit_rows(student_features)
    kernel = jnp.exp(project(teacher_unit, teacher_weight) / TEACHER_TEMP)
    col_scale = jnp.ones((samples,), jnp.float32)
    row_scale = jnp.ones((protos,), jnp.float32)
    for step in range(ITERS):
        row_scale = 1.0 / (protos * jnp.dot(col_scale, kernel, precision=lax.Precision.HIGHEST))
        col_scale = 1.0 / (samples * jnp.dot(kernel, row_scale, precision=lax.Precision.HIGHEST))
    block_rows = samples // N_SMP

    def one_block(weight_total, block_index):
        start = (block_index * block_rows).astype(jnp.int32)
        kernel_block = lax.dynamic_slice_in_dim(kernel, start, block_rows, 0)
        unit_block = lax.dynamic_slice_in_dim(student_unit, start, block_rows, 0)
        scale_block = lax.dynamic_slice_in_dim(student_scale, start, block_rows, 0)
        col_block = lax.dynamic_slice_in_dim(col_scale, start, block_rows, 0)
        feats = lax.dynamic_slice_in_dim(student_features, start, block_rows, 0).astype(jnp.float32)
        targets = samples * kernel_block * row_scale[None, :] * col_block[:, None]
        logits = project(unit_block, student_weight) / STUDENT_TEMP
        expo = jnp.exp(logits)
        totals = lax.optimization_barrier(jnp.sum(expo, axis=1))
        weighted = lax.optimization_barrier(jnp.sum(targets * logits, axis=1))
        probs = expo / totals[:, None]
        loss_block = jnp.log(totals) - weighted
        logit_grad = ((probs - targets) / (samples * STUDENT_TEMP)).astype(jnp.bfloat16)
        unit_grad = jnp.dot(logit_grad, student_weight, preferred_element_type=jnp.float32)
        inner_prod = lax.optimization_barrier(jnp.sum(feats * unit_grad, axis=1))
        grad_block = scale_block[:, None] * unit_grad - (scale_block ** 3 * inner_prod)[:, None] * feats
        weight_part = lax.dot_general(logit_grad, unit_block, (((0,), (0,)), ((), ())), preferred_element_type=jnp.float32)
        weight_total = weight_total + weight_part.astype(jnp.bfloat16).astype(jnp.float32)
        return (weight_total, (loss_block, grad_block))
    start_carry = jnp.zeros(student_weight.shape, jnp.float32)
    grad_weight, (loss_blocks, grad_blocks) = lax.scan(one_block, start_carry, jnp.arange(N_SMP, dtype=jnp.int32))
    grad_features = grad_blocks.reshape(student_features.shape)
    return (loss_blocks.reshape((samples,)), grad_features, grad_weight)
```

```python
import jax
import jax.numpy as jnp
import numpy as np
from jax import lax
from jax.sharding import PartitionSpec as P

ITERS = 3
TEACHER_TEMP = 0.07
STUDENT_TEMP = 0.1
BOTH = ("smp", "proto")
PARTS = {"x": 4, "yh": 2, "yl": 4, "z": 8, "c": 2}


def groups(names):
    order = list(PARTS)
    index = np.arange(512).reshape(tuple(PARTS.values()))
    inner = [order.index(n) for n in names]
    outer = [i for i in range(len(order)) if i not in inner]
    size = int(np.prod([PARTS[n] for n in names]))
    return index.transpose(outer + inner).reshape(-1, size).tolist()


def gathered(x, names):
    group = groups(names)
    copies = jnp.broadcast_to(x[None], (len(group[0]), *x.shape))
    return lax.all_to_all(copies, BOTH, 0, 0, tiled=True, axis_index_groups=group)


def sent_to_protos(x):
    return lax.all_to_all(jnp.broadcast_to(x[None], (64, *x.shape)), "proto", 0, 0, tiled=True)


def unit_columns(features):
    values = features.astype(jnp.float32)
    scale = lax.rsqrt(jnp.sum(values * values, axis=0) + 1e-06)
    return (values * scale[None, :]).astype(jnp.bfloat16), scale


def on_device(teacher_features, student_features, teacher_weight, student_weight):
    f32, bf16 = jnp.float32, jnp.bfloat16
    me = lax.axis_index("smp")
    samples, protos = 1024, 131072
    raw = jnp.concatenate([teacher_features.T, student_features.T], axis=0)
    first = gathered(raw, ("yh", "yl", "z"))
    teacher_1, student_1 = first[:, :8], first[:, 8:]
    teacher_2 = gathered(teacher_1, ("x",))
    teacher_2, student_1 = lax.optimization_barrier((teacher_2, student_1))
    teacher_3 = gathered(teacher_2, ("c",))
    teacher_all = teacher_3.reshape(2, 4, 2, 4, 8, 8, 128).transpose(3, 4, 0, 5, 1, 2, 6).reshape(512, 1024)
    student_2 = lax.all_gather(
        student_1.reshape(512, 128), BOTH, axis=0, tiled=True, axis_index_groups=groups(("x", "c"))
    )
    student_all = student_2.reshape(4, 2, 2, 4, 8, 8, 128).transpose(3, 4, 1, 5, 0, 2, 6).reshape(512, 1024)

    teacher_unit, unused = unit_columns(teacher_all)
    kernel = jnp.exp(jnp.dot(teacher_weight, teacher_unit, preferred_element_type=f32) / TEACHER_TEMP)
    student_unit, student_scale = unit_columns(student_all)
    logits = jnp.dot(student_weight, student_unit, preferred_element_type=f32) / STUDENT_TEMP
    expo = jnp.exp(logits)
    local_total = jnp.sum(expo, axis=0)

    col_scale = jnp.ones((samples,), f32)
    for step in range(ITERS):
        row_scale = 1.0 / (protos * jnp.sum(kernel * col_scale[None, :], axis=1))
        part = jnp.sum(kernel * row_scale[:, None], axis=0)
        if step < ITERS - 1:
            mass = jnp.sum(sent_to_protos(part.reshape(8, 128)), axis=0).reshape(-1)
        else:
            kernel_own = lax.dynamic_slice_in_dim(kernel, me * 128, 128, 1)
            logits_own = lax.dynamic_slice_in_dim(logits, me * 128, 128, 1)
            weighted = jnp.sum(kernel_own * row_scale[:, None] * logits_own, axis=0)
            packed = jnp.concatenate([part, local_total, weighted]).reshape(17, 128)
            sums = jnp.sum(sent_to_protos(packed), axis=0)
            mass, total, weighted = sums[:8].reshape(-1), sums[8:16].reshape(-1), sums[16]
        col_scale = 1.0 / (samples * mass)
    targets = samples * kernel * row_scale[:, None] * col_scale[None, :]
    logit_grad = ((expo / total[None, :] - targets) / (samples * STUDENT_TEMP)).astype(bf16)

    total_own = lax.dynamic_slice_in_dim(total, me * 128, 128)
    col_own = lax.dynamic_slice_in_dim(col_scale, me * 128, 128)
    sample_loss = jnp.log(total_own) - samples * col_own * weighted

    grad_own = lax.dynamic_slice_in_dim(logit_grad, me * 128, 128, 1)
    features_own = lax.dynamic_slice_in_dim(student_all, me * 128, 128, 1).astype(f32)
    scale_own = lax.dynamic_slice_in_dim(student_scale, me * 128, 128)
    unit_part = lax.dot_general(
        student_weight, grad_own, (((0,), (0,)), ((), ())), preferred_element_type=f32
    )
    inner_part = jnp.sum(features_own * unit_part, axis=0)
    pieces = jnp.concatenate(
        [unit_part.reshape(64, 8, 128), jnp.broadcast_to(inner_part[None, None], (64, 1, 128))], axis=1
    )
    unit_sums = jnp.sum(lax.all_to_all(pieces, "proto", 0, 0, tiled=True), axis=0)
    unit_grad, inner_prod = unit_sums[:8], unit_sums[8]
    feats = student_features.T.astype(f32)
    grad_features = scale_own[None] * unit_grad - (scale_own**3 * inner_prod)[None] * feats

    unit_slice = lax.dynamic_slice_in_dim(student_unit, me * 64, 64, 0)
    grad_weight = lax.dot_general(
        unit_slice, logit_grad, (((1,), (1,)), ((), ())), preferred_element_type=f32
    )
    return sample_loss, grad_features.T, grad_weight.T


def solution(mesh):
    placed = (P("smp", "proto"), P("smp", "proto"), P("proto", None), P("proto", None))
    return jax.shard_map(
        on_device,
        mesh=mesh,
        in_specs=placed,
        out_specs=(P("smp"), P("smp", "proto"), P("proto", "smp")),
        check_vma=False,
    )
```

```python
import jax
import jax.numpy as jnp
import numpy as np
from jax import lax
from jax.sharding import PartitionSpec as P

ITERS = 3
TEACHER_TEMP = 0.07
STUDENT_TEMP = 0.1
BOTH = ("smp", "proto")
PARTS = {"x": 4, "yh": 2, "yl": 4, "z": 8, "c": 2}


def groups(names):
    order = list(PARTS)
    index = np.arange(512).reshape(tuple(PARTS.values()))
    inner = [order.index(n) for n in names]
    outer = [i for i in range(len(order)) if i not in inner]
    size = int(np.prod([PARTS[n] for n in names]))
    return index.transpose(outer + inner).reshape(-1, size).tolist()


def gathered(x, names):
    group = groups(names)
    copies = jnp.broadcast_to(x[None], (len(group[0]), *x.shape))
    return lax.all_to_all(copies, BOTH, 0, 0, tiled=True, axis_index_groups=group)


def sent_to_protos(x):
    return lax.all_to_all(jnp.broadcast_to(x[None], (64, *x.shape)), "proto", 0, 0, tiled=True)


def unit_columns(features):
    values = features.astype(jnp.float32)
    scale = lax.rsqrt(jnp.sum(values * values, axis=0) + 1e-06)
    return (values * scale[None, :]).astype(jnp.bfloat16), scale


def on_device(teacher_features, student_features, teacher_weight, student_weight):
    f32, bf16 = jnp.float32, jnp.bfloat16
    me = lax.axis_index("smp")
    samples, protos = 1024, 131072
    raw = jnp.concatenate([teacher_features.T, student_features.T], axis=0)
    first = gathered(raw, ("yh", "yl", "z"))
    second = gathered(first, ("x",))
    third = gathered(second, ("c",)).reshape(2, 4, 2, 4, 8, 2, 8, 128)
    both = third.transpose(5, 3, 4, 0, 6, 1, 2, 7).reshape(2, 512, 1024)
    teacher_all, student_all = both[0], both[1]

    teacher_unit, unused = unit_columns(teacher_all)
    kernel = jnp.exp(jnp.dot(teacher_weight, teacher_unit, preferred_element_type=f32) / TEACHER_TEMP)
    student_unit, student_scale = unit_columns(student_all)
    logits = jnp.dot(student_weight, student_unit, preferred_element_type=f32) / STUDENT_TEMP
    expo = jnp.exp(logits)
    local_total = jnp.sum(expo, axis=0)

    col_scale = jnp.ones((samples,), f32)
    for step in range(ITERS):
        row_scale = 1.0 / (protos * jnp.sum(kernel * col_scale[None, :], axis=1))
        part = jnp.sum(kernel * row_scale[:, None], axis=0)
        if step < ITERS - 1:
            mass = jnp.sum(sent_to_protos(part.reshape(8, 128)), axis=0).reshape(-1)
        else:
            kernel_own = lax.dynamic_slice_in_dim(kernel, me * 128, 128, 1)
            logits_own = lax.dynamic_slice_in_dim(logits, me * 128, 128, 1)
            weighted = jnp.sum(kernel_own * row_scale[:, None] * logits_own, axis=0)
            packed = jnp.concatenate([part, local_total, weighted]).reshape(17, 128)
            sums = jnp.sum(sent_to_protos(packed), axis=0)
            mass, total, weighted = sums[:8].reshape(-1), sums[8:16].reshape(-1), sums[16]
        col_scale = 1.0 / (samples * mass)
    targets = samples * kernel * row_scale[:, None] * col_scale[None, :]
    logit_grad = ((expo / total[None, :] - targets) / (samples * STUDENT_TEMP)).astype(bf16)

    total_own = lax.dynamic_slice_in_dim(total, me * 128, 128)
    col_own = lax.dynamic_slice_in_dim(col_scale, me * 128, 128)
    sample_loss = jnp.log(total_own) - samples * col_own * weighted

    grad_own = lax.dynamic_slice_in_dim(logit_grad, me * 128, 128, 1)
    features_own = lax.dynamic_slice_in_dim(student_all, me * 128, 128, 1).astype(f32)
    scale_own = lax.dynamic_slice_in_dim(student_scale, me * 128, 128)
    unit_part = lax.dot_general(
        student_weight, grad_own, (((0,), (0,)), ((), ())), preferred_element_type=f32
    )
    inner_part = jnp.sum(features_own * unit_part, axis=0)
    pieces = jnp.concatenate(
        [unit_part.reshape(64, 8, 128), jnp.broadcast_to(inner_part[None, None], (64, 1, 128))], axis=1
    )
    unit_sums = jnp.sum(lax.all_to_all(pieces, "proto", 0, 0, tiled=True), axis=0)
    unit_grad, inner_prod = unit_sums[:8], unit_sums[8]
    feats = student_features.T.astype(f32)
    grad_features = scale_own[None] * unit_grad - (scale_own**3 * inner_prod)[None] * feats

    unit_slice = lax.dynamic_slice_in_dim(student_unit, me * 64, 64, 0)
    grad_weight = lax.dot_general(
        unit_slice, logit_grad, (((1,), (1,)), ((), ())), preferred_element_type=f32
    )
    return sample_loss, grad_features.T, grad_weight.T


def solution(mesh):
    placed = (P("smp", "proto"), P("smp", "proto"), P("proto", None), P("proto", None))
    return jax.shard_map(
        on_device,
        mesh=mesh,
        in_specs=placed,
        out_specs=(P("smp"), P("smp", "proto"), P("proto", "smp")),
        check_vma=False,
    )
```

```python
import jax
import jax.numpy as jnp
import numpy as np
from jax import lax
from jax.experimental import pallas as pl
from jax.experimental.pallas import tpu as pltpu
from jax.sharding import PartitionSpec as P

ITERS = 3
TEACHER_TEMP = 0.07
STUDENT_TEMP = 0.1
BOTH = ("smp", "proto")
PARTS = {"x": 4, "yh": 2, "yl": 4, "z": 8, "c": 2}
B, K, D = 1024, 131072, 512
ROWS = 2048
TILE = 256
BLOCKS = 8
f32, bf16 = jnp.float32, jnp.bfloat16
VMEM = pl.BlockSpec(memory_space=pltpu.VMEM)
SMEM = pl.BlockSpec(memory_space=pltpu.SMEM)
ANY = pl.BlockSpec(memory_space=pl.ANY)


def groups(names):
    order = list(PARTS)
    index = np.arange(512).reshape(tuple(PARTS.values()))
    inner = [order.index(n) for n in names]
    outer = [i for i in range(len(order)) if i not in inner]
    size = int(np.prod([PARTS[n] for n in names]))
    return index.transpose(outer + inner).reshape(-1, size).tolist()


def gathered(x, names):
    group = groups(names)
    copies = jnp.broadcast_to(x[None], (len(group[0]), *x.shape))
    return lax.all_to_all(copies, BOTH, 0, 0, tiled=True, axis_index_groups=group)


def sent_to_protos(x):
    return lax.all_to_all(x, "proto", 0, 0, tiled=True)


def far(x):
    return pltpu.with_memory_space_constraint(x, pltpu.HBM)


def limits():
    return pltpu.CompilerParams(vmem_limit_bytes=24 * 2**20)


def cost(flops=0, moved=0, exps=0):
    return pl.CostEstimate(flops=flops, bytes_accessed=moved, transcendentals=exps)


def call(body, outs, ins, out_specs=None, scratch=(), **work):
    return pl.pallas_call(
        body,
        out_shape=outs,
        in_specs=ins,
        out_specs=out_specs or [VMEM] * len(outs),
        scratch_shapes=scratch,
        compiler_params=limits(),
        cost_estimate=cost(**work),
    )


def streamed(body, outs, ins, out_specs, scratch=(), **work):
    return pl.pallas_call(
        body,
        out_shape=outs,
        grid_spec=pltpu.PrefetchScalarGridSpec(
            num_scalar_prefetch=1,
            grid=(ROWS // TILE,),
            in_specs=ins,
            out_specs=out_specs,
            scratch_shapes=scratch,
        ),
        compiler_params=limits(),
        cost_estimate=cost(**work),
    )


def whole(*dims):
    return pl.BlockSpec(dims, lambda i, me: (0,) * len(dims))


def stripe(width):
    return pl.BlockSpec((TILE, width), lambda i, me: (i, 0))


def features_of(third_ref, x, yh):
    base = pl.multiple_of(yh * 32, 32) if not isinstance(yh, int) else yh * 32
    halves = [third_ref[c, x, pl.ds(base, 32)].astype(f32) for c in range(2)]
    return [
        jnp.stack([h[:, which * 8 : which * 8 + 8] for h in halves], axis=1).reshape(D, 128)
        for which in range(2)
    ]


def unit_columns(values):
    scale = lax.rsqrt(jnp.sum(folded(values * values), axis=0, keepdims=True) + 1e-06)
    return (values * scale).astype(bf16), scale


def folded(total):
    return jnp.sum(total.reshape(-1, 8, total.shape[1]), axis=0)


def as_blocks(wide):
    row = jnp.sum(wide, axis=0, keepdims=True)
    return jnp.concatenate([row[:, s * 128 : (s + 1) * 128] for s in range(BLOCKS)], axis=0)


def as_row(blocks):
    return jnp.concatenate([blocks[s : s + 1, :] for s in range(BLOCKS)], axis=1)


def stage_out(stage_ref, out_ref, sem_ref, i, value):
    slot = lax.rem(i, 2)
    rows = pl.ds(pl.multiple_of(i * TILE, TILE), TILE)
    copy = pltpu.make_async_copy(stage_ref.at[slot], out_ref.at[rows], sem_ref.at[slot])

    @pl.when(i >= 2)
    def _():
        copy.wait()

    stage_ref[slot] = value
    copy.start()


def stage_end(stage_ref, out_ref, sem_ref):
    for slot in range(2):
        rows = pl.ds((ROWS // TILE - 2 + slot) * TILE, TILE)
        pltpu.make_async_copy(stage_ref.at[slot], out_ref.at[rows], sem_ref.at[slot]).wait()


def first_kernel(
    me_ref, third_ref, weight_ref, kernel_out, unit_out, sent_ref, scale_ref, features_ref,
    teacher_ref, student_ref, stage_ref, mass_ref, sem_ref, unit_sem,
):
    for s in range(BLOCKS):
        teacher, student = features_of(third_ref, s // 2, s % 2)
        teacher_ref[:, s * 128 : (s + 1) * 128] = unit_columns(teacher)[0]
        unit, scale = unit_columns(student)
        student_ref[:, s * 128 : (s + 1) * 128] = unit
        scale_ref[s : s + 1, :] = scale
    unit_copy = pltpu.make_async_copy(student_ref, unit_out, unit_sem)
    unit_copy.start()
    me = me_ref[0]
    features_ref[...] = features_of(third_ref, me // 2, lax.rem(me, 2))[1]
    mass_ref[...] = jnp.zeros_like(mass_ref)

    @pl.loop(0, ROWS // TILE)
    def _(i):
        rows = pl.ds(pl.multiple_of(i * TILE, TILE), TILE)
        kernel = jnp.exp(
            jnp.dot(weight_ref[rows, :], teacher_ref[...], preferred_element_type=f32) * (1.0 / TEACHER_TEMP)
        )
        stage_out(stage_ref, kernel_out, sem_ref, i, kernel)
        row_scale = 1.0 / (K * jnp.sum(kernel, axis=1, keepdims=True))
        mass_ref[...] += folded(kernel * row_scale)

    sent_ref[...] = jnp.broadcast_to(as_blocks(mass_ref[...])[None], sent_ref.shape)
    stage_end(stage_ref, kernel_out, sem_ref)
    unit_copy.wait()


def student_kernel(
    me_ref, unit_ref, weight_ref, logits_out, own_ref, total_ref, stage_ref, sum_ref, sem_ref
):
    sum_ref[...] = jnp.zeros_like(sum_ref)
    lanes = pl.ds(pl.multiple_of(me_ref[0] * 128, 128), 128)

    @pl.loop(0, ROWS // TILE)
    def _(i):
        rows = pl.ds(pl.multiple_of(i * TILE, TILE), TILE)
        logits = jnp.dot(weight_ref[rows, :], unit_ref[...], preferred_element_type=f32) * (1.0 / STUDENT_TEMP)
        stage_out(stage_ref, logits_out, sem_ref, i, logits)
        own_ref[rows, :] = stage_ref[lax.rem(i, 2), :, lanes]
        sum_ref[...] += folded(jnp.exp(logits))

    total_ref[...] = as_blocks(sum_ref[...])
    stage_end(stage_ref, logits_out, sem_ref)


def second_kernel(me_ref, got_ref, kernel_ref, total_ref, sent_ref, col_ref, mass_ref):
    i = pl.program_id(0)

    @pl.when(i == 0)
    def _():
        col_ref[...] = as_row(1.0 / (B * jnp.sum(got_ref[...], axis=0)))
        mass_ref[...] = jnp.zeros_like(mass_ref)

    kernel = kernel_ref[...]
    row_scale = 1.0 / (K * jnp.sum(kernel * col_ref[...], axis=1, keepdims=True))
    mass_ref[...] += folded(kernel * row_scale)

    @pl.when(i == ROWS // TILE - 1)
    def _():
        both = jnp.concatenate([as_blocks(mass_ref[...]), total_ref[...]], axis=0)
        sent_ref[...] = jnp.broadcast_to(both[None], sent_ref.shape)


def third_kernel(
    me_ref, got_ref, kernel_ref, scaled_ref, sent_ref, total_ref, col_out, col_ref, mass_ref
):
    i = pl.program_id(0)

    @pl.when(i == 0)
    def _():
        got = jnp.sum(got_ref[...], axis=0)
        total_ref[...] = got[8:, :]
        col = 1.0 / (B * got[:8, :])
        col_out[...] = col
        col_ref[...] = as_row(col)
        mass_ref[...] = jnp.zeros_like(mass_ref)

    kernel = kernel_ref[...]
    row_scale = 1.0 / (K * jnp.sum(kernel * col_ref[...], axis=1, keepdims=True))
    lanes = pl.ds(pl.multiple_of(me_ref[0] * 128, 128), 128)
    scaled_ref[...] = kernel_ref[:, lanes] * row_scale
    mass_ref[...] += folded(kernel * row_scale)

    @pl.when(i == ROWS // TILE - 1)
    def _():
        sent_ref[...] = jnp.broadcast_to(as_blocks(mass_ref[...])[None], sent_ref.shape)


def split_rows(value):
    high = value.astype(bf16).astype(f32)
    middle = (value - high).astype(bf16).astype(f32)
    return [high, middle, value - high - middle]


def own_kernel(
    me_ref, got_ref, scaled_ref, logits_ref, total_ref, features_ref, weight_ref, sent_ref, col_ref, grad_ref
):
    me = me_ref[0]
    col_ref[...] = 1.0 / (B * jnp.sum(got_ref[...], axis=0))
    own_col = col_ref[pl.ds(me, 1), :] * B
    own_total = 1.0 / total_ref[pl.ds(me, 1), :]
    logits = logits_ref[...]
    targets = scaled_ref[...] * own_col
    weighted = jnp.sum(folded(targets * logits), axis=0, keepdims=True)
    grad_ref[...] = ((jnp.exp(logits) * own_total - targets) * (1.0 / (B * STUDENT_TEMP))).astype(bf16)
    unit_part = lax.dot_general(
        grad_ref[...], weight_ref[...], (((0,), (0,)), ((), ())), preferred_element_type=f32
    ).T
    inner = jnp.sum(folded(features_ref[...] * unit_part), axis=0, keepdims=True)
    extra = jnp.concatenate(split_rows(inner) + split_rows(weighted) + [jnp.zeros((2, 128), f32)], axis=0)
    pieces = unit_part.reshape(64, 8, 128)
    sent_ref[...] = jnp.concatenate(
        [pieces, jnp.broadcast_to(extra[None], (64, 8, 128))], axis=1
    ).astype(bf16)


def weight_kernel(
    me_ref, kernel_ref, logits_ref, total_ref, before_ref, col_ref, unit_ref, out_ref, rows_ref
):
    @pl.when(pl.program_id(0) == 0)
    def _():
        rows_ref[0:1, :] = as_row(before_ref[...])
        rows_ref[1:2, :] = as_row(col_ref[...] * B)
        rows_ref[2:3, :] = as_row(1.0 / total_ref[...])

    kernel = kernel_ref[...]
    row_scale = 1.0 / (K * jnp.sum(kernel * rows_ref[0:1, :], axis=1, keepdims=True))
    targets = kernel * row_scale * rows_ref[1:2, :]
    probs = jnp.exp(logits_ref[...]) * rows_ref[2:3, :]
    grad = ((probs - targets) * (1.0 / (B * STUDENT_TEMP))).astype(bf16)
    out_ref[...] = lax.dot_general(unit_ref[...], grad, (((1,), (1,)), ((), ())), preferred_element_type=f32)


def final_kernel(me_ref, got_ref, features_ref, scale_ref, total_ref, features_out, loss_out):
    me = me_ref[0]
    got = jnp.sum(got_ref[...].astype(f32), axis=0)
    inner = got[8:9] + got[9:10] + got[10:11]
    weighted = got[11:12] + got[12:13] + got[13:14]
    scale = scale_ref[pl.ds(me, 1), :]
    features_out[...] = scale * got[:8] - (scale * scale * scale * inner) * features_ref[...].astype(f32)
    loss_out[...] = jnp.log(total_ref[pl.ds(me, 1), :]) - weighted


def shape(dims, dtype=f32):
    return jax.ShapeDtypeStruct(dims, dtype)


def on_device(teacher_features, student_features, teacher_weight, student_weight):
    me = lax.axis_index("smp").astype(jnp.int32).reshape(1)
    raw = jnp.concatenate([teacher_features.T, student_features.T], axis=0)
    first = gathered(raw, ("yh", "yl", "z"))
    second = gathered(first, ("x",))
    third = gathered(second, ("c",))

    pair = pltpu.SemaphoreType.DMA((2,))
    stage = pltpu.VMEM((2, TILE, B), f32)
    row, rows8 = pltpu.VMEM((1, B), f32), pltpu.VMEM((8, B), f32)
    matmul = dict(flops=2 * ROWS * B * D, moved=12 * 2**20, exps=ROWS * B)
    kernel, student_unit, sent_1, student_scale, features_own = call(
        first_kernel,
        [pltpu.HBM((ROWS, B), f32), pltpu.HBM((D, B), bf16), shape((64, 8, 128)), shape((8, 128)), shape((D, 128))],
        [SMEM, VMEM, VMEM],
        [ANY, ANY, VMEM, VMEM, VMEM],
        [pltpu.VMEM((D, B), bf16), pltpu.VMEM((D, B), bf16), stage, rows8, pair, pltpu.SemaphoreType.DMA],
        **matmul,
    )(me, third, teacher_weight)
    got_1 = sent_to_protos(sent_1)
    logits, logits_own, local_total = call(
        student_kernel,
        [pltpu.HBM((ROWS, B), f32), shape((ROWS, 128)), shape((8, 128))],
        [SMEM, VMEM, VMEM],
        [ANY, VMEM, VMEM],
        [stage, rows8, pair],
        **matmul,
    )(me, student_unit, student_weight)
    (sent_2,) = streamed(
        second_kernel,
        [shape((64, 16, 128))],
        [whole(64, 8, 128), stripe(B), whole(8, 128)],
        [whole(64, 16, 128)],
        [row, rows8],
        flops=4 * ROWS * B,
        moved=8 * 2**20,
    )(me, got_1, far(kernel), local_total)
    got_2 = sent_to_protos(sent_2)
    scaled_own, sent_3, total, col_before = streamed(
        third_kernel,
        [shape((ROWS, 128)), shape((64, 8, 128)), shape((8, 128)), shape((8, 128))],
        [whole(64, 16, 128), stripe(B)],
        [stripe(128), whole(64, 8, 128), whole(8, 128), whole(8, 128)],
        [row, rows8],
        flops=4 * ROWS * B,
        moved=8 * 2**20,
    )(me, got_2, far(kernel))
    got_3 = sent_to_protos(sent_3)
    sent_4, col_scale = call(
        own_kernel,
        [shape((64, 16, 128), bf16), shape((8, 128))],
        [SMEM] + [VMEM] * 6,
        None,
        [pltpu.VMEM((ROWS, 128), bf16)],
        flops=2 * ROWS * 128 * D,
        moved=4 * 2**20,
        exps=ROWS * 128,
    )(me, got_3, scaled_own, logits_own, total, features_own, student_weight)
    got_4 = sent_to_protos(sent_4)
    (grad_weight,) = streamed(
        weight_kernel,
        [shape((64, ROWS))],
        [stripe(B), stripe(B), whole(8, 128), whole(8, 128), whole(8, 128),
         pl.BlockSpec((64, B), lambda i, me: (me[0], 0))],
        [pl.BlockSpec((64, TILE), lambda i, me: (0, i))],
        [rows8],
        flops=2 * ROWS * B * 64,
        moved=17 * 2**20,
        exps=ROWS * B,
    )(me, far(kernel), far(logits), total, col_before, col_scale, student_unit)
    grad_features, loss = call(
        final_kernel, [shape((8, 128)), shape((1, 128))], [SMEM] + [VMEM] * 4
    )(me, got_4, student_features.T, student_scale, total)
    return loss.reshape(128), grad_features.T, grad_weight.T


def solution(mesh):
    placed = (P("smp", "proto"), P("smp", "proto"), P("proto", None), P("proto", None))
    return jax.shard_map(
        on_device,
        mesh=mesh,
        in_specs=placed,
        out_specs=(P("smp"), P("smp", "proto"), P("proto", "smp")),
        check_vma=False,
    )
```

```python
import jax
import jax.numpy as jnp
import numpy as np
from jax import lax
from jax.experimental import pallas as pl
from jax.experimental.pallas import tpu as pltpu
from jax.sharding import PartitionSpec as P

ITERS = 3
TEACHER_TEMP = 0.07
STUDENT_TEMP = 0.1
BOTH = ("smp", "proto")
PARTS = {"x": 4, "yh": 2, "yl": 4, "z": 8, "c": 2}
B, K, D = 1024, 131072, 512
ROWS = 2048
TILE = 256
WIDE = 512
BLOCKS = 8
f32, bf16 = jnp.float32, jnp.bfloat16
VMEM = pl.BlockSpec(memory_space=pltpu.VMEM)
SMEM = pl.BlockSpec(memory_space=pltpu.SMEM)
ANY = pl.BlockSpec(memory_space=pl.ANY)


def groups(names):
    order = list(PARTS)
    index = np.arange(512).reshape(tuple(PARTS.values()))
    inner = [order.index(n) for n in names]
    outer = [i for i in range(len(order)) if i not in inner]
    size = int(np.prod([PARTS[n] for n in names]))
    return index.transpose(outer + inner).reshape(-1, size).tolist()


def gathered(x, names):
    group = groups(names)
    copies = jnp.broadcast_to(x[None], (len(group[0]), *x.shape))
    return lax.all_to_all(copies, BOTH, 0, 0, tiled=True, axis_index_groups=group)


def sent_to_protos(x):
    return lax.all_to_all(x, "proto", 0, 0, tiled=True)


def far(x):
    return pltpu.with_memory_space_constraint(x, pltpu.HBM)


def limits():
    return pltpu.CompilerParams(vmem_limit_bytes=24 * 2**20)


def cost(flops=0, moved=0, exps=0):
    return pl.CostEstimate(flops=flops, bytes_accessed=moved, transcendentals=exps)


def call(body, outs, ins, out_specs=None, scratch=(), **work):
    return pl.pallas_call(
        body,
        out_shape=outs,
        in_specs=ins,
        out_specs=out_specs or [VMEM] * len(outs),
        scratch_shapes=scratch,
        compiler_params=limits(),
        cost_estimate=cost(**work),
    )


def streamed(body, outs, ins, out_specs, scratch=(), **work):
    return pl.pallas_call(
        body,
        out_shape=outs,
        grid_spec=pltpu.PrefetchScalarGridSpec(
            num_scalar_prefetch=1,
            grid=(ROWS // TILE,),
            in_specs=ins,
            out_specs=out_specs,
            scratch_shapes=scratch,
        ),
        compiler_params=limits(),
        cost_estimate=cost(**work),
    )


def whole(*dims):
    return pl.BlockSpec(dims, lambda i, me: (0,) * len(dims))


def stripe(width):
    return pl.BlockSpec((TILE, width), lambda i, me: (i, 0))


def features_of(third_ref, x, yh):
    base = pl.multiple_of(yh * 32, 32) if not isinstance(yh, int) else yh * 32
    halves = [third_ref[c, x, pl.ds(base, 32)].astype(f32) for c in range(2)]
    return [
        jnp.stack([h[:, which * 8 : which * 8 + 8] for h in halves], axis=1).reshape(D, 128)
        for which in range(2)
    ]


def unit_columns(values):
    scale = lax.rsqrt(jnp.sum(folded(values * values), axis=0, keepdims=True) + 1e-06)
    return (values * scale).astype(bf16), scale


def folded(total):
    return jnp.sum(total.reshape(-1, 8, total.shape[1]), axis=0)


def as_blocks(wide):
    row = jnp.sum(wide, axis=0, keepdims=True)
    return jnp.concatenate([row[:, s * 128 : (s + 1) * 128] for s in range(BLOCKS)], axis=0)


def as_row(blocks):
    return jnp.concatenate([blocks[s : s + 1, :] for s in range(BLOCKS)], axis=1)


def stage_out(stage_ref, out_ref, sem_ref, i, value):
    slot = lax.rem(i, 2)
    rows = pl.ds(pl.multiple_of(i * TILE, TILE), TILE)
    copy = pltpu.make_async_copy(stage_ref.at[slot], out_ref.at[rows], sem_ref.at[slot])

    @pl.when(i >= 2)
    def _():
        copy.wait()

    stage_ref[slot] = value
    copy.start()


def stage_end(stage_ref, out_ref, sem_ref):
    for slot in range(2):
        rows = pl.ds((ROWS // TILE - 2 + slot) * TILE, TILE)
        pltpu.make_async_copy(stage_ref.at[slot], out_ref.at[rows], sem_ref.at[slot]).wait()


def first_kernel(
    me_ref, third_ref, weight_ref, kernel_out, unit_out, sent_ref, scale_ref, features_ref,
    teacher_ref, student_ref, stage_ref, mass_ref, sem_ref, unit_sem,
):
    for s in range(BLOCKS):
        teacher, student = features_of(third_ref, s // 2, s % 2)
        teacher_ref[:, s * 128 : (s + 1) * 128] = unit_columns(teacher)[0]
        unit, scale = unit_columns(student)
        student_ref[:, s * 128 : (s + 1) * 128] = unit
        scale_ref[s : s + 1, :] = scale
    unit_copy = pltpu.make_async_copy(student_ref, unit_out, unit_sem)
    unit_copy.start()
    me = me_ref[0]
    features_ref[...] = features_of(third_ref, me // 2, lax.rem(me, 2))[1]
    mass_ref[...] = jnp.zeros_like(mass_ref)

    def copy_out(i):
        rows = pl.ds(pl.multiple_of(i * WIDE, WIDE), WIDE)
        return pltpu.make_async_copy(stage_ref.at[rows], kernel_out.at[rows], sem_ref.at[i])

    @pl.loop(0, ROWS // WIDE)
    def _(i):
        rows = pl.ds(pl.multiple_of(i * WIDE, WIDE), WIDE)
        kernel = jnp.exp(
            jnp.dot(weight_ref[rows, :], teacher_ref[...], preferred_element_type=f32) * (1.0 / TEACHER_TEMP)
        )
        stage_ref[rows, :] = kernel
        copy_out(i).start()
        row_scale = 1.0 / (K * jnp.sum(kernel, axis=1, keepdims=True))
        mass_ref[...] += folded(kernel * row_scale)

    sent_ref[...] = jnp.broadcast_to(as_blocks(mass_ref[...]).astype(bf16)[None], sent_ref.shape)
    for i in range(ROWS // WIDE):
        copy_out(i).wait()
    unit_copy.wait()


def student_kernel(
    me_ref, unit_ref, weight_ref, logits_out, own_ref, total_ref, stage_ref, sum_ref, sem_ref
):
    sum_ref[...] = jnp.zeros_like(sum_ref)
    lanes = pl.ds(pl.multiple_of(me_ref[0] * 128, 128), 128)

    @pl.loop(0, ROWS // TILE)
    def _(i):
        rows = pl.ds(pl.multiple_of(i * TILE, TILE), TILE)
        logits = jnp.dot(weight_ref[rows, :], unit_ref[...], preferred_element_type=f32) * (1.0 / STUDENT_TEMP)
        stage_out(stage_ref, logits_out, sem_ref, i, logits)
        own_ref[rows, :] = stage_ref[lax.rem(i, 2), :, lanes]
        sum_ref[...] += folded(jnp.exp(logits))

    total_ref[...] = as_blocks(sum_ref[...])
    stage_end(stage_ref, logits_out, sem_ref)


def received(got_ref):
    return jnp.sum(got_ref[...].astype(f32), axis=0)


def second_kernel(got_ref, far_ref, total_ref, kernel_ref, sent_ref, kept_ref, col_ref, mass_ref, sem_ref):
    def copy_in(i):
        rows = pl.ds(pl.multiple_of(i * TILE, TILE), TILE)
        return pltpu.make_async_copy(far_ref.at[rows], kernel_ref.at[rows], sem_ref.at[i])

    for i in range(ROWS // TILE):
        copy_in(i).start()
    col_ref[...] = as_row(1.0 / (B * received(got_ref)))
    mass_ref[...] = jnp.zeros_like(mass_ref)

    @pl.loop(0, ROWS // TILE)
    def _(i):
        copy_in(i).wait()
        kernel = kernel_ref[pl.ds(pl.multiple_of(i * TILE, TILE), TILE), :]
        row_scale = 1.0 / (K * jnp.sum(kernel * col_ref[...], axis=1, keepdims=True))
        mass_ref[...] += folded(kernel * row_scale)

    mass = as_blocks(mass_ref[...]).astype(bf16).astype(f32)
    kept_ref[...] = mass
    total = total_ref[...]
    high = total.astype(bf16).astype(f32)
    packed = jnp.concatenate([mass, high, total - high], axis=0).astype(bf16)
    sent_ref[...] = jnp.broadcast_to(packed[None], sent_ref.shape)


def third_kernel(
    me_ref, got_ref, kernel_ref, kept_ref, scaled_ref, sent_ref, total_ref, col_out, before_ref, col_ref, mass_ref
):
    got = received(got_ref)
    before_ref[...] = got[:8, :]
    total_ref[...] = got[8:16, :] + got[16:, :]
    col = 1.0 / (B * got[:8, :])
    col_out[...] = col
    col_ref[...] = as_row(col)
    mass_ref[...] = jnp.zeros_like(mass_ref)
    lanes = pl.ds(pl.multiple_of(me_ref[0] * 128, 128), 128)

    @pl.loop(0, ROWS // TILE)
    def _(i):
        rows = pl.ds(pl.multiple_of(i * TILE, TILE), TILE)
        kernel = kernel_ref[rows, :]
        row_scale = 1.0 / (K * jnp.sum(kernel * col_ref[...], axis=1, keepdims=True))
        scaled_ref[rows, :] = kernel_ref[rows, lanes] * row_scale
        mass_ref[...] += folded(kernel * row_scale)

    change = as_blocks(mass_ref[...]) - kept_ref[...]
    sent_ref[...] = jnp.broadcast_to(change.astype(bf16)[None], sent_ref.shape)


def split_rows(value):
    high = value.astype(bf16).astype(f32)
    middle = (value - high).astype(bf16).astype(f32)
    return [high, middle, value - high - middle]


def own_kernel(
    me_ref, got_ref, before_ref, scaled_ref, logits_ref, total_ref, features_ref, weight_ref, sent_ref, col_ref,
    grad_ref,
):
    me = me_ref[0]
    col_ref[...] = 1.0 / (B * (before_ref[...] + received(got_ref)))
    own_col = col_ref[pl.ds(me, 1), :] * B
    own_total = 1.0 / total_ref[pl.ds(me, 1), :]
    logits = logits_ref[...]
    targets = scaled_ref[...] * own_col
    weighted = jnp.sum(folded(targets * logits), axis=0, keepdims=True)
    grad_ref[...] = ((jnp.exp(logits) * own_total - targets) * (1.0 / (B * STUDENT_TEMP))).astype(bf16)
    unit_part = lax.dot_general(
        grad_ref[...], weight_ref[...], (((0,), (0,)), ((), ())), preferred_element_type=f32
    ).T
    inner = jnp.sum(folded(features_ref[...] * unit_part), axis=0, keepdims=True)
    extra = jnp.concatenate(split_rows(inner) + split_rows(weighted) + [jnp.zeros((2, 128), f32)], axis=0)
    pieces = unit_part.reshape(64, 8, 128)
    sent_ref[...] = jnp.concatenate(
        [pieces, jnp.broadcast_to(extra[None], (64, 8, 128))], axis=1
    ).astype(bf16)


def weight_kernel(
    me_ref, kernel_ref, logits_ref, total_ref, before_ref, col_ref, unit_ref, out_ref, rows_ref
):
    @pl.when(pl.program_id(0) == 0)
    def _():
        rows_ref[0:1, :] = as_row(before_ref[...])
        rows_ref[1:2, :] = as_row(col_ref[...] * B)
        rows_ref[2:3, :] = as_row(1.0 / total_ref[...])

    kernel = kernel_ref[...]
    row_scale = 1.0 / (K * jnp.sum(kernel * rows_ref[0:1, :], axis=1, keepdims=True))
    targets = kernel * row_scale * rows_ref[1:2, :]
    probs = jnp.exp(logits_ref[...]) * rows_ref[2:3, :]
    grad = ((probs - targets) * (1.0 / (B * STUDENT_TEMP))).astype(bf16)
    out_ref[...] = lax.dot_general(unit_ref[...], grad, (((1,), (1,)), ((), ())), preferred_element_type=f32)


def final_kernel(me_ref, got_ref, features_ref, scale_ref, total_ref, features_out, loss_out):
    me = me_ref[0]
    got = received(got_ref)
    inner = got[8:9] + got[9:10] + got[10:11]
    weighted = got[11:12] + got[12:13] + got[13:14]
    scale = scale_ref[pl.ds(me, 1), :]
    features_out[...] = scale * got[:8] - (scale * scale * scale * inner) * features_ref[...].astype(f32)
    loss_out[...] = jnp.log(total_ref[pl.ds(me, 1), :]) - weighted


def shape(dims, dtype=f32):
    return jax.ShapeDtypeStruct(dims, dtype)


def on_device(teacher_features, student_features, teacher_weight, student_weight):
    me = lax.axis_index("smp").astype(jnp.int32).reshape(1)
    raw = jnp.concatenate([teacher_features.T, student_features.T], axis=0)
    first = gathered(raw, ("yh", "yl", "z"))
    second = gathered(first, ("x",))
    third = gathered(second, ("c",))

    pair = pltpu.SemaphoreType.DMA((2,))
    stage = pltpu.VMEM((2, TILE, B), f32)
    row, rows8 = pltpu.VMEM((1, B), f32), pltpu.VMEM((8, B), f32)
    matmul = dict(flops=2 * ROWS * B * D, moved=12 * 2**20, exps=ROWS * B)
    kernel, student_unit, sent_1, student_scale, features_own = call(
        first_kernel,
        [pltpu.HBM((ROWS, B), f32), pltpu.HBM((D, B), bf16), shape((64, 8, 128), bf16), shape((8, 128)), shape((D, 128))],
        [SMEM, VMEM, VMEM],
        [ANY, ANY, VMEM, VMEM, VMEM],
        [pltpu.VMEM((D, B), bf16), pltpu.VMEM((D, B), bf16), pltpu.VMEM((ROWS, B), f32), rows8,
         pltpu.SemaphoreType.DMA((ROWS // WIDE,)), pltpu.SemaphoreType.DMA],
        **matmul,
    )(me, third, teacher_weight)
    got_1 = sent_to_protos(sent_1)
    logits, logits_own, local_total = call(
        student_kernel,
        [pltpu.HBM((ROWS, B), f32), shape((ROWS, 128)), shape((8, 128))],
        [SMEM, VMEM, VMEM],
        [ANY, VMEM, VMEM],
        [stage, rows8, pair],
        **matmul,
    )(me, student_unit, student_weight)
    kernel_near, sent_2, kept = call(
        second_kernel,
        [pltpu.VMEM((ROWS, B), f32), shape((64, 24, 128), bf16), shape((8, 128))],
        [VMEM, ANY, VMEM],
        None,
        [row, rows8, pltpu.SemaphoreType.DMA((ROWS // TILE,))],
        flops=4 * ROWS * B,
        moved=8 * 2**20,
    )(got_1, far(kernel), local_total)
    got_2 = sent_to_protos(sent_2)
    scaled_own, sent_3, total, col_before, before = call(
        third_kernel,
        [shape((ROWS, 128)), shape((64, 8, 128), bf16), shape((8, 128)), shape((8, 128)), shape((8, 128))],
        [SMEM, VMEM, VMEM, VMEM],
        None,
        [row, rows8],
        flops=4 * ROWS * B,
        moved=8 * 2**20,
    )(me, got_2, kernel_near, kept)
    got_3 = sent_to_protos(sent_3)
    sent_4, col_scale = call(
        own_kernel,
        [shape((64, 16, 128), bf16), shape((8, 128))],
        [SMEM] + [VMEM] * 7,
        None,
        [pltpu.VMEM((ROWS, 128), bf16)],
        flops=2 * ROWS * 128 * D,
        moved=4 * 2**20,
        exps=ROWS * 128,
    )(me, got_3, before, scaled_own, logits_own, total, features_own, student_weight)
    got_4 = sent_to_protos(sent_4)
    (grad_weight,) = streamed(
        weight_kernel,
        [shape((64, ROWS))],
        [stripe(B), stripe(B), whole(8, 128), whole(8, 128), whole(8, 128),
         pl.BlockSpec((64, B), lambda i, me: (me[0], 0))],
        [pl.BlockSpec((64, TILE), lambda i, me: (0, i))],
        [rows8],
        flops=2 * ROWS * B * 64,
        moved=17 * 2**20,
        exps=ROWS * B,
    )(me, far(kernel), far(logits), total, col_before, col_scale, student_unit)
    grad_features, loss = call(
        final_kernel, [shape((8, 128)), shape((1, 128))], [SMEM] + [VMEM] * 4
    )(me, got_4, student_features.T, student_scale, total)
    return loss.reshape(128), grad_features.T, grad_weight.T


def solution(mesh):
    placed = (P("smp", "proto"), P("smp", "proto"), P("proto", None), P("proto", None))
    return jax.shard_map(
        on_device,
        mesh=mesh,
        in_specs=placed,
        out_specs=(P("smp"), P("smp", "proto"), P("proto", "smp")),
        check_vma=False,
    )
```

```python
import jax
import jax.numpy as jnp
import numpy as np
from jax import lax
from jax.experimental import pallas as pl
from jax.experimental.pallas import tpu as pltpu
from jax.sharding import PartitionSpec as P

ITERS = 3
TEACHER_TEMP = 0.07
STUDENT_TEMP = 0.1
BOTH = ("smp", "proto")
PARTS = {"x": 4, "yh": 2, "yl": 4, "z": 8, "c": 2}
B, K, D = 1024, 131072, 512
ROWS = 2048
SHARE = 1.0 / (1024 * 0.1)
TILE = 256
WIDE = 512
BLOCKS = 8
f32, bf16 = jnp.float32, jnp.bfloat16
VMEM = pl.BlockSpec(memory_space=pltpu.VMEM)
SMEM = pl.BlockSpec(memory_space=pltpu.SMEM)
ANY = pl.BlockSpec(memory_space=pl.ANY)


def groups(names):
    order = list(PARTS)
    index = np.arange(512).reshape(tuple(PARTS.values()))
    inner = [order.index(n) for n in names]
    outer = [i for i in range(len(order)) if i not in inner]
    size = int(np.prod([PARTS[n] for n in names]))
    return index.transpose(outer + inner).reshape(-1, size).tolist()


def gathered(x, names):
    group = groups(names)
    copies = jnp.broadcast_to(x[None], (len(group[0]), *x.shape))
    return lax.all_to_all(copies, BOTH, 0, 0, tiled=True, axis_index_groups=group)


def sent_to_protos(x):
    return lax.all_to_all(x, "proto", 0, 0, tiled=True)


def far(x):
    return pltpu.with_memory_space_constraint(x, pltpu.HBM)


def limits():
    return pltpu.CompilerParams(vmem_limit_bytes=24 * 2**20)


def cost(flops=0, moved=0, exps=0):
    return pl.CostEstimate(flops=flops, bytes_accessed=moved, transcendentals=exps)


def call(body, outs, ins, out_specs=None, scratch=(), **work):
    return pl.pallas_call(
        body,
        out_shape=outs,
        in_specs=ins,
        out_specs=out_specs or [VMEM] * len(outs),
        scratch_shapes=scratch,
        compiler_params=limits(),
        cost_estimate=cost(**work),
    )


def streamed(body, outs, ins, out_specs, scratch=(), **work):
    return pl.pallas_call(
        body,
        out_shape=outs,
        grid_spec=pltpu.PrefetchScalarGridSpec(
            num_scalar_prefetch=1,
            grid=(ROWS // TILE,),
            in_specs=ins,
            out_specs=out_specs,
            scratch_shapes=scratch,
        ),
        compiler_params=limits(),
        cost_estimate=cost(**work),
    )


def whole(*dims):
    return pl.BlockSpec(dims, lambda i, me: (0,) * len(dims))


def stripe(width):
    return pl.BlockSpec((TILE, width), lambda i, me: (i, 0))


def features_of(third_ref, x, yh):
    base = pl.multiple_of(yh * 32, 32) if not isinstance(yh, int) else yh * 32
    halves = [third_ref[c, x, pl.ds(base, 32)].astype(f32) for c in range(2)]
    return [
        jnp.stack([h[:, which * 8 : which * 8 + 8] for h in halves], axis=1).reshape(D, 128)
        for which in range(2)
    ]


def unit_columns(values):
    scale = lax.rsqrt(jnp.sum(folded(values * values), axis=0, keepdims=True) + 1e-06)
    return (values * scale).astype(bf16), scale


def folded(total):
    return jnp.sum(total.reshape(-1, 8, total.shape[1]), axis=0)


def as_blocks(wide):
    row = jnp.sum(wide, axis=0, keepdims=True)
    return jnp.concatenate([row[:, s * 128 : (s + 1) * 128] for s in range(BLOCKS)], axis=0)


def as_row(blocks):
    return jnp.concatenate([blocks[s : s + 1, :] for s in range(BLOCKS)], axis=1)


def stage_out(stage_ref, out_ref, sem_ref, i, value):
    slot = lax.rem(i, 2)
    rows = pl.ds(pl.multiple_of(i * TILE, TILE), TILE)
    copy = pltpu.make_async_copy(stage_ref.at[slot], out_ref.at[rows], sem_ref.at[slot])

    @pl.when(i >= 2)
    def _():
        copy.wait()

    stage_ref[slot] = value
    copy.start()


def stage_end(stage_ref, out_ref, sem_ref):
    for slot in range(2):
        rows = pl.ds((ROWS // TILE - 2 + slot) * TILE, TILE)
        pltpu.make_async_copy(stage_ref.at[slot], out_ref.at[rows], sem_ref.at[slot]).wait()


def first_kernel(
    me_ref, third_ref, weight_ref, kernel_out, unit_out, sent_ref, scale_ref, features_ref,
    teacher_ref, student_ref, stage_ref, mass_ref, sem_ref, unit_sem,
):
    for s in range(BLOCKS):
        teacher, student = features_of(third_ref, s // 2, s % 2)
        teacher_ref[:, s * 128 : (s + 1) * 128] = unit_columns(teacher)[0]
        unit, scale = unit_columns(student)
        student_ref[:, s * 128 : (s + 1) * 128] = unit
        scale_ref[s : s + 1, :] = scale
    unit_copy = pltpu.make_async_copy(student_ref, unit_out, unit_sem)
    unit_copy.start()
    me = me_ref[0]
    features_ref[...] = features_of(third_ref, me // 2, lax.rem(me, 2))[1]
    mass_ref[...] = jnp.zeros_like(mass_ref)

    def copy_out(i):
        rows = pl.ds(pl.multiple_of(i * WIDE, WIDE), WIDE)
        return pltpu.make_async_copy(stage_ref.at[rows], kernel_out.at[rows], sem_ref.at[i])

    @pl.loop(0, ROWS // WIDE)
    def _(i):
        rows = pl.ds(pl.multiple_of(i * WIDE, WIDE), WIDE)
        kernel = jnp.exp(
            jnp.dot(weight_ref[rows, :], teacher_ref[...], preferred_element_type=f32) * (1.0 / TEACHER_TEMP)
        )
        stage_ref[rows, :] = kernel
        copy_out(i).start()
        row_scale = 1.0 / (K * jnp.sum(kernel, axis=1, keepdims=True))
        mass_ref[...] += folded(kernel * row_scale)

    sent_ref[...] = jnp.broadcast_to(as_blocks(mass_ref[...]).astype(bf16)[None], sent_ref.shape)
    for i in range(ROWS // WIDE):
        copy_out(i).wait()
    unit_copy.wait()


def student_kernel(
    me_ref, unit_ref, weight_ref, logits_out, own_ref, total_ref, stage_ref, sum_ref, sem_ref
):
    sum_ref[...] = jnp.zeros_like(sum_ref)
    lanes = pl.ds(pl.multiple_of(me_ref[0] * 128, 128), 128)

    @pl.loop(0, ROWS // TILE)
    def _(i):
        rows = pl.ds(pl.multiple_of(i * TILE, TILE), TILE)
        logits = jnp.dot(weight_ref[rows, :], unit_ref[...], preferred_element_type=f32) * (1.0 / STUDENT_TEMP)
        stage_out(stage_ref, logits_out, sem_ref, i, logits)
        own_ref[rows, :] = stage_ref[lax.rem(i, 2), :, lanes]
        sum_ref[...] += folded(jnp.exp(logits))

    total_ref[...] = as_blocks(sum_ref[...])
    stage_end(stage_ref, logits_out, sem_ref)


def received(got_ref):
    return jnp.sum(got_ref[...].astype(f32), axis=0)


def second_kernel(got_ref, far_ref, total_ref, kernel_ref, sent_ref, kept_ref, col_ref, mass_ref, sem_ref):
    def copy_in(i):
        rows = pl.ds(pl.multiple_of(i * TILE, TILE), TILE)
        return pltpu.make_async_copy(far_ref.at[rows], kernel_ref.at[rows], sem_ref.at[i])

    for i in range(ROWS // TILE):
        copy_in(i).start()
    col_ref[...] = as_row(1.0 / (B * received(got_ref)))
    mass_ref[...] = jnp.zeros_like(mass_ref)

    @pl.loop(0, ROWS // TILE)
    def _(i):
        copy_in(i).wait()
        kernel = kernel_ref[pl.ds(pl.multiple_of(i * TILE, TILE), TILE), :]
        row_scale = 1.0 / (K * jnp.sum(kernel * col_ref[...], axis=1, keepdims=True))
        mass_ref[...] += folded(kernel * row_scale)

    mass = as_blocks(mass_ref[...]).astype(bf16).astype(f32)
    kept_ref[...] = mass
    total = total_ref[...]
    high = total.astype(bf16).astype(f32)
    packed = jnp.concatenate([mass, high, total - high], axis=0).astype(bf16)
    sent_ref[...] = jnp.broadcast_to(packed[None], sent_ref.shape)


def split_rows(value):
    high = value.astype(bf16).astype(f32)
    return [high, value - high]


def third_kernel(
    me_ref, got_ref, kernel_ref, kept_ref, logits_ref, features_ref, weight_ref,
    sent_ref, total_ref, before_ref, col_ref, mass_ref, scaled_ref, pair_ref,
):
    me = me_ref[0]
    got = received(got_ref)
    before_ref[...] = got[:8, :]
    total_ref[...] = got[8:16, :] + got[16:, :]
    col_ref[...] = as_row(1.0 / (B * got[:8, :]))
    mass_ref[...] = jnp.zeros_like(mass_ref)
    lanes = pl.ds(pl.multiple_of(me * 128, 128), 128)

    @pl.loop(0, ROWS // TILE)
    def _(i):
        rows = pl.ds(pl.multiple_of(i * TILE, TILE), TILE)
        kernel = kernel_ref[rows, :]
        row_scale = 1.0 / (K * jnp.sum(kernel * col_ref[...], axis=1, keepdims=True))
        scaled_ref[rows, :] = kernel_ref[rows, lanes] * row_scale
        mass_ref[...] += folded(kernel * row_scale)

    change = as_blocks(mass_ref[...]) - kept_ref[...]
    logits = logits_ref[...]
    own_col = 1.0 / before_ref[pl.ds(me, 1), :]
    own_total = 1.0 / total_ref[pl.ds(me, 1), :]
    targets = scaled_ref[...] * own_col
    weighted = jnp.sum(folded(targets * logits), axis=0, keepdims=True)
    pair_ref[:, :128] = ((jnp.exp(logits) * own_total - targets) * SHARE).astype(bf16)
    pair_ref[:, 128:] = (targets * SHARE).astype(bf16)
    parts = lax.dot_general(
        pair_ref[...], weight_ref[...], (((0,), (0,)), ((), ())), preferred_element_type=f32
    )
    grad_part, target_part = parts[:128, :].T, parts[128:, :].T
    features = features_ref[...]
    inner_grad = jnp.sum(folded(features * grad_part), axis=0, keepdims=True)
    inner_target = jnp.sum(folded(features * target_part), axis=0, keepdims=True)
    extra = jnp.concatenate(
        split_rows(inner_grad) + split_rows(inner_target) + split_rows(weighted) + [jnp.zeros((2, 128), f32)],
        axis=0,
    )

    def everywhere(rows):
        return jnp.broadcast_to(rows[None], (64, 8, 128))

    sent_ref[...] = jnp.concatenate(
        [everywhere(change), grad_part.reshape(64, 8, 128), target_part.reshape(64, 8, 128), everywhere(extra)],
        axis=1,
    ).astype(bf16)


def weight_kernel(
    me_ref, kernel_ref, logits_ref, total_ref, before_ref, unit_ref, out_ref, targets_ref, rows_ref
):
    @pl.when(pl.program_id(0) == 0)
    def _():
        rows_ref[0:1, :] = as_row(1.0 / (B * before_ref[...]))
        rows_ref[1:2, :] = as_row(1.0 / before_ref[...])
        rows_ref[2:3, :] = as_row(1.0 / total_ref[...])

    kernel = kernel_ref[...]
    row_scale = 1.0 / (K * jnp.sum(kernel * rows_ref[0:1, :], axis=1, keepdims=True))
    targets = kernel * row_scale * rows_ref[1:2, :]
    probs = jnp.exp(logits_ref[...]) * rows_ref[2:3, :]
    grad = ((probs - targets) * SHARE).astype(bf16)
    targets_ref[...] = (targets * SHARE).astype(bf16)
    out_ref[...] = lax.dot_general(unit_ref[...], grad, (((1,), (1,)), ((), ())), preferred_element_type=f32)


def final_kernel(
    me_ref, got_ref, features_ref, scale_ref, total_ref, before_ref, unit_ref, near_ref, targets_far,
    features_out, loss_out, weight_out, change_ref, targets_ref, sem_ref,
):
    def copy_in(i):
        rows = pl.ds(i * WIDE, WIDE)
        return pltpu.make_async_copy(targets_far.at[rows], targets_ref.at[rows], sem_ref.at[i])

    for i in range(ROWS // WIDE):
        copy_in(i).start()
    me = me_ref[0]
    got = received(got_ref)
    before = before_ref[...]
    change_ref[...] = got[:8] / (before + got[:8])
    own = change_ref[pl.ds(me, 1), :]
    unit_grad = got[8:16] + own * got[16:24]
    inner = (got[24:25] + got[25:26]) + own * (got[26:27] + got[27:28])
    scale = scale_ref[pl.ds(me, 1), :]
    features_out[...] = scale * unit_grad - (scale * scale * scale * inner) * features_ref[...].astype(f32)
    loss_out[...] = jnp.log(total_ref[pl.ds(me, 1), :]) - (1.0 - own) * (got[28:29] + got[29:30])
    units = unit_ref[pl.ds(pl.multiple_of(me * 64, 64), 64), :].astype(f32)
    moved = (units * as_row(change_ref[...])).astype(bf16)
    for i in range(ROWS // WIDE):
        copy_in(i).wait()
        rows = pl.ds(i * WIDE, WIDE)
        weight_out[:, rows] = near_ref[:, rows] + lax.dot_general(
            moved, targets_ref[rows, :], (((1,), (1,)), ((), ())), preferred_element_type=f32
        )


def shape(dims, dtype=f32):
    return jax.ShapeDtypeStruct(dims, dtype)


def on_device(teacher_features, student_features, teacher_weight, student_weight):
    me = lax.axis_index("smp").astype(jnp.int32).reshape(1)
    raw = jnp.concatenate([teacher_features.T, student_features.T], axis=0)
    raw, me = lax.optimization_barrier((raw, me))
    first = gathered(raw, ("yh", "yl", "z"))
    second = gathered(first, ("x",))
    third = gathered(second, ("c",))

    pair = pltpu.SemaphoreType.DMA((2,))
    stage = pltpu.VMEM((2, TILE, B), f32)
    row, rows8 = pltpu.VMEM((1, B), f32), pltpu.VMEM((8, B), f32)
    rows8_small = pltpu.VMEM((8, 128), f32)
    matmul = dict(flops=2 * ROWS * B * D, moved=12 * 2**20, exps=ROWS * B)
    kernel, student_unit, sent_1, student_scale, features_own = call(
        first_kernel,
        [pltpu.HBM((ROWS, B), f32), pltpu.HBM((D, B), bf16), shape((64, 8, 128), bf16), shape((8, 128)), shape((D, 128))],
        [SMEM, VMEM, VMEM],
        [ANY, ANY, VMEM, VMEM, VMEM],
        [pltpu.VMEM((D, B), bf16), pltpu.VMEM((D, B), bf16), pltpu.VMEM((ROWS, B), f32), rows8,
         pltpu.SemaphoreType.DMA((ROWS // WIDE,)), pltpu.SemaphoreType.DMA],
        **matmul,
    )(me, third, teacher_weight)
    got_1 = sent_to_protos(sent_1)
    logits, logits_own, local_total = call(
        student_kernel,
        [pltpu.HBM((ROWS, B), f32), shape((ROWS, 128)), shape((8, 128))],
        [SMEM, VMEM, VMEM],
        [ANY, VMEM, VMEM],
        [stage, rows8, pair],
        **matmul,
    )(me, student_unit, student_weight)
    kernel_near, sent_2, kept = call(
        second_kernel,
        [pltpu.VMEM((ROWS, B), f32), shape((64, 24, 128), bf16), shape((8, 128))],
        [VMEM, ANY, VMEM],
        None,
        [row, rows8, pltpu.SemaphoreType.DMA((ROWS // TILE,))],
        flops=4 * ROWS * B,
        moved=8 * 2**20,
    )(got_1, far(kernel), local_total)
    got_2 = sent_to_protos(sent_2)
    sent_3, total, before = call(
        third_kernel,
        [shape((64, 32, 128), bf16), shape((8, 128)), shape((8, 128))],
        [SMEM] + [VMEM] * 6,
        None,
        [row, rows8, pltpu.VMEM((ROWS, 128), f32), pltpu.VMEM((ROWS, 256), bf16)],
        flops=2 * ROWS * 256 * D,
        moved=12 * 2**20,
        exps=ROWS * 128,
    )(me, got_2, kernel_near, kept, logits_own, features_own, student_weight)
    got_3 = sent_to_protos(sent_3)
    weight_near, targets = streamed(
        weight_kernel,
        [shape((64, ROWS)), pltpu.HBM((ROWS, B), bf16)],
        [stripe(B), stripe(B), whole(8, 128), whole(8, 128), pl.BlockSpec((64, B), lambda i, me: (me[0], 0))],
        [pl.BlockSpec((64, TILE), lambda i, me: (0, i)), stripe(B)],
        [rows8],
        flops=2 * ROWS * B * 64,
        moved=21 * 2**20,
        exps=ROWS * B,
    )(me, far(kernel), far(logits), total, before, student_unit)
    grad_features, loss, grad_weight = call(
        final_kernel,
        [shape((8, 128)), shape((1, 128)), shape((64, ROWS))],
        [SMEM] + [VMEM] * 7 + [ANY],
        None,
        [rows8_small, pltpu.VMEM((ROWS, B), bf16), pltpu.SemaphoreType.DMA((ROWS // WIDE,))],
        flops=2 * ROWS * B * 64,
        moved=5 * 2**20,
    )(
        me, got_3, student_features.T, student_scale, total, before, student_unit, weight_near, far(targets)
    )
    return loss.reshape(128), grad_features.T, grad_weight.T


def solution(mesh):
    placed = (P("smp", "proto"), P("smp", "proto"), P("proto", None), P("proto", None))
    return jax.shard_map(
        on_device,
        mesh=mesh,
        in_specs=placed,
        out_specs=(P("smp"), P("smp", "proto"), P("proto", "smp")),
        check_vma=False,
    )
```

```python
import jax
import jax.numpy as jnp
import numpy as np
from jax import lax
from jax.experimental import pallas as pl
from jax.experimental.pallas import tpu as pltpu
from jax.sharding import PartitionSpec as P

ITERS = 3
TEACHER_TEMP = 0.07
STUDENT_TEMP = 0.1
BOTH = ("smp", "proto")
PARTS = {"x": 4, "yh": 2, "yl": 4, "z": 8, "c": 2}
B, K, D = 1024, 131072, 512
ROWS = 2048
SHARE = 1.0 / (1024 * 0.1)
TILE = 256
WIDE = 512
QUARTER = 16
BLOCKS = 8
f32, bf16 = jnp.float32, jnp.bfloat16
VMEM = pl.BlockSpec(memory_space=pltpu.VMEM)
SMEM = pl.BlockSpec(memory_space=pltpu.SMEM)
ANY = pl.BlockSpec(memory_space=pl.ANY)


def groups(names):
    order = list(PARTS)
    index = np.arange(512).reshape(tuple(PARTS.values()))
    inner = [order.index(n) for n in names]
    outer = [i for i in range(len(order)) if i not in inner]
    size = int(np.prod([PARTS[n] for n in names]))
    return index.transpose(outer + inner).reshape(-1, size).tolist()


def gathered(x, names):
    group = groups(names)
    copies = jnp.broadcast_to(x[None], (len(group[0]), *x.shape))
    return lax.all_to_all(copies, BOTH, 0, 0, tiled=True, axis_index_groups=group)


def sent_to_protos(x):
    return lax.all_to_all(x, "proto", 0, 0, tiled=True)


def far(x):
    return pltpu.with_memory_space_constraint(x, pltpu.HBM)


def limits():
    return pltpu.CompilerParams(vmem_limit_bytes=24 * 2**20)


def cost(flops=0, moved=0, exps=0):
    return pl.CostEstimate(flops=flops, bytes_accessed=moved, transcendentals=exps)


def call(body, outs, ins, out_specs=None, scratch=(), **work):
    return pl.pallas_call(
        body,
        out_shape=outs,
        in_specs=ins,
        out_specs=out_specs or [VMEM] * len(outs),
        scratch_shapes=scratch,
        compiler_params=limits(),
        cost_estimate=cost(**work),
    )


def streamed(body, outs, ins, out_specs, scratch=(), **work):
    return pl.pallas_call(
        body,
        out_shape=outs,
        grid_spec=pltpu.PrefetchScalarGridSpec(
            num_scalar_prefetch=1,
            grid=(ROWS // TILE,),
            in_specs=ins,
            out_specs=out_specs,
            scratch_shapes=scratch,
        ),
        compiler_params=limits(),
        cost_estimate=cost(**work),
    )


def whole(*dims):
    return pl.BlockSpec(dims, lambda i, me: (0,) * len(dims))


def stripe(width):
    return pl.BlockSpec((TILE, width), lambda i, me: (i, 0))


def features_of(cores, x, yh, which):
    base = yh * 32 if isinstance(yh, int) else pl.multiple_of(yh * 32, 32)
    halves = [ref[x, pl.ds(base, 32)].astype(f32)[:, which * 8 : which * 8 + 8] for ref in cores]
    return jnp.stack(halves, axis=1).reshape(D, 128)


def unit_columns(values):
    scale = lax.rsqrt(jnp.sum(folded(values * values), axis=0, keepdims=True) + 1e-06)
    return (values * scale).astype(bf16), scale


def folded(total):
    return jnp.sum(total.reshape(-1, 8, total.shape[1]), axis=0)


def as_blocks(wide):
    row = jnp.sum(wide, axis=0, keepdims=True)
    return jnp.concatenate([row[:, s * 128 : (s + 1) * 128] for s in range(BLOCKS)], axis=0)


def as_row(blocks):
    return jnp.concatenate([blocks[s : s + 1, :] for s in range(BLOCKS)], axis=1)


def first_kernel(
    me_ref, own_ref, other_ref, weight_far, kernel_out, unit_ref, sent_out, scale_ref, features_ref,
    teacher_ref, weight_ref, stage_ref, sent_ref, mass_ref, sem_ref, weight_sem, sent_sem,
):
    me, core = me_ref[0], me_ref[1]

    def copy_in(i):
        rows = pl.ds(pl.multiple_of(i * WIDE, WIDE), WIDE)
        return pltpu.make_async_copy(weight_far.at[rows], weight_ref.at[rows], weight_sem.at[i])

    for i in range(ROWS // WIDE):
        copy_in(i).start()

    def by_core(body):
        @pl.when(core == 0)
        def _():
            body((own_ref, other_ref))

        @pl.when(core == 1)
        def _():
            body((other_ref, own_ref))

    def teacher_units(cores):
        for s in range(BLOCKS):
            values = features_of(cores, s // 2, s % 2, 0)
            teacher_ref[:, s * 128 : (s + 1) * 128] = unit_columns(values)[0]

    def student_units(cores):
        for s in range(BLOCKS):
            values = features_of(cores, s // 2, s % 2, 1)
            unit, scale = unit_columns(values)
            unit_ref[:, s * 128 : (s + 1) * 128] = unit
            scale_ref[s : s + 1, :] = scale
        features_ref[...] = features_of(cores, me // 2, lax.rem(me, 2), 1)

    def copy_out(i):
        rows = pl.ds(pl.multiple_of(i * WIDE, WIDE), WIDE)
        return pltpu.make_async_copy(stage_ref.at[rows], kernel_out.at[rows], sem_ref.at[i])

    by_core(teacher_units)
    mass_ref[...] = jnp.zeros_like(mass_ref)

    @pl.loop(0, ROWS // WIDE)
    def _(i):
        copy_in(i).wait()
        rows = pl.ds(pl.multiple_of(i * WIDE, WIDE), WIDE)
        kernel = jnp.exp(
            jnp.dot(weight_ref[rows, :], teacher_ref[...], preferred_element_type=f32) * (1.0 / TEACHER_TEMP)
        )
        stage_ref[rows, :] = kernel
        copy_out(i).start()
        row_scale = 1.0 / (K * jnp.sum(kernel, axis=1, keepdims=True))
        mass_ref[...] += folded(kernel * row_scale)

    sent_ref[...] = jnp.broadcast_to(as_blocks(mass_ref[...]).astype(bf16)[None], sent_ref.shape)
    sent_copy = pltpu.make_async_copy(sent_ref, sent_out, sent_sem)
    sent_copy.start()
    by_core(student_units)
    sent_copy.wait()
    for i in range(ROWS // WIDE):
        copy_out(i).wait()


def student_kernel(
    me_ref, unit_ref, weight_ref, logits_out, own_out, total_ref, stage_ref, own_ref, sum_ref, sem_ref, own_sem
):
    sum_ref[...] = jnp.zeros_like(sum_ref)
    lanes = pl.ds(pl.multiple_of(me_ref[0] * 128, 128), 128)

    def copies(i):
        rows = pl.ds(pl.multiple_of(i * WIDE, WIDE), WIDE)
        return (
            pltpu.make_async_copy(stage_ref.at[rows], logits_out.at[rows], sem_ref.at[i]),
            pltpu.make_async_copy(own_ref.at[rows], own_out.at[rows], own_sem.at[i]),
        )

    @pl.loop(0, ROWS // WIDE)
    def _(i):
        rows = pl.ds(pl.multiple_of(i * WIDE, WIDE), WIDE)
        logits = jnp.dot(weight_ref[rows, :], unit_ref[...], preferred_element_type=f32) * (1.0 / STUDENT_TEMP)
        stage_ref[rows, :] = logits
        own_ref[rows, :] = stage_ref[rows, lanes]
        for copy in copies(i):
            copy.start()
        sum_ref[...] += folded(jnp.exp(logits))

    total_ref[...] = as_blocks(sum_ref[...])
    for i in range(ROWS // WIDE):
        for copy in copies(i):
            copy.wait()


def received(got_ref):
    return jnp.sum(got_ref[...].astype(f32), axis=0)


def second_kernel(got_ref, far_ref, total_ref, kernel_ref, sent_ref, kept_ref, col_ref, mass_ref, sem_ref):
    def copy_in(i):
        rows = pl.ds(pl.multiple_of(i * TILE, TILE), TILE)
        return pltpu.make_async_copy(far_ref.at[rows], kernel_ref.at[rows], sem_ref.at[i])

    for i in range(ROWS // TILE):
        copy_in(i).start()
    col_ref[...] = as_row(1.0 / (B * received(got_ref)))
    mass_ref[...] = jnp.zeros_like(mass_ref)

    @pl.loop(0, ROWS // TILE)
    def _(i):
        copy_in(i).wait()
        kernel = kernel_ref[pl.ds(pl.multiple_of(i * TILE, TILE), TILE), :]
        row_scale = 1.0 / (K * jnp.sum(kernel * col_ref[...], axis=1, keepdims=True))
        mass_ref[...] += folded(kernel * row_scale)

    mass = as_blocks(mass_ref[...]).astype(bf16).astype(f32)
    kept_ref[...] = mass
    total = total_ref[...]
    high = total.astype(bf16).astype(f32)
    packed = jnp.concatenate([mass, high, total - high], axis=0).astype(bf16)
    sent_ref[...] = jnp.broadcast_to(packed[None], sent_ref.shape)


def split_rows(value):
    high = value.astype(bf16).astype(f32)
    return [high, value - high]


def third_kernel(
    me_ref, got_ref, kernel_ref, kept_ref, logits_ref, features_ref, weight_ref,
    sent_out, total_ref, before_ref, col_ref, mass_ref, scaled_ref, pair_ref, sent_ref, sem_ref,
):
    me = me_ref[0]
    got = received(got_ref)
    before_ref[...] = got[:8, :]
    total_ref[...] = got[8:16, :] + got[16:, :]
    col_ref[...] = as_row(1.0 / (B * got[:8, :]))
    mass_ref[...] = jnp.zeros_like(mass_ref)
    lanes = pl.ds(pl.multiple_of(me * 128, 128), 128)

    @pl.loop(0, ROWS // TILE)
    def _(i):
        rows = pl.ds(pl.multiple_of(i * TILE, TILE), TILE)
        kernel = kernel_ref[rows, :]
        row_scale = 1.0 / (K * jnp.sum(kernel * col_ref[...], axis=1, keepdims=True))
        scaled_ref[rows, :] = kernel_ref[rows, lanes] * row_scale
        mass_ref[...] += folded(kernel * row_scale)

    change = as_blocks(mass_ref[...]) - kept_ref[...]
    logits = logits_ref[...]
    own_col = 1.0 / before_ref[pl.ds(me, 1), :]
    own_total = 1.0 / total_ref[pl.ds(me, 1), :]
    targets = scaled_ref[...] * own_col
    weighted = jnp.sum(folded(targets * logits), axis=0, keepdims=True)
    pair_ref[:, :128] = ((jnp.exp(logits) * own_total - targets) * SHARE).astype(bf16)
    pair_ref[:, 128:] = (targets * SHARE).astype(bf16)
    parts = lax.dot_general(
        pair_ref[...], weight_ref[...], (((0,), (0,)), ((), ())), preferred_element_type=f32
    )
    grad_part, target_part = parts[:128, :].T, parts[128:, :].T
    features = features_ref[...]
    inner_grad = jnp.sum(folded(features * grad_part), axis=0, keepdims=True)
    inner_target = jnp.sum(folded(features * target_part), axis=0, keepdims=True)
    extra = jnp.concatenate(
        split_rows(inner_grad) + split_rows(inner_target) + split_rows(weighted) + [jnp.zeros((2, 128), f32)],
        axis=0,
    )

    def everywhere(rows):
        return jnp.broadcast_to(rows[None], (QUARTER, 8, 128))

    def copy_out(i):
        part = pl.ds(i * QUARTER, QUARTER)
        return pltpu.make_async_copy(sent_ref.at[part], sent_out.at[part], sem_ref.at[i])

    grad_part, target_part = grad_part.reshape(64, 8, 128), target_part.reshape(64, 8, 128)
    for i in range(64 // QUARTER):
        part = slice(i * QUARTER, (i + 1) * QUARTER)
        sent_ref[part] = jnp.concatenate(
            [everywhere(change), grad_part[part], target_part[part], everywhere(extra)], axis=1
        ).astype(bf16)
        copy_out(i).start()
    for i in range(64 // QUARTER):
        copy_out(i).wait()


def weight_kernel(
    me_ref, kernel_ref, logits_ref, total_ref, before_ref, unit_ref, out_ref, targets_ref, rows_ref
):
    @pl.when(pl.program_id(0) == 0)
    def _():
        rows_ref[0:1, :] = as_row(1.0 / (B * before_ref[...]))
        rows_ref[1:2, :] = as_row(1.0 / before_ref[...])
        rows_ref[2:3, :] = as_row(1.0 / total_ref[...])

    kernel = kernel_ref[...]
    row_scale = 1.0 / (K * jnp.sum(kernel * rows_ref[0:1, :], axis=1, keepdims=True))
    targets = kernel * row_scale * rows_ref[1:2, :]
    probs = jnp.exp(logits_ref[...]) * rows_ref[2:3, :]
    grad = ((probs - targets) * SHARE).astype(bf16)
    targets_ref[...] = (targets * SHARE).astype(bf16)
    out_ref[...] = lax.dot_general(unit_ref[...], grad, (((1,), (1,)), ((), ())), preferred_element_type=f32)


def final_kernel(
    me_ref, got_ref, features_ref, scale_ref, total_ref, before_ref, unit_ref, near_ref, targets_far,
    features_out, loss_out, weight_out, change_ref, targets_ref, weight_ref, sem_ref, out_sem,
):
    def copy_in(i):
        rows = pl.ds(i * WIDE, WIDE)
        return pltpu.make_async_copy(targets_far.at[rows], targets_ref.at[rows], sem_ref.at[i])

    for i in range(ROWS // WIDE):
        copy_in(i).start()
    me = me_ref[0]
    got = received(got_ref)
    before = before_ref[...]
    change_ref[...] = got[:8] / (before + got[:8])
    own = change_ref[pl.ds(me, 1), :]
    unit_grad = got[8:16] + own * got[16:24]
    inner = (got[24:25] + got[25:26]) + own * (got[26:27] + got[27:28])
    scale = scale_ref[pl.ds(me, 1), :]
    features_out[...] = scale * unit_grad - (scale * scale * scale * inner) * features_ref[...].astype(f32)
    loss_out[...] = jnp.log(total_ref[pl.ds(me, 1), :]) - (1.0 - own) * (got[28:29] + got[29:30])
    units = unit_ref[pl.ds(pl.multiple_of(me * 64, 64), 64), :].astype(f32)
    moved = (units * as_row(change_ref[...])).astype(bf16)

    def copy_out(i):
        rows = pl.ds(i * WIDE, WIDE)
        return pltpu.make_async_copy(weight_ref.at[:, rows], weight_out.at[:, rows], out_sem.at[i])

    for i in range(ROWS // WIDE):
        copy_in(i).wait()
        rows = pl.ds(i * WIDE, WIDE)
        weight_ref[:, rows] = near_ref[:, rows] + lax.dot_general(
            moved, targets_ref[rows, :], (((1,), (1,)), ((), ())), preferred_element_type=f32
        )
        copy_out(i).start()
    for i in range(ROWS // WIDE):
        copy_out(i).wait()


def shape(dims, dtype=f32):
    return jax.ShapeDtypeStruct(dims, dtype)


def on_device(teacher_features, student_features, teacher_weight, student_weight):
    core = lax.rem(lax.axis_index("proto"), 2)
    me = jnp.stack([lax.axis_index("smp"), core]).astype(jnp.int32)
    raw = jnp.concatenate([teacher_features.T, student_features.T], axis=0)
    raw, me = lax.optimization_barrier((raw, me))
    first = gathered(raw, ("yh", "yl", "z"))
    second = gathered(first, ("x",))
    other = lax.ppermute(second, "proto", [(i, i ^ 1) for i in range(64)])

    stage = pltpu.VMEM((ROWS, B), f32)
    wide_sems, near_sems = pltpu.SemaphoreType.DMA((ROWS // WIDE,)), pltpu.SemaphoreType.DMA((ROWS // TILE,))
    row, rows8 = pltpu.VMEM((1, B), f32), pltpu.VMEM((8, B), f32)
    rows8_small = pltpu.VMEM((8, 128), f32)
    matmul = dict(flops=2 * ROWS * B * D, moved=12 * 2**20, exps=ROWS * B)
    kernel, student_unit, sent_1, student_scale, features_own = call(
        first_kernel,
        [pltpu.HBM((ROWS, B), f32), shape((D, B), bf16), pltpu.HBM((64, 8, 128), bf16), shape((8, 128)),
         shape((D, 128))],
        [SMEM, VMEM, VMEM, ANY],
        [ANY, VMEM, ANY, VMEM, VMEM],
        [pltpu.VMEM((D, B), bf16), pltpu.VMEM((ROWS, D), bf16), stage, pltpu.VMEM((64, 8, 128), bf16), rows8,
         wide_sems, wide_sems, pltpu.SemaphoreType.DMA],
        **matmul,
    )(me, second, other, far(teacher_weight))
    got_1 = sent_to_protos(sent_1)
    logits, logits_own, local_total = call(
        student_kernel,
        [pltpu.HBM((ROWS, B), f32), pltpu.HBM((ROWS, 128), f32), shape((8, 128))],
        [SMEM, VMEM, VMEM],
        [ANY, ANY, VMEM],
        [stage, pltpu.VMEM((ROWS, 128), f32), rows8, wide_sems, wide_sems],
        **matmul,
    )(me, student_unit, student_weight)
    kernel_near, sent_2, kept = call(
        second_kernel,
        [pltpu.VMEM((ROWS, B), f32), shape((64, 24, 128), bf16), shape((8, 128))],
        [VMEM, ANY, VMEM],
        None,
        [row, rows8, near_sems],
        flops=4 * ROWS * B,
        moved=8 * 2**20,
    )(got_1, far(kernel), local_total)
    got_2 = sent_to_protos(sent_2)
    sent_3, total, before = call(
        third_kernel,
        [pltpu.HBM((64, 32, 128), bf16), shape((8, 128)), shape((8, 128))],
        [SMEM] + [VMEM] * 6,
        [ANY, VMEM, VMEM],
        [row, rows8, pltpu.VMEM((ROWS, 128), f32), pltpu.VMEM((ROWS, 256), bf16),
         pltpu.VMEM((64, 32, 128), bf16), pltpu.SemaphoreType.DMA((64 // QUARTER,))],
        flops=2 * ROWS * 256 * D,
        moved=12 * 2**20,
        exps=ROWS * 128,
    )(me, got_2, kernel_near, kept, logits_own, features_own, student_weight)
    got_3 = sent_to_protos(sent_3)
    weight_near, targets = streamed(
        weight_kernel,
        [shape((64, ROWS)), pltpu.HBM((ROWS, B), bf16)],
        [stripe(B), stripe(B), whole(8, 128), whole(8, 128), pl.BlockSpec((64, B), lambda i, me: (me[0], 0))],
        [pl.BlockSpec((64, TILE), lambda i, me: (0, i)), stripe(B)],
        [rows8],
        flops=2 * ROWS * B * 64,
        moved=21 * 2**20,
        exps=ROWS * B,
    )(me, far(kernel), far(logits), total, before, student_unit)
    grad_features, loss, grad_weight = call(
        final_kernel,
        [shape((8, 128)), shape((1, 128)), pltpu.HBM((64, ROWS), f32)],
        [SMEM] + [VMEM] * 7 + [ANY],
        [VMEM, VMEM, ANY],
        [rows8_small, pltpu.VMEM((ROWS, B), bf16), pltpu.VMEM((64, ROWS), f32), wide_sems, wide_sems],
        flops=2 * ROWS * B * 64,
        moved=5 * 2**20,
    )(
        me, got_3, student_features.T, student_scale, total, before, student_unit, weight_near, far(targets)
    )
    return loss.reshape(128), grad_features.T, grad_weight.T


def solution(mesh):
    placed = (P("smp", "proto"), P("smp", "proto"), P("proto", None), P("proto", None))
    return jax.shard_map(
        on_device,
        mesh=mesh,
        in_specs=placed,
        out_specs=(P("smp"), P("smp", "proto"), P("proto", "smp")),
        check_vma=False,
    )
```

```python
import jax
import jax.numpy as jnp
import numpy as np
from jax import lax
from jax.experimental import pallas as pl
from jax.experimental.pallas import tpu as pltpu
from jax.sharding import PartitionSpec as P

ITERS = 3
TEACHER_TEMP = 0.07
STUDENT_TEMP = 0.1
BOTH = ("smp", "proto")
PARTS = {"x": 4, "yh": 2, "yl": 4, "z": 8, "c": 2}
B, K, D = 1024, 131072, 512
ROWS = 2048
SHARE = 1.0 / (1024 * 0.1)
TILE = 256
WIDE = 512
BLOCKS = 8
f32, bf16 = jnp.float32, jnp.bfloat16
VMEM = pl.BlockSpec(memory_space=pltpu.VMEM)
SMEM = pl.BlockSpec(memory_space=pltpu.SMEM)
ANY = pl.BlockSpec(memory_space=pl.ANY)


def groups(names):
    order = list(PARTS)
    index = np.arange(512).reshape(tuple(PARTS.values()))
    inner = [order.index(n) for n in names]
    outer = [i for i in range(len(order)) if i not in inner]
    size = int(np.prod([PARTS[n] for n in names]))
    return index.transpose(outer + inner).reshape(-1, size).tolist()


def gathered(x, names):
    group = groups(names)
    copies = jnp.broadcast_to(x[None], (len(group[0]), *x.shape))
    return lax.all_to_all(copies, BOTH, 0, 0, tiled=True, axis_index_groups=group)


def sent_to_protos(x):
    return lax.all_to_all(x, "proto", 0, 0, tiled=True)


def far(x):
    return pltpu.with_memory_space_constraint(x, pltpu.HBM)


def limits():
    return pltpu.CompilerParams(vmem_limit_bytes=24 * 2**20)


def cost(flops=0, moved=0, exps=0):
    return pl.CostEstimate(flops=flops, bytes_accessed=moved, transcendentals=exps)


def call(body, outs, ins, out_specs=None, scratch=(), **work):
    return pl.pallas_call(
        body,
        out_shape=outs,
        in_specs=ins,
        out_specs=out_specs or [VMEM] * len(outs),
        scratch_shapes=scratch,
        compiler_params=limits(),
        cost_estimate=cost(**work),
    )


def streamed(body, outs, ins, out_specs, scratch=(), **work):
    return pl.pallas_call(
        body,
        out_shape=outs,
        grid_spec=pltpu.PrefetchScalarGridSpec(
            num_scalar_prefetch=1,
            grid=(ROWS // TILE,),
            in_specs=ins,
            out_specs=out_specs,
            scratch_shapes=scratch,
        ),
        compiler_params=limits(),
        cost_estimate=cost(**work),
    )


def whole(*dims):
    return pl.BlockSpec(dims, lambda i, me: (0,) * len(dims))


def stripe(width):
    return pl.BlockSpec((TILE, width), lambda i, me: (i, 0))


def features_of(cores, x, yh, which):
    base = yh * 32 if isinstance(yh, int) else pl.multiple_of(yh * 32, 32)
    halves = [ref[x, pl.ds(base, 32)].astype(f32)[:, which * 8 : which * 8 + 8] for ref in cores]
    return jnp.stack(halves, axis=1).reshape(D, 128)


def unit_columns(values):
    scale = lax.rsqrt(jnp.sum(folded(values * values), axis=0, keepdims=True) + 1e-06)
    return (values * scale).astype(bf16), scale


def folded(total):
    return jnp.sum(total.reshape(-1, 8, total.shape[1]), axis=0)


def as_blocks(wide):
    row = jnp.sum(wide, axis=0, keepdims=True)
    return jnp.concatenate([row[:, s * 128 : (s + 1) * 128] for s in range(BLOCKS)], axis=0)


def as_row(blocks):
    return jnp.concatenate([blocks[s : s + 1, :] for s in range(BLOCKS)], axis=1)


def fetch_kernel(far_ref, near_ref, sem_ref):
    copies = []
    for i in range(ROWS // WIDE):
        rows = pl.ds(i * WIDE, WIDE)
        copies.append(pltpu.make_async_copy(far_ref.at[rows], near_ref.at[rows], sem_ref.at[i]))
    for copy in copies:
        copy.start()
    for copy in copies:
        copy.wait()


def first_kernel(
    me_ref, own_ref, other_ref, weight_ref, kernel_out, unit_ref, sent_out, scale_ref, features_ref,
    teacher_ref, stage_ref, sent_ref, mass_ref, sem_ref, sent_sem,
):
    me, core = me_ref[0], me_ref[1]

    def by_core(body):
        @pl.when(core == 0)
        def _():
            body((own_ref, other_ref))

        @pl.when(core == 1)
        def _():
            body((other_ref, own_ref))

    def teacher_units(cores):
        for s in range(BLOCKS):
            values = features_of(cores, s // 2, s % 2, 0)
            teacher_ref[:, s * 128 : (s + 1) * 128] = unit_columns(values)[0]

    def student_units(cores):
        for s in range(BLOCKS):
            values = features_of(cores, s // 2, s % 2, 1)
            unit, scale = unit_columns(values)
            unit_ref[:, s * 128 : (s + 1) * 128] = unit
            scale_ref[s : s + 1, :] = scale
        features_ref[...] = features_of(cores, me // 2, lax.rem(me, 2), 1)

    def copy_out(i):
        rows = pl.ds(pl.multiple_of(i * WIDE, WIDE), WIDE)
        return pltpu.make_async_copy(stage_ref.at[rows], kernel_out.at[rows], sem_ref.at[i])

    by_core(teacher_units)
    mass_ref[...] = jnp.zeros_like(mass_ref)

    @pl.loop(0, ROWS // WIDE)
    def _(i):
        rows = pl.ds(pl.multiple_of(i * WIDE, WIDE), WIDE)
        kernel = jnp.exp(
            jnp.dot(weight_ref[rows, :], teacher_ref[...], preferred_element_type=f32) * (1.0 / TEACHER_TEMP)
        )
        stage_ref[rows, :] = kernel
        copy_out(i).start()
        row_scale = 1.0 / (K * jnp.sum(kernel, axis=1, keepdims=True))
        mass_ref[...] += folded(kernel * row_scale)

    sent_ref[...] = jnp.broadcast_to(as_blocks(mass_ref[...]).astype(bf16)[None], sent_ref.shape)
    sent_copy = pltpu.make_async_copy(sent_ref, sent_out, sent_sem)
    sent_copy.start()
    by_core(student_units)
    sent_copy.wait()
    for i in range(ROWS // WIDE):
        copy_out(i).wait()


def student_kernel(
    me_ref, unit_ref, weight_ref, logits_out, own_out, total_ref, stage_ref, own_ref, sum_ref, sem_ref, own_sem
):
    sum_ref[...] = jnp.zeros_like(sum_ref)
    lanes = pl.ds(pl.multiple_of(me_ref[0] * 128, 128), 128)

    def copies(i):
        rows = pl.ds(pl.multiple_of(i * WIDE, WIDE), WIDE)
        return (
            pltpu.make_async_copy(stage_ref.at[rows], logits_out.at[rows], sem_ref.at[i]),
            pltpu.make_async_copy(own_ref.at[rows], own_out.at[rows], own_sem.at[i]),
        )

    @pl.loop(0, ROWS // WIDE)
    def _(i):
        rows = pl.ds(pl.multiple_of(i * WIDE, WIDE), WIDE)
        logits = jnp.dot(weight_ref[rows, :], unit_ref[...], preferred_element_type=f32) * (1.0 / STUDENT_TEMP)
        stage_ref[rows, :] = logits
        own_ref[rows, :] = stage_ref[rows, lanes]
        for copy in copies(i):
            copy.start()
        sum_ref[...] += folded(jnp.exp(logits))

    total_ref[...] = as_blocks(sum_ref[...])
    for i in range(ROWS // WIDE):
        for copy in copies(i):
            copy.wait()


def received(got_ref):
    return jnp.sum(got_ref[...].astype(f32), axis=0)


def second_kernel(got_ref, far_ref, total_ref, kernel_ref, sent_ref, kept_ref, col_ref, mass_ref, sem_ref):
    def copy_in(i):
        rows = pl.ds(pl.multiple_of(i * TILE, TILE), TILE)
        return pltpu.make_async_copy(far_ref.at[rows], kernel_ref.at[rows], sem_ref.at[i])

    for i in range(ROWS // TILE):
        copy_in(i).start()
    col_ref[...] = as_row(1.0 / (B * received(got_ref)))
    mass_ref[...] = jnp.zeros_like(mass_ref)

    @pl.loop(0, ROWS // TILE)
    def _(i):
        copy_in(i).wait()
        kernel = kernel_ref[pl.ds(pl.multiple_of(i * TILE, TILE), TILE), :]
        row_scale = 1.0 / (K * jnp.sum(kernel * col_ref[...], axis=1, keepdims=True))
        mass_ref[...] += folded(kernel * row_scale)

    mass = as_blocks(mass_ref[...]).astype(bf16).astype(f32)
    kept_ref[...] = mass
    total = total_ref[...]
    high = total.astype(bf16).astype(f32)
    packed = jnp.concatenate([mass, high, total - high], axis=0).astype(bf16)
    sent_ref[...] = jnp.broadcast_to(packed[None], sent_ref.shape)


def split_rows(value):
    high = value.astype(bf16).astype(f32)
    return [high, value - high]


def third_kernel(
    me_ref, got_ref, kernel_ref, kept_ref, logits_ref, features_ref, weight_ref,
    sent_ref, total_ref, before_ref, col_ref, mass_ref, scaled_ref, pair_ref,
):
    me = me_ref[0]
    got = received(got_ref)
    before_ref[...] = got[:8, :]
    total_ref[...] = got[8:16, :] + got[16:, :]
    col_ref[...] = as_row(1.0 / (B * got[:8, :]))
    mass_ref[...] = jnp.zeros_like(mass_ref)
    lanes = pl.ds(pl.multiple_of(me * 128, 128), 128)

    @pl.loop(0, ROWS // TILE)
    def _(i):
        rows = pl.ds(pl.multiple_of(i * TILE, TILE), TILE)
        kernel = kernel_ref[rows, :]
        row_scale = 1.0 / (K * jnp.sum(kernel * col_ref[...], axis=1, keepdims=True))
        scaled_ref[rows, :] = kernel_ref[rows, lanes] * row_scale
        mass_ref[...] += folded(kernel * row_scale)

    change = as_blocks(mass_ref[...]) - kept_ref[...]
    logits = logits_ref[...]
    own_col = 1.0 / before_ref[pl.ds(me, 1), :]
    own_total = 1.0 / total_ref[pl.ds(me, 1), :]
    targets = scaled_ref[...] * own_col
    weighted = jnp.sum(folded(targets * logits), axis=0, keepdims=True)
    pair_ref[:, :128] = ((jnp.exp(logits) * own_total - targets) * SHARE).astype(bf16)
    pair_ref[:, 128:] = (targets * SHARE).astype(bf16)
    parts = lax.dot_general(
        pair_ref[...], weight_ref[...], (((0,), (0,)), ((), ())), preferred_element_type=f32
    )
    grad_part, target_part = parts[:128, :].T, parts[128:, :].T
    features = features_ref[...]
    inner_grad = jnp.sum(folded(features * grad_part), axis=0, keepdims=True)
    inner_target = jnp.sum(folded(features * target_part), axis=0, keepdims=True)
    extra = jnp.concatenate(
        split_rows(inner_grad) + split_rows(inner_target) + split_rows(weighted) + [jnp.zeros((2, 128), f32)],
        axis=0,
    )

    def everywhere(rows):
        return jnp.broadcast_to(rows[None], (64, 8, 128))

    sent_ref[...] = jnp.concatenate(
        [everywhere(change), grad_part.reshape(64, 8, 128), target_part.reshape(64, 8, 128), everywhere(extra)],
        axis=1,
    ).astype(bf16)


def weight_kernel(
    me_ref, kernel_ref, logits_ref, total_ref, before_ref, unit_ref, out_ref, targets_ref, rows_ref
):
    @pl.when(pl.program_id(0) == 0)
    def _():
        rows_ref[0:1, :] = as_row(1.0 / (B * before_ref[...]))
        rows_ref[1:2, :] = as_row(1.0 / before_ref[...])
        rows_ref[2:3, :] = as_row(1.0 / total_ref[...])

    kernel = kernel_ref[...]
    row_scale = 1.0 / (K * jnp.sum(kernel * rows_ref[0:1, :], axis=1, keepdims=True))
    targets = kernel * row_scale * rows_ref[1:2, :]
    probs = jnp.exp(logits_ref[...]) * rows_ref[2:3, :]
    grad = ((probs - targets) * SHARE).astype(bf16)
    targets_ref[...] = (targets * SHARE).astype(bf16)
    out_ref[...] = lax.dot_general(unit_ref[...], grad, (((1,), (1,)), ((), ())), preferred_element_type=f32)


def final_kernel(
    me_ref, got_ref, features_ref, scale_ref, total_ref, before_ref, unit_ref, near_ref, targets_far,
    features_out, loss_out, weight_out, change_ref, targets_ref, sem_ref,
):
    def copy_in(i):
        rows = pl.ds(i * WIDE, WIDE)
        return pltpu.make_async_copy(targets_far.at[rows], targets_ref.at[rows], sem_ref.at[i])

    for i in range(ROWS // WIDE):
        copy_in(i).start()
    me = me_ref[0]
    got = received(got_ref)
    before = before_ref[...]
    change_ref[...] = got[:8] / (before + got[:8])
    own = change_ref[pl.ds(me, 1), :]
    unit_grad = got[8:16] + own * got[16:24]
    inner = (got[24:25] + got[25:26]) + own * (got[26:27] + got[27:28])
    scale = scale_ref[pl.ds(me, 1), :]
    features_out[...] = scale * unit_grad - (scale * scale * scale * inner) * features_ref[...].astype(f32)
    loss_out[...] = jnp.log(total_ref[pl.ds(me, 1), :]) - (1.0 - own) * (got[28:29] + got[29:30])
    units = unit_ref[pl.ds(pl.multiple_of(me * 64, 64), 64), :].astype(f32)
    moved = (units * as_row(change_ref[...])).astype(bf16)
    for i in range(ROWS // WIDE):
        copy_in(i).wait()
        rows = pl.ds(i * WIDE, WIDE)
        weight_out[:, rows] = near_ref[:, rows] + lax.dot_general(
            moved, targets_ref[rows, :], (((1,), (1,)), ((), ())), preferred_element_type=f32
        )


def shape(dims, dtype=f32):
    return jax.ShapeDtypeStruct(dims, dtype)


def on_device(teacher_features, student_features, teacher_weight, student_weight):
    core = lax.rem(lax.axis_index("proto"), 2)
    me = jnp.stack([lax.axis_index("smp"), core]).astype(jnp.int32)
    raw = jnp.concatenate([teacher_features.T, student_features.T], axis=0)
    raw, me = lax.optimization_barrier((raw, me))
    first = gathered(raw, ("yh", "yl", "z"))
    second = gathered(first, ("x",))
    second, teacher_weight = lax.optimization_barrier((second, teacher_weight))
    other = lax.ppermute(second, "proto", [(i, i ^ 1) for i in range(64)])

    stage = pltpu.VMEM((ROWS, B), f32)
    wide_sems, near_sems = pltpu.SemaphoreType.DMA((ROWS // WIDE,)), pltpu.SemaphoreType.DMA((ROWS // TILE,))
    row, rows8 = pltpu.VMEM((1, B), f32), pltpu.VMEM((8, B), f32)
    rows8_small = pltpu.VMEM((8, 128), f32)
    matmul = dict(flops=2 * ROWS * B * D, moved=12 * 2**20, exps=ROWS * B)
    (weight_near,) = call(
        fetch_kernel, [pltpu.VMEM((ROWS, D), bf16)], [ANY], None, [wide_sems], moved=4 * 2**20
    )(far(teacher_weight))
    kernel, student_unit, sent_1, student_scale, features_own = call(
        first_kernel,
        [pltpu.HBM((ROWS, B), f32), shape((D, B), bf16), pltpu.HBM((64, 8, 128), bf16), shape((8, 128)),
         shape((D, 128))],
        [SMEM, VMEM, VMEM, VMEM],
        [ANY, VMEM, ANY, VMEM, VMEM],
        [pltpu.VMEM((D, B), bf16), stage, pltpu.VMEM((64, 8, 128), bf16), rows8, wide_sems,
         pltpu.SemaphoreType.DMA],
        **matmul,
    )(me, second, other, weight_near)
    got_1 = sent_to_protos(sent_1)
    logits, logits_own, local_total = call(
        student_kernel,
        [pltpu.HBM((ROWS, B), f32), pltpu.HBM((ROWS, 128), f32), shape((8, 128))],
        [SMEM, VMEM, VMEM],
        [ANY, ANY, VMEM],
        [stage, pltpu.VMEM((ROWS, 128), f32), rows8, wide_sems, wide_sems],
        **matmul,
    )(me, student_unit, student_weight)
    kernel_near, sent_2, kept = call(
        second_kernel,
        [pltpu.VMEM((ROWS, B), f32), shape((64, 24, 128), bf16), shape((8, 128))],
        [VMEM, ANY, VMEM],
        None,
        [row, rows8, near_sems],
        flops=4 * ROWS * B,
        moved=8 * 2**20,
    )(got_1, far(kernel), local_total)
    got_2 = sent_to_protos(sent_2)
    sent_3, total, before = call(
        third_kernel,
        [shape((64, 32, 128), bf16), shape((8, 128)), shape((8, 128))],
        [SMEM] + [VMEM] * 6,
        None,
        [row, rows8, pltpu.VMEM((ROWS, 128), f32), pltpu.VMEM((ROWS, 256), bf16)],
        flops=2 * ROWS * 256 * D,
        moved=12 * 2**20,
        exps=ROWS * 128,
    )(me, got_2, kernel_near, kept, logits_own, features_own, student_weight)
    got_3 = sent_to_protos(sent_3)
    weight_near, targets = streamed(
        weight_kernel,
        [shape((64, ROWS)), pltpu.HBM((ROWS, B), bf16)],
        [stripe(B), stripe(B), whole(8, 128), whole(8, 128), pl.BlockSpec((64, B), lambda i, me: (me[0], 0))],
        [pl.BlockSpec((64, TILE), lambda i, me: (0, i)), stripe(B)],
        [rows8],
        flops=2 * ROWS * B * 64,
        moved=21 * 2**20,
        exps=ROWS * B,
    )(me, far(kernel), far(logits), total, before, student_unit)
    grad_features, loss, grad_weight = call(
        final_kernel,
        [shape((8, 128)), shape((1, 128)), shape((64, ROWS))],
        [SMEM] + [VMEM] * 7 + [ANY],
        None,
        [rows8_small, pltpu.VMEM((ROWS, B), bf16), wide_sems],
        flops=2 * ROWS * B * 64,
        moved=5 * 2**20,
    )(
        me, got_3, student_features.T, student_scale, total, before, student_unit, weight_near, far(targets)
    )
    return loss.reshape(128), grad_features.T, grad_weight.T


def solution(mesh):
    placed = (P("smp", "proto"), P("smp", "proto"), P("proto", None), P("proto", None))
    return jax.shard_map(
        on_device,
        mesh=mesh,
        in_specs=placed,
        out_specs=(P("smp"), P("smp", "proto"), P("proto", "smp")),
        check_vma=False,
    )
```

```python
import jax
import jax.numpy as jnp
import numpy as np
from jax import lax
from jax.experimental import pallas as pl
from jax.experimental.pallas import tpu as pltpu
from jax.sharding import PartitionSpec as P

ITERS = 3
TEACHER_TEMP = 0.07
STUDENT_TEMP = 0.1
BOTH = ("smp", "proto")
PARTS = {"x": 4, "yh": 2, "yl": 4, "z": 8, "c": 2}
B, K, D = 1024, 131072, 512
ROWS = 2048
SHARE = 1.0 / (1024 * 0.1)
TILE = 256
WIDE = 512
HALF = 4
BLOCKS = 8
f32, bf16 = jnp.float32, jnp.bfloat16
VMEM = pl.BlockSpec(memory_space=pltpu.VMEM)
ANY = pl.BlockSpec(memory_space=pl.ANY)


def groups(names):
    order = list(PARTS)
    index = np.arange(512).reshape(tuple(PARTS.values()))
    inner = [order.index(n) for n in names]
    outer = [i for i in range(len(order)) if i not in inner]
    size = int(np.prod([PARTS[n] for n in names]))
    return index.transpose(outer + inner).reshape(-1, size).tolist()


def gathered(x, names):
    group = groups(names)
    copies = jnp.broadcast_to(x[None], (len(group[0]), *x.shape))
    return lax.all_to_all(copies, BOTH, 0, 0, tiled=True, axis_index_groups=group)


def sent_to_protos(x):
    return lax.all_to_all(x, "proto", 0, 0, tiled=True)


def far(x):
    return pltpu.with_memory_space_constraint(x, pltpu.HBM)


def limits():
    return pltpu.CompilerParams(vmem_limit_bytes=24 * 2**20)


def cost(flops=0, moved=0, exps=0):
    return pl.CostEstimate(flops=flops, bytes_accessed=moved, transcendentals=exps)


def call(body, outs, ins, out_specs=None, scratch=(), **work):
    return pl.pallas_call(
        body,
        out_shape=outs,
        in_specs=ins,
        out_specs=out_specs or [VMEM] * len(outs),
        scratch_shapes=scratch,
        compiler_params=limits(),
        cost_estimate=cost(**work),
    )


def streamed(body, outs, ins, out_specs, scratch=(), **work):
    return pl.pallas_call(
        body,
        out_shape=outs,
        grid=(ROWS // TILE,),
        in_specs=ins,
        out_specs=out_specs,
        scratch_shapes=scratch,
        compiler_params=limits(),
        cost_estimate=cost(**work),
    )


def whole(*dims):
    return pl.BlockSpec(dims, lambda i: (0,) * len(dims))


def stripe(width):
    return pl.BlockSpec((TILE, width), lambda i: (i, 0))


def features_of(cores, x, yh, which):
    base = yh * 32 if isinstance(yh, int) else pl.multiple_of(yh * 32, 32)
    halves = [ref[x, pl.ds(base, 32)].astype(f32)[:, which * 8 : which * 8 + 8] for ref in cores]
    return jnp.stack(halves, axis=1).reshape(D, 128)


def unit_columns(values):
    scale = lax.rsqrt(jnp.sum(folded(values * values), axis=0, keepdims=True) + 1e-06)
    return (values * scale).astype(bf16), scale


def folded(total):
    return jnp.sum(total.reshape(-1, 8, total.shape[1]), axis=0)


def as_blocks(wide):
    row = jnp.sum(wide, axis=0, keepdims=True)
    return jnp.concatenate([row[:, s * 128 : (s + 1) * 128] for s in range(BLOCKS)], axis=0)


def as_row(blocks):
    return jnp.concatenate([blocks[s : s + 1, :] for s in range(BLOCKS)], axis=1)


def fetch_kernel(far_ref, near_ref, sem_ref):
    copies = []
    for i in range(ROWS // WIDE):
        rows = pl.ds(i * WIDE, WIDE)
        copies.append(pltpu.make_async_copy(far_ref.at[rows], near_ref.at[rows], sem_ref.at[i]))
    for copy in copies:
        copy.start()
    for copy in copies:
        copy.wait()


def first_kernel(
    own_ref, other_ref, weight_ref, kernel_out, unit_ref, sent_out, scale_ref, features_ref,
    teacher_ref, stage_ref, sent_ref, mass_ref, sem_ref, sent_sem,
):
    me, core = lax.axis_index("smp"), lax.rem(lax.axis_index("proto"), 2)

    def by_core(body):
        @pl.when(core == 0)
        def _():
            body((own_ref, other_ref))

        @pl.when(core == 1)
        def _():
            body((other_ref, own_ref))

    def teacher_units(cores):
        for s in range(BLOCKS):
            values = features_of(cores, s // 2, s % 2, 0)
            teacher_ref[:, s * 128 : (s + 1) * 128] = unit_columns(values)[0]

    def student_units(cores):
        for s in range(BLOCKS):
            values = features_of(cores, s // 2, s % 2, 1)
            unit, scale = unit_columns(values)
            unit_ref[:, s * 128 : (s + 1) * 128] = unit
            scale_ref[s : s + 1, :] = scale
        features_ref[...] = features_of(cores, me // 2, lax.rem(me, 2), 1)

    def copy_out(i):
        rows = pl.ds(pl.multiple_of(i * WIDE, WIDE), WIDE)
        return pltpu.make_async_copy(stage_ref.at[rows], kernel_out.at[rows], sem_ref.at[i])

    by_core(teacher_units)
    mass_ref[...] = jnp.zeros_like(mass_ref)

    @pl.loop(0, ROWS // WIDE)
    def _(i):
        rows = pl.ds(pl.multiple_of(i * WIDE, WIDE), WIDE)
        kernel = jnp.exp(
            jnp.dot(weight_ref[rows, :], teacher_ref[...], preferred_element_type=f32) * (1.0 / TEACHER_TEMP)
        )
        stage_ref[rows, :] = kernel
        copy_out(i).start()
        row_scale = 1.0 / (K * jnp.sum(kernel, axis=1, keepdims=True))
        mass_ref[...] += folded(kernel * row_scale)

    sent_ref[...] = jnp.broadcast_to(as_blocks(mass_ref[...]).astype(bf16)[None], sent_ref.shape)
    sent_copy = pltpu.make_async_copy(sent_ref, sent_out, sent_sem)
    sent_copy.start()
    by_core(student_units)
    sent_copy.wait()
    for i in range(ROWS // WIDE):
        copy_out(i).wait()


def student_kernel(
    unit_ref, weight_ref, logits_out, own_out, total_ref, stage_ref, own_ref, sum_ref, sem_ref, own_sem
):
    sum_ref[...] = jnp.zeros_like(sum_ref)
    lanes = pl.ds(pl.multiple_of(lax.axis_index("smp") * 128, 128), 128)

    def copies(i):
        rows = pl.ds(pl.multiple_of(i * WIDE, WIDE), WIDE)
        return (
            pltpu.make_async_copy(stage_ref.at[rows], logits_out.at[rows], sem_ref.at[i]),
            pltpu.make_async_copy(own_ref.at[rows], own_out.at[rows], own_sem.at[i]),
        )

    @pl.loop(0, ROWS // WIDE)
    def _(i):
        rows = pl.ds(pl.multiple_of(i * WIDE, WIDE), WIDE)
        logits = jnp.dot(weight_ref[rows, :], unit_ref[...], preferred_element_type=f32) * (1.0 / STUDENT_TEMP)
        stage_ref[rows, :] = logits
        own_ref[rows, :] = stage_ref[rows, lanes]
        for copy in copies(i):
            copy.start()
        sum_ref[...] += folded(jnp.exp(logits))

    total_ref[...] = as_blocks(sum_ref[...])
    for i in range(ROWS // WIDE):
        for copy in copies(i):
            copy.wait()


def received(got_ref):
    return jnp.sum(got_ref[...].astype(f32), axis=0)


def second_kernel(got_ref, far_ref, total_ref, kernel_ref, sent_ref, kept_ref, col_ref, mass_ref, sem_ref):
    def copy_in(i):
        rows = pl.ds(pl.multiple_of(i * TILE, TILE), TILE)
        return pltpu.make_async_copy(far_ref.at[rows], kernel_ref.at[rows], sem_ref.at[i])

    for i in range(ROWS // TILE):
        copy_in(i).start()
    col_ref[...] = as_row(1.0 / (B * received(got_ref)))
    mass_ref[...] = jnp.zeros_like(mass_ref)

    @pl.loop(0, ROWS // TILE)
    def _(i):
        copy_in(i).wait()
        kernel = kernel_ref[pl.ds(pl.multiple_of(i * TILE, TILE), TILE), :]
        row_scale = 1.0 / (K * jnp.sum(kernel * col_ref[...], axis=1, keepdims=True))
        mass_ref[...] += folded(kernel * row_scale)

    mass = as_blocks(mass_ref[...]).astype(bf16).astype(f32)
    kept_ref[...] = mass
    total = total_ref[...]
    high = total.astype(bf16).astype(f32)
    packed = jnp.concatenate([mass, high, total - high], axis=0).astype(bf16)
    sent_ref[...] = jnp.broadcast_to(packed[None], sent_ref.shape)


def split_rows(value):
    high = value.astype(bf16).astype(f32)
    return [high, value - high]


def third_kernel(
    got_ref, kernel_ref, kept_ref, logits_ref, features_ref, weight_ref,
    sent_ref, total_ref, before_ref, col_ref, mass_ref, scaled_ref, pair_ref,
):
    me = lax.axis_index("smp")
    got = received(got_ref)
    before_ref[...] = got[:8, :]
    total_ref[...] = got[8:16, :] + got[16:, :]
    col_ref[...] = as_row(1.0 / (B * got[:8, :]))
    mass_ref[...] = jnp.zeros_like(mass_ref)
    lanes = pl.ds(pl.multiple_of(me * 128, 128), 128)

    @pl.loop(0, ROWS // TILE)
    def _(i):
        rows = pl.ds(pl.multiple_of(i * TILE, TILE), TILE)
        kernel = kernel_ref[rows, :]
        row_scale = 1.0 / (K * jnp.sum(kernel * col_ref[...], axis=1, keepdims=True))
        scaled_ref[rows, :] = kernel_ref[rows, lanes] * row_scale
        mass_ref[...] += folded(kernel * row_scale)

    change = as_blocks(mass_ref[...]) - kept_ref[...]
    logits = logits_ref[...]
    own_col = 1.0 / before_ref[pl.ds(me, 1), :]
    own_total = 1.0 / total_ref[pl.ds(me, 1), :]
    targets = scaled_ref[...] * own_col
    weighted = jnp.sum(folded(targets * logits), axis=0, keepdims=True)
    pair_ref[:, :128] = ((jnp.exp(logits) * own_total - targets) * SHARE).astype(bf16)
    pair_ref[:, 128:] = (targets * SHARE).astype(bf16)
    parts = lax.dot_general(
        pair_ref[...], weight_ref[...], (((0,), (0,)), ((), ())), preferred_element_type=f32
    )
    grad_part, target_part = parts[:128, :].T, parts[128:, :].T
    features = features_ref[...]
    inner_grad = jnp.sum(folded(features * grad_part), axis=0, keepdims=True)
    inner_target = jnp.sum(folded(features * target_part), axis=0, keepdims=True)
    extra = jnp.concatenate(
        split_rows(inner_grad) + split_rows(inner_target) + split_rows(weighted) + [jnp.zeros((2, 128), f32)],
        axis=0,
    )

    def everywhere(rows):
        return jnp.broadcast_to(rows[None], (64, 8, 128))

    sent_ref[...] = jnp.concatenate(
        [everywhere(change), grad_part.reshape(64, 8, 128), target_part.reshape(64, 8, 128), everywhere(extra)],
        axis=1,
    ).astype(bf16)


def weight_kernel(
    kernel_ref, logits_ref, total_ref, before_ref, unit_ref, out_ref, near_ref, far_ref, slice_ref, rows_ref
):
    @pl.when(pl.program_id(0) == 0)
    def _():
        rows_ref[0:1, :] = as_row(1.0 / (B * before_ref[...]))
        rows_ref[1:2, :] = as_row(1.0 / before_ref[...])
        rows_ref[2:3, :] = as_row(1.0 / total_ref[...])

    kernel = kernel_ref[...]
    row_scale = 1.0 / (K * jnp.sum(kernel * rows_ref[0:1, :], axis=1, keepdims=True))
    targets = kernel * row_scale * rows_ref[1:2, :]
    probs = jnp.exp(logits_ref[...]) * rows_ref[2:3, :]
    grad = ((probs - targets) * SHARE).astype(bf16)
    shared = (targets * SHARE).astype(bf16)

    @pl.when(pl.program_id(0) < HALF)
    def _():
        near_ref[...] = shared

    @pl.when(pl.program_id(0) >= HALF)
    def _():
        far_ref[...] = shared

    units = unit_ref[pl.ds(pl.multiple_of(lax.axis_index("smp") * 64, 64), 64), :]
    slice_ref[...] = units
    out_ref[...] = lax.dot_general(units, grad, (((1,), (1,)), ((), ())), preferred_element_type=f32)


def final_kernel(
    got_ref, features_ref, scale_ref, total_ref, before_ref, unit_ref, near_ref, held_ref, targets_far,
    features_out, loss_out, weight_out, change_ref, targets_ref, sem_ref,
):
    def copy_in(i):
        rows = pl.ds(i * TILE, TILE)
        return pltpu.make_async_copy(targets_far.at[rows], targets_ref.at[rows], sem_ref.at[i])

    for i in range(ROWS // TILE - HALF):
        copy_in(i).start()
    me = lax.axis_index("smp")
    got = received(got_ref)
    before = before_ref[...]
    change_ref[...] = got[:8] / (before + got[:8])
    own = change_ref[pl.ds(me, 1), :]
    unit_grad = got[8:16] + own * got[16:24]
    inner = (got[24:25] + got[25:26]) + own * (got[26:27] + got[27:28])
    scale = scale_ref[pl.ds(me, 1), :]
    features_out[...] = scale * unit_grad - (scale * scale * scale * inner) * features_ref[...].astype(f32)
    loss_out[...] = jnp.log(total_ref[pl.ds(me, 1), :]) - (1.0 - own) * (got[28:29] + got[29:30])
    moved = (unit_ref[...].astype(f32) * as_row(change_ref[...])).astype(bf16)

    def correct(start, targets):
        rows = pl.ds(start, targets.shape[0])
        weight_out[:, rows] = near_ref[:, rows] + lax.dot_general(
            moved, targets, (((1,), (1,)), ((), ())), preferred_element_type=f32
        )

    for i in range(HALF):
        correct(i * TILE, held_ref[pl.ds(i * TILE, TILE), :])
    for i in range(ROWS // TILE - HALF):
        copy_in(i).wait()
        correct((HALF + i) * TILE, targets_ref[pl.ds(i * TILE, TILE), :])


def shape(dims, dtype=f32):
    return jax.ShapeDtypeStruct(dims, dtype)


def on_device(teacher_features, student_features, teacher_weight, student_weight):
    raw = jnp.concatenate([teacher_features.T, student_features.T], axis=0)
    first = gathered(raw, ("yh", "yl", "z"))
    second = gathered(first, ("x",))
    second, teacher_weight = lax.optimization_barrier((second, teacher_weight))
    other = lax.ppermute(second, "proto", [(i, i ^ 1) for i in range(64)])

    stage = pltpu.VMEM((ROWS, B), f32)
    wide_sems, near_sems = pltpu.SemaphoreType.DMA((ROWS // WIDE,)), pltpu.SemaphoreType.DMA((ROWS // TILE,))
    row, rows8 = pltpu.VMEM((1, B), f32), pltpu.VMEM((8, B), f32)
    rows8_small = pltpu.VMEM((8, 128), f32)
    matmul = dict(flops=2 * ROWS * B * D, moved=12 * 2**20, exps=ROWS * B)
    (weight_near,) = call(
        fetch_kernel, [pltpu.VMEM((ROWS, D), bf16)], [ANY], None, [wide_sems], moved=4 * 2**20
    )(far(teacher_weight))
    kernel, student_unit, sent_1, student_scale, features_own = call(
        first_kernel,
        [pltpu.HBM((ROWS, B), f32), shape((D, B), bf16), pltpu.HBM((64, 8, 128), bf16), shape((8, 128)),
         shape((D, 128))],
        [VMEM, VMEM, VMEM],
        [ANY, VMEM, ANY, VMEM, VMEM],
        [pltpu.VMEM((D, B), bf16), stage, pltpu.VMEM((64, 8, 128), bf16), rows8, wide_sems,
         pltpu.SemaphoreType.DMA],
        **matmul,
    )(second, other, weight_near)
    got_1 = sent_to_protos(sent_1)
    logits, logits_own, local_total = call(
        student_kernel,
        [pltpu.HBM((ROWS, B), f32), pltpu.HBM((ROWS, 128), f32), shape((8, 128))],
        [VMEM, VMEM],
        [ANY, ANY, VMEM],
        [stage, pltpu.VMEM((ROWS, 128), f32), rows8, wide_sems, wide_sems],
        **matmul,
    )(student_unit, student_weight)
    kernel_near, sent_2, kept = call(
        second_kernel,
        [pltpu.VMEM((ROWS, B), f32), shape((64, 24, 128), bf16), shape((8, 128))],
        [VMEM, ANY, VMEM],
        None,
        [row, rows8, near_sems],
        flops=4 * ROWS * B,
        moved=8 * 2**20,
    )(got_1, far(kernel), local_total)
    got_2 = sent_to_protos(sent_2)
    sent_3, total, before = call(
        third_kernel,
        [shape((64, 32, 128), bf16), shape((8, 128)), shape((8, 128))],
        [VMEM] * 6,
        None,
        [row, rows8, pltpu.VMEM((ROWS, 128), f32), pltpu.VMEM((ROWS, 256), bf16)],
        flops=2 * ROWS * 256 * D,
        moved=12 * 2**20,
        exps=ROWS * 128,
    )(got_2, kernel_near, kept, logits_own, features_own, student_weight)
    got_3 = sent_to_protos(sent_3)
    partial, targets_near, targets_far, unit_slice = streamed(
        weight_kernel,
        [shape((64, ROWS)), pltpu.VMEM((HALF * TILE, B), bf16), pltpu.HBM((ROWS - HALF * TILE, B), bf16),
         shape((64, B), bf16)],
        [stripe(B), stripe(B), whole(8, 128), whole(8, 128), whole(D, B)],
        [pl.BlockSpec((64, TILE), lambda i: (0, i)),
         pl.BlockSpec((TILE, B), lambda i: (jnp.minimum(i, HALF - 1), 0)),
         pl.BlockSpec((TILE, B), lambda i: (jnp.maximum(i - HALF, 0), 0)), whole(64, B)],
        [rows8],
        flops=2 * ROWS * B * 64,
        moved=21 * 2**20,
        exps=ROWS * B,
    )(far(kernel), far(logits), total, before, student_unit)
    grad_features, loss, grad_weight = call(
        final_kernel,
        [shape((8, 128)), shape((1, 128)), shape((64, ROWS))],
        [VMEM] * 8 + [ANY],
        None,
        [rows8_small, pltpu.VMEM((ROWS - HALF * TILE, B), bf16), near_sems],
        flops=2 * ROWS * B * 64,
        moved=5 * 2**20,
    )(
        got_3, student_features.T, student_scale, total, before, unit_slice, partial, targets_near,
        far(targets_far),
    )
    return loss.reshape(128), grad_features.T, grad_weight.T


def solution(mesh):
    placed = (P("smp", "proto"), P("smp", "proto"), P("proto", None), P("proto", None))
    return jax.shard_map(
        on_device,
        mesh=mesh,
        in_specs=placed,
        out_specs=(P("smp"), P("smp", "proto"), P("proto", "smp")),
        check_vma=False,
    )
```

```python
import jax
import jax.numpy as jnp
import numpy as np
from jax import lax
from jax.experimental import pallas as pl
from jax.experimental.pallas import tpu as pltpu
from jax.sharding import PartitionSpec as P

ITERS = 3
TEACHER_TEMP = 0.07
STUDENT_TEMP = 0.1
BOTH = ("smp", "proto")
PARTS = {"x": 4, "yh": 2, "yl": 4, "z": 8, "c": 2}
B, K, D = 1024, 131072, 512
ROWS = 2048
SHARE = 1.0 / (1024 * 0.1)
TILE = 256
WIDE = 512
HALF = 4
BLOCKS = 8
f32, bf16 = jnp.float32, jnp.bfloat16
VMEM = pl.BlockSpec(memory_space=pltpu.VMEM)
ANY = pl.BlockSpec(memory_space=pl.ANY)


def groups(names):
    order = list(PARTS)
    index = np.arange(512).reshape(tuple(PARTS.values()))
    inner = [order.index(n) for n in names]
    outer = [i for i in range(len(order)) if i not in inner]
    size = int(np.prod([PARTS[n] for n in names]))
    return index.transpose(outer + inner).reshape(-1, size).tolist()


def gathered(x, names):
    group = groups(names)
    copies = jnp.broadcast_to(x[None], (len(group[0]), *x.shape))
    return lax.all_to_all(copies, BOTH, 0, 0, tiled=True, axis_index_groups=group)


def sent_to_protos(x):
    return lax.all_to_all(x, "proto", 0, 0, tiled=True)


def far(x):
    return pltpu.with_memory_space_constraint(x, pltpu.HBM)


def limits():
    return pltpu.CompilerParams(vmem_limit_bytes=24 * 2**20)


def cost(flops=0, moved=0, exps=0):
    return pl.CostEstimate(flops=flops, bytes_accessed=moved, transcendentals=exps)


def call(body, outs, ins, out_specs=None, scratch=(), **work):
    return pl.pallas_call(
        body,
        out_shape=outs,
        in_specs=ins,
        out_specs=out_specs or [VMEM] * len(outs),
        scratch_shapes=scratch,
        compiler_params=limits(),
        cost_estimate=cost(**work),
    )


def streamed(body, outs, ins, out_specs, scratch=(), **work):
    return pl.pallas_call(
        body,
        out_shape=outs,
        grid=(ROWS // TILE,),
        in_specs=ins,
        out_specs=out_specs,
        scratch_shapes=scratch,
        compiler_params=limits(),
        cost_estimate=cost(**work),
    )


def whole(*dims):
    return pl.BlockSpec(dims, lambda i: (0,) * len(dims))


def stripe(width):
    return pl.BlockSpec((TILE, width), lambda i: (i, 0))


def features_of(cores, x, yh, which):
    base = yh * 32 if isinstance(yh, int) else pl.multiple_of(yh * 32, 32)
    halves = [ref[x, pl.ds(base, 32)].astype(f32)[:, which * 8 : which * 8 + 8] for ref in cores]
    return jnp.stack(halves, axis=1).reshape(D, 128)


def unit_columns(values):
    scale = lax.rsqrt(jnp.sum(folded(values * values), axis=0, keepdims=True) + 1e-06)
    return (values * scale).astype(bf16), scale


def folded(total):
    return jnp.sum(total.reshape(-1, 8, total.shape[1]), axis=0)


def as_blocks(wide):
    row = jnp.sum(wide, axis=0, keepdims=True)
    return jnp.concatenate([row[:, s * 128 : (s + 1) * 128] for s in range(BLOCKS)], axis=0)


def as_row(blocks):
    return jnp.concatenate([blocks[s : s + 1, :] for s in range(BLOCKS)], axis=1)


def fetch_kernel(far_ref, near_ref, sem_ref):
    copies = []
    for i in range(ROWS // WIDE):
        rows = pl.ds(i * WIDE, WIDE)
        copies.append(pltpu.make_async_copy(far_ref.at[rows], near_ref.at[rows], sem_ref.at[i]))
    for copy in copies:
        copy.start()
    for copy in copies:
        copy.wait()


def first_kernel(
    own_ref, other_ref, weight_ref, kernel_out, unit_ref, sent_out, scale_ref, features_ref,
    teacher_ref, stage_ref, sent_ref, mass_ref, sem_ref, sent_sem,
):
    me, core = lax.axis_index("smp"), lax.rem(lax.axis_index("proto"), 2)

    def by_core(body):
        @pl.when(core == 0)
        def _():
            body((own_ref, other_ref))

        @pl.when(core == 1)
        def _():
            body((other_ref, own_ref))

    def teacher_units(cores):
        for s in range(BLOCKS):
            values = features_of(cores, s // 2, s % 2, 0)
            teacher_ref[:, s * 128 : (s + 1) * 128] = unit_columns(values)[0]

    def student_units(cores):
        for s in range(BLOCKS):
            values = features_of(cores, s // 2, s % 2, 1)
            unit, scale = unit_columns(values)
            unit_ref[:, s * 128 : (s + 1) * 128] = unit
            scale_ref[s : s + 1, :] = scale
        features_ref[...] = features_of(cores, me // 2, lax.rem(me, 2), 1)

    def copy_out(i):
        rows = pl.ds(pl.multiple_of(i * WIDE, WIDE), WIDE)
        return pltpu.make_async_copy(stage_ref.at[rows], kernel_out.at[rows], sem_ref.at[i])

    by_core(teacher_units)
    mass_ref[...] = jnp.zeros_like(mass_ref)

    @pl.loop(0, ROWS // WIDE)
    def _(i):
        rows = pl.ds(pl.multiple_of(i * WIDE, WIDE), WIDE)
        kernel = jnp.exp(
            jnp.dot(weight_ref[rows, :], teacher_ref[...], preferred_element_type=f32) * (1.0 / TEACHER_TEMP)
        )
        stage_ref[rows, :] = kernel
        copy_out(i).start()
        row_scale = 1.0 / (K * jnp.sum(kernel, axis=1, keepdims=True))
        mass_ref[...] += folded(kernel * row_scale)

    sent_ref[...] = jnp.broadcast_to(as_blocks(mass_ref[...]).astype(bf16)[None], sent_ref.shape)
    sent_copy = pltpu.make_async_copy(sent_ref, sent_out, sent_sem)
    sent_copy.start()
    by_core(student_units)
    sent_copy.wait()
    for i in range(ROWS // WIDE):
        copy_out(i).wait()


def student_kernel(
    unit_ref, weight_ref, logits_out, own_out, total_ref, stage_ref, own_ref, sum_ref, sem_ref, own_sem
):
    sum_ref[...] = jnp.zeros_like(sum_ref)
    lanes = pl.ds(pl.multiple_of(lax.axis_index("smp") * 128, 128), 128)

    def copies(i):
        rows = pl.ds(pl.multiple_of(i * WIDE, WIDE), WIDE)
        return (
            pltpu.make_async_copy(stage_ref.at[rows], logits_out.at[rows], sem_ref.at[i]),
            pltpu.make_async_copy(own_ref.at[rows], own_out.at[rows], own_sem.at[i]),
        )

    @pl.loop(0, ROWS // WIDE)
    def _(i):
        rows = pl.ds(pl.multiple_of(i * WIDE, WIDE), WIDE)
        logits = jnp.dot(weight_ref[rows, :], unit_ref[...], preferred_element_type=f32) * (1.0 / STUDENT_TEMP)
        stage_ref[rows, :] = logits
        own_ref[rows, :] = stage_ref[rows, lanes]
        for copy in copies(i):
            copy.start()
        sum_ref[...] += folded(jnp.exp(logits))

    total_ref[...] = as_blocks(sum_ref[...])
    for i in range(ROWS // WIDE):
        for copy in copies(i):
            copy.wait()


def received(got_ref):
    return jnp.sum(got_ref[...].astype(f32), axis=0)


def second_kernel(got_ref, far_ref, total_ref, kernel_ref, sent_ref, kept_ref, col_ref, mass_ref, sem_ref):
    def copy_in(i):
        rows = pl.ds(pl.multiple_of(i * TILE, TILE), TILE)
        return pltpu.make_async_copy(far_ref.at[rows], kernel_ref.at[rows], sem_ref.at[i])

    for i in range(ROWS // TILE):
        copy_in(i).start()
    col_ref[...] = as_row(1.0 / (B * received(got_ref)))
    mass_ref[...] = jnp.zeros_like(mass_ref)

    @pl.loop(0, ROWS // TILE)
    def _(i):
        copy_in(i).wait()
        kernel = kernel_ref[pl.ds(pl.multiple_of(i * TILE, TILE), TILE), :]
        row_scale = 1.0 / (K * jnp.sum(kernel * col_ref[...], axis=1, keepdims=True))
        mass_ref[...] += folded(kernel * row_scale)

    mass = as_blocks(mass_ref[...]).astype(bf16).astype(f32)
    kept_ref[...] = mass
    total = total_ref[...]
    step = jnp.exp2(jnp.floor(jnp.log2(total)) - 7.0)
    place = lax.axis_index("proto").astype(f32)
    spread = total + step * ((place + 0.5) * (1.0 / 64) - 0.5)
    packed = jnp.concatenate([mass, spread], axis=0).astype(bf16)
    sent_ref[...] = jnp.broadcast_to(packed[None], sent_ref.shape)


def split_rows(value):
    high = value.astype(bf16).astype(f32)
    return [high, value - high]


def third_kernel(
    got_ref, kernel_ref, kept_ref, logits_ref, features_ref, weight_ref,
    sent_ref, total_ref, before_ref, col_ref, mass_ref, scaled_ref, pair_ref,
):
    me = lax.axis_index("smp")
    got = received(got_ref)
    before_ref[...] = got[:8, :]
    total_ref[...] = got[8:, :]
    col_ref[...] = as_row(1.0 / (B * got[:8, :]))
    mass_ref[...] = jnp.zeros_like(mass_ref)
    lanes = pl.ds(pl.multiple_of(me * 128, 128), 128)

    @pl.loop(0, ROWS // TILE)
    def _(i):
        rows = pl.ds(pl.multiple_of(i * TILE, TILE), TILE)
        kernel = kernel_ref[rows, :]
        row_scale = 1.0 / (K * jnp.sum(kernel * col_ref[...], axis=1, keepdims=True))
        scaled_ref[rows, :] = kernel_ref[rows, lanes] * row_scale
        mass_ref[...] += folded(kernel * row_scale)

    change = as_blocks(mass_ref[...]) - kept_ref[...]
    logits = logits_ref[...]
    own_col = 1.0 / before_ref[pl.ds(me, 1), :]
    own_total = 1.0 / total_ref[pl.ds(me, 1), :]
    targets = scaled_ref[...] * own_col
    weighted = jnp.sum(folded(targets * logits), axis=0, keepdims=True)
    pair_ref[:, :128] = ((jnp.exp(logits) * own_total - targets) * SHARE).astype(bf16)
    pair_ref[:, 128:] = (targets * SHARE).astype(bf16)
    parts = lax.dot_general(
        pair_ref[...], weight_ref[...], (((0,), (0,)), ((), ())), preferred_element_type=f32
    )
    grad_part, target_part = parts[:128, :].T, parts[128:, :].T
    features = features_ref[...]
    inner_grad = jnp.sum(folded(features * grad_part), axis=0, keepdims=True)
    inner_target = jnp.sum(folded(features * target_part), axis=0, keepdims=True)
    extra = jnp.concatenate(
        split_rows(inner_grad) + split_rows(inner_target) + split_rows(weighted) + [jnp.zeros((2, 128), f32)],
        axis=0,
    )

    def everywhere(rows):
        return jnp.broadcast_to(rows[None], (64, 8, 128))

    sent_ref[...] = jnp.concatenate(
        [everywhere(change), grad_part.reshape(64, 8, 128), target_part.reshape(64, 8, 128), everywhere(extra)],
        axis=1,
    ).astype(bf16)


def weight_kernel(
    kernel_ref, logits_ref, total_ref, before_ref, unit_ref, out_ref, near_ref, far_ref, slice_ref, rows_ref
):
    @pl.when(pl.program_id(0) == 0)
    def _():
        rows_ref[0:1, :] = as_row(1.0 / (B * before_ref[...]))
        rows_ref[1:2, :] = as_row(1.0 / before_ref[...])
        rows_ref[2:3, :] = as_row(1.0 / total_ref[...])

    kernel = kernel_ref[...]
    row_scale = 1.0 / (K * jnp.sum(kernel * rows_ref[0:1, :], axis=1, keepdims=True))
    targets = kernel * row_scale * rows_ref[1:2, :]
    probs = jnp.exp(logits_ref[...]) * rows_ref[2:3, :]
    grad = ((probs - targets) * SHARE).astype(bf16)
    shared = (targets * SHARE).astype(bf16)

    @pl.when(pl.program_id(0) < HALF)
    def _():
        near_ref[...] = shared

    @pl.when(pl.program_id(0) >= HALF)
    def _():
        far_ref[...] = shared

    units = unit_ref[pl.ds(pl.multiple_of(lax.axis_index("smp") * 64, 64), 64), :]
    slice_ref[...] = units
    out_ref[...] = lax.dot_general(units, grad, (((1,), (1,)), ((), ())), preferred_element_type=f32)


def final_kernel(
    got_ref, features_ref, scale_ref, total_ref, before_ref, unit_ref, near_ref, held_ref, targets_far,
    features_out, loss_out, weight_out, change_ref, targets_ref, sem_ref,
):
    def copy_in(i):
        rows = pl.ds(i * TILE, TILE)
        return pltpu.make_async_copy(targets_far.at[rows], targets_ref.at[rows], sem_ref.at[i])

    for i in range(ROWS // TILE - HALF):
        copy_in(i).start()
    me = lax.axis_index("smp")
    got = received(got_ref)
    before = before_ref[...]
    change_ref[...] = got[:8] / (before + got[:8])
    own = change_ref[pl.ds(me, 1), :]
    unit_grad = got[8:16] + own * got[16:24]
    inner = (got[24:25] + got[25:26]) + own * (got[26:27] + got[27:28])
    scale = scale_ref[pl.ds(me, 1), :]
    features_out[...] = scale * unit_grad - (scale * scale * scale * inner) * features_ref[...].astype(f32)
    loss_out[...] = jnp.log(total_ref[pl.ds(me, 1), :]) - (1.0 - own) * (got[28:29] + got[29:30])
    moved = (unit_ref[...].astype(f32) * as_row(change_ref[...])).astype(bf16)

    def correct(start, targets):
        rows = pl.ds(start, targets.shape[0])
        weight_out[:, rows] = near_ref[:, rows] + lax.dot_general(
            moved, targets, (((1,), (1,)), ((), ())), preferred_element_type=f32
        )

    for i in range(HALF):
        correct(i * TILE, held_ref[pl.ds(i * TILE, TILE), :])
    for i in range(ROWS // TILE - HALF):
        copy_in(i).wait()
        correct((HALF + i) * TILE, targets_ref[pl.ds(i * TILE, TILE), :])


def shape(dims, dtype=f32):
    return jax.ShapeDtypeStruct(dims, dtype)


def on_device(teacher_features, student_features, teacher_weight, student_weight):
    raw = jnp.concatenate([teacher_features.T, student_features.T], axis=0)
    first = gathered(raw, ("yh", "yl", "z"))
    second = gathered(first, ("x",))
    second, teacher_weight = lax.optimization_barrier((second, teacher_weight))
    other = lax.ppermute(second, "proto", [(i, i ^ 1) for i in range(64)])

    stage = pltpu.VMEM((ROWS, B), f32)
    wide_sems, near_sems = pltpu.SemaphoreType.DMA((ROWS // WIDE,)), pltpu.SemaphoreType.DMA((ROWS // TILE,))
    row, rows8 = pltpu.VMEM((1, B), f32), pltpu.VMEM((8, B), f32)
    rows8_small = pltpu.VMEM((8, 128), f32)
    matmul = dict(flops=2 * ROWS * B * D, moved=12 * 2**20, exps=ROWS * B)
    (weight_near,) = call(
        fetch_kernel, [pltpu.VMEM((ROWS, D), bf16)], [ANY], None, [wide_sems], moved=4 * 2**20
    )(far(teacher_weight))
    kernel, student_unit, sent_1, student_scale, features_own = call(
        first_kernel,
        [pltpu.HBM((ROWS, B), f32), shape((D, B), bf16), pltpu.HBM((64, 8, 128), bf16), shape((8, 128)),
         shape((D, 128))],
        [VMEM, VMEM, VMEM],
        [ANY, VMEM, ANY, VMEM, VMEM],
        [pltpu.VMEM((D, B), bf16), stage, pltpu.VMEM((64, 8, 128), bf16), rows8, wide_sems,
         pltpu.SemaphoreType.DMA],
        **matmul,
    )(second, other, weight_near)
    got_1 = sent_to_protos(sent_1)
    logits, logits_own, local_total = call(
        student_kernel,
        [pltpu.HBM((ROWS, B), f32), pltpu.HBM((ROWS, 128), f32), shape((8, 128))],
        [VMEM, VMEM],
        [ANY, ANY, VMEM],
        [stage, pltpu.VMEM((ROWS, 128), f32), rows8, wide_sems, wide_sems],
        **matmul,
    )(student_unit, student_weight)
    kernel_near, sent_2, kept = call(
        second_kernel,
        [pltpu.VMEM((ROWS, B), f32), shape((64, 16, 128), bf16), shape((8, 128))],
        [VMEM, ANY, VMEM],
        None,
        [row, rows8, near_sems],
        flops=4 * ROWS * B,
        moved=8 * 2**20,
    )(got_1, far(kernel), local_total)
    got_2 = sent_to_protos(sent_2)
    sent_3, total, before = call(
        third_kernel,
        [shape((64, 32, 128), bf16), shape((8, 128)), shape((8, 128))],
        [VMEM] * 6,
        None,
        [row, rows8, pltpu.VMEM((ROWS, 128), f32), pltpu.VMEM((ROWS, 256), bf16)],
        flops=2 * ROWS * 256 * D,
        moved=12 * 2**20,
        exps=ROWS * 128,
    )(got_2, kernel_near, kept, logits_own, features_own, student_weight)
    got_3 = sent_to_protos(sent_3)
    partial, targets_near, targets_far, unit_slice = streamed(
        weight_kernel,
        [shape((64, ROWS)), pltpu.VMEM((HALF * TILE, B), bf16), pltpu.HBM((ROWS - HALF * TILE, B), bf16),
         shape((64, B), bf16)],
        [stripe(B), stripe(B), whole(8, 128), whole(8, 128), whole(D, B)],
        [pl.BlockSpec((64, TILE), lambda i: (0, i)),
         pl.BlockSpec((TILE, B), lambda i: (jnp.minimum(i, HALF - 1), 0)),
         pl.BlockSpec((TILE, B), lambda i: (jnp.maximum(i - HALF, 0), 0)), whole(64, B)],
        [rows8],
        flops=2 * ROWS * B * 64,
        moved=21 * 2**20,
        exps=ROWS * B,
    )(far(kernel), far(logits), total, before, student_unit)
    grad_features, loss, grad_weight = call(
        final_kernel,
        [shape((8, 128)), shape((1, 128)), shape((64, ROWS))],
        [VMEM] * 8 + [ANY],
        None,
        [rows8_small, pltpu.VMEM((ROWS - HALF * TILE, B), bf16), near_sems],
        flops=2 * ROWS * B * 64,
        moved=5 * 2**20,
    )(
        got_3, student_features.T, student_scale, total, before, unit_slice, partial, targets_near,
        far(targets_far),
    )
    return loss.reshape(128), grad_features.T, grad_weight.T


def solution(mesh):
    placed = (P("smp", "proto"), P("smp", "proto"), P("proto", None), P("proto", None))
    return jax.shard_map(
        on_device,
        mesh=mesh,
        in_specs=placed,
        out_specs=(P("smp"), P("smp", "proto"), P("proto", "smp")),
        check_vma=False,
    )
```

```python
import jax
import jax.numpy as jnp
import numpy as np
from jax import lax
from jax.experimental import pallas as pl
from jax.experimental.pallas import tpu as pltpu
from jax.sharding import PartitionSpec as P

ITERS = 3
TEACHER_TEMP = 0.07
STUDENT_TEMP = 0.1
BOTH = ("smp", "proto")
PARTS = {"x": 4, "yh": 2, "yl": 4, "z": 8, "c": 2}
B, K, D = 1024, 131072, 512
ROWS = 2048
SHARE = 1.0 / (1024 * 0.1)
TILE = 256
WIDE = 512
HALF = 4
FAR = 1536
BLOCKS = 8
f32, bf16 = jnp.float32, jnp.bfloat16
VMEM = pl.BlockSpec(memory_space=pltpu.VMEM)
ANY = pl.BlockSpec(memory_space=pl.ANY)


def groups(names):
    order = list(PARTS)
    index = np.arange(512).reshape(tuple(PARTS.values()))
    inner = [order.index(n) for n in names]
    outer = [i for i in range(len(order)) if i not in inner]
    size = int(np.prod([PARTS[n] for n in names]))
    return index.transpose(outer + inner).reshape(-1, size).tolist()


def gathered(x, names):
    group = groups(names)
    copies = jnp.broadcast_to(x[None], (len(group[0]), *x.shape))
    return lax.all_to_all(copies, BOTH, 0, 0, tiled=True, axis_index_groups=group)


def sent_to_protos(x):
    return lax.all_to_all(x, "proto", 0, 0, tiled=True)


def far(x):
    return pltpu.with_memory_space_constraint(x, pltpu.HBM)


def limits():
    return pltpu.CompilerParams(vmem_limit_bytes=24 * 2**20)


def cost(flops=0, moved=0, exps=0):
    return pl.CostEstimate(flops=flops, bytes_accessed=moved, transcendentals=exps)


def call(body, outs, ins, out_specs=None, scratch=(), aliases=None, **work):
    return pl.pallas_call(
        body,
        out_shape=outs,
        in_specs=ins,
        out_specs=out_specs or [VMEM] * len(outs),
        scratch_shapes=scratch,
        input_output_aliases=aliases or {},
        compiler_params=limits(),
        cost_estimate=cost(**work),
    )


def streamed(body, outs, ins, out_specs, scratch=(), **work):
    return pl.pallas_call(
        body,
        out_shape=outs,
        grid=(ROWS // TILE,),
        in_specs=ins,
        out_specs=out_specs,
        scratch_shapes=scratch,
        compiler_params=limits(),
        cost_estimate=cost(**work),
    )


def whole(*dims):
    return pl.BlockSpec(dims, lambda i: (0,) * len(dims))


def stripe(width):
    return pl.BlockSpec((TILE, width), lambda i: (i, 0))


def features_of(cores, x, yh, which):
    base = yh * 32 if isinstance(yh, int) else pl.multiple_of(yh * 32, 32)
    halves = [ref[x, pl.ds(base, 32)].astype(f32)[:, which * 8 : which * 8 + 8] for ref in cores]
    return jnp.stack(halves, axis=1).reshape(D, 128)


def unit_columns(values):
    scale = lax.rsqrt(jnp.sum(folded(values * values), axis=0, keepdims=True) + 1e-06)
    return (values * scale).astype(bf16), scale


def folded(total):
    return jnp.sum(total.reshape(-1, 8, total.shape[1]), axis=0)


def as_blocks(wide):
    row = jnp.sum(wide, axis=0, keepdims=True)
    return jnp.concatenate([row[:, s * 128 : (s + 1) * 128] for s in range(BLOCKS)], axis=0)


def as_row(blocks):
    return jnp.concatenate([blocks[s : s + 1, :] for s in range(BLOCKS)], axis=1)


def fetch_kernel(far_ref, near_ref, sem_ref):
    copies = []
    for i in range(ROWS // WIDE):
        rows = pl.ds(i * WIDE, WIDE)
        copies.append(pltpu.make_async_copy(far_ref.at[rows], near_ref.at[rows], sem_ref.at[i]))
    for copy in copies:
        copy.start()
    for copy in copies:
        copy.wait()


def first_kernel(
    own_ref, other_ref, weight_ref, kernel_out, near_ref, unit_ref, sent_out, scale_ref, features_ref,
    teacher_ref, stage_ref, sent_ref, mass_ref, sem_ref, sent_sem,
):
    me, core = lax.axis_index("smp"), lax.rem(lax.axis_index("proto"), 2)

    def by_core(body):
        @pl.when(core == 0)
        def _():
            body((own_ref, other_ref))

        @pl.when(core == 1)
        def _():
            body((other_ref, own_ref))

    def teacher_units(cores):
        for s in range(BLOCKS):
            values = features_of(cores, s // 2, s % 2, 0)
            teacher_ref[:, s * 128 : (s + 1) * 128] = unit_columns(values)[0]

    def student_units(cores):
        for s in range(BLOCKS):
            values = features_of(cores, s // 2, s % 2, 1)
            unit, scale = unit_columns(values)
            unit_ref[:, s * 128 : (s + 1) * 128] = unit
            scale_ref[s : s + 1, :] = scale
        features_ref[...] = features_of(cores, me // 2, lax.rem(me, 2), 1)

    def copy_out(i):
        rows = pl.ds(pl.multiple_of(i * WIDE, WIDE), WIDE)
        return pltpu.make_async_copy(stage_ref.at[rows], kernel_out.at[rows], sem_ref.at[i])

    by_core(teacher_units)
    mass_ref[...] = jnp.zeros_like(mass_ref)

    def tile(rows, kept_ref, kept_rows):
        kernel = jnp.exp(
            jnp.dot(weight_ref[rows, :], teacher_ref[...], preferred_element_type=f32) * (1.0 / TEACHER_TEMP)
        )
        kept_ref[kept_rows, :] = kernel
        row_scale = 1.0 / (K * jnp.sum(kernel, axis=1, keepdims=True))
        mass_ref[...] += folded(kernel * row_scale)

    @pl.loop(0, FAR // WIDE)
    def _(i):
        rows = pl.ds(pl.multiple_of(i * WIDE, WIDE), WIDE)
        tile(rows, stage_ref, rows)
        copy_out(i).start()

    tile(pl.ds(FAR, ROWS - FAR), near_ref, pl.ds(0, ROWS - FAR))
    sent_ref[...] = jnp.broadcast_to(as_blocks(mass_ref[...]).astype(bf16)[None], sent_ref.shape)
    sent_copy = pltpu.make_async_copy(sent_ref, sent_out, sent_sem)
    sent_copy.start()
    by_core(student_units)
    sent_copy.wait()
    for i in range(FAR // WIDE):
        copy_out(i).wait()


def student_kernel(
    unit_ref, weight_far, near_ref, kernel_ref, logits_out, own_out, total_ref, kernel_out,
    weight_ref, stage_ref, own_ref, sum_ref, sem_ref, own_sem, weight_sem, near_sem,
):
    def copy_in(i):
        rows = pl.ds(pl.multiple_of(i * WIDE, WIDE), WIDE)
        return pltpu.make_async_copy(weight_far.at[rows], weight_ref.at[rows], weight_sem.at[i])

    for i in range(ROWS // WIDE):
        copy_in(i).start()
    near_copy = pltpu.make_async_copy(near_ref, kernel_out.at[pl.ds(FAR, ROWS - FAR)], near_sem)
    near_copy.start()
    sum_ref[...] = jnp.zeros_like(sum_ref)
    lanes = pl.ds(pl.multiple_of(lax.axis_index("smp") * 128, 128), 128)

    def copies(i):
        rows = pl.ds(pl.multiple_of(i * WIDE, WIDE), WIDE)
        return (
            pltpu.make_async_copy(stage_ref.at[rows], logits_out.at[rows], sem_ref.at[i]),
            pltpu.make_async_copy(own_ref.at[rows], own_out.at[rows], own_sem.at[i]),
        )

    @pl.loop(0, ROWS // WIDE)
    def _(i):
        copy_in(i).wait()
        rows = pl.ds(pl.multiple_of(i * WIDE, WIDE), WIDE)
        logits = jnp.dot(weight_ref[rows, :], unit_ref[...], preferred_element_type=f32) * (1.0 / STUDENT_TEMP)
        stage_ref[rows, :] = logits
        own_ref[rows, :] = stage_ref[rows, lanes]
        for copy in copies(i):
            copy.start()
        sum_ref[...] += folded(jnp.exp(logits))

    total_ref[...] = as_blocks(sum_ref[...])
    for i in range(ROWS // WIDE):
        for copy in copies(i):
            copy.wait()
    near_copy.wait()


def received(got_ref):
    return jnp.sum(got_ref[...].astype(f32), axis=0)


def second_kernel(
    got_ref, far_ref, near_ref, total_ref, kernel_ref, sent_ref, kept_ref, col_ref, mass_ref, sem_ref
):
    def copy_in(i):
        rows = pl.ds(pl.multiple_of(i * TILE, TILE), TILE)
        return pltpu.make_async_copy(far_ref.at[rows], kernel_ref.at[rows], sem_ref.at[i])

    for i in range(FAR // TILE):
        copy_in(i).start()
    col_ref[...] = as_row(1.0 / (B * received(got_ref)))
    mass_ref[...] = jnp.zeros_like(mass_ref)

    def add(kernel):
        row_scale = 1.0 / (K * jnp.sum(kernel * col_ref[...], axis=1, keepdims=True))
        mass_ref[...] += folded(kernel * row_scale)

    @pl.loop(0, (ROWS - FAR) // TILE)
    def _(i):
        start = pl.multiple_of(i * TILE, TILE)
        kernel = near_ref[pl.ds(start, TILE), :]
        kernel_ref[pl.ds(FAR + start, TILE), :] = kernel
        add(kernel)

    @pl.loop(0, FAR // TILE)
    def _(i):
        copy_in(i).wait()
        add(kernel_ref[pl.ds(pl.multiple_of(i * TILE, TILE), TILE), :])

    mass = as_blocks(mass_ref[...]).astype(bf16).astype(f32)
    kept_ref[...] = mass
    total = total_ref[...]
    step = jnp.exp2(jnp.floor(jnp.log2(total)) - 7.0)
    place = lax.axis_index("proto").astype(f32)
    spread = total + step * ((place + 0.5) * (1.0 / 64) - 0.5)
    packed = jnp.concatenate([mass, spread], axis=0).astype(bf16)
    sent_ref[...] = jnp.broadcast_to(packed[None], sent_ref.shape)


def split_rows(value):
    high = value.astype(bf16).astype(f32)
    return [high, value - high]


def third_kernel(
    got_ref, kernel_ref, kept_ref, features_ref, logits_far, weight_far,
    sent_ref, total_ref, before_ref, col_ref, mass_ref, scaled_ref, pair_ref, logits_ref, weight_ref, sem_ref,
):
    copies = [pltpu.make_async_copy(logits_far, logits_ref, sem_ref.at[0])]
    for i in range(ROWS // WIDE):
        rows = pl.ds(i * WIDE, WIDE)
        copies.append(pltpu.make_async_copy(weight_far.at[rows], weight_ref.at[rows], sem_ref.at[1 + i]))
    for copy in copies:
        copy.start()
    me = lax.axis_index("smp")
    got = received(got_ref)
    before_ref[...] = got[:8, :]
    total_ref[...] = got[8:, :]
    col_ref[...] = as_row(1.0 / (B * got[:8, :]))
    mass_ref[...] = jnp.zeros_like(mass_ref)
    lanes = pl.ds(pl.multiple_of(me * 128, 128), 128)

    @pl.loop(0, ROWS // TILE)
    def _(i):
        rows = pl.ds(pl.multiple_of(i * TILE, TILE), TILE)
        kernel = kernel_ref[rows, :]
        row_scale = 1.0 / (K * jnp.sum(kernel * col_ref[...], axis=1, keepdims=True))
        scaled_ref[rows, :] = kernel_ref[rows, lanes] * row_scale
        mass_ref[...] += folded(kernel * row_scale)

    change = as_blocks(mass_ref[...]) - kept_ref[...]
    copies[0].wait()
    logits = logits_ref[...]
    own_col = 1.0 / before_ref[pl.ds(me, 1), :]
    own_total = 1.0 / total_ref[pl.ds(me, 1), :]
    targets = scaled_ref[...] * own_col
    weighted = jnp.sum(folded(targets * logits), axis=0, keepdims=True)
    pair_ref[:, :128] = ((jnp.exp(logits) * own_total - targets) * SHARE).astype(bf16)
    pair_ref[:, 128:] = (targets * SHARE).astype(bf16)
    for copy in copies[1:]:
        copy.wait()
    parts = lax.dot_general(
        pair_ref[...], weight_ref[...], (((0,), (0,)), ((), ())), preferred_element_type=f32
    )
    grad_part, target_part = parts[:128, :].T, parts[128:, :].T
    features = features_ref[...]
    inner_grad = jnp.sum(folded(features * grad_part), axis=0, keepdims=True)
    inner_target = jnp.sum(folded(features * target_part), axis=0, keepdims=True)
    extra = jnp.concatenate(
        split_rows(inner_grad) + split_rows(inner_target) + split_rows(weighted) + [jnp.zeros((2, 128), f32)],
        axis=0,
    )

    def everywhere(rows):
        return jnp.broadcast_to(rows[None], (64, 8, 128))

    sent_ref[...] = jnp.concatenate(
        [everywhere(change), grad_part.reshape(64, 8, 128), target_part.reshape(64, 8, 128), everywhere(extra)],
        axis=1,
    ).astype(bf16)


def weight_kernel(
    kernel_ref, logits_ref, total_ref, before_ref, unit_ref, out_ref, near_ref, far_ref, slice_ref, rows_ref
):
    @pl.when(pl.program_id(0) == 0)
    def _():
        rows_ref[0:1, :] = as_row(1.0 / (B * before_ref[...]))
        rows_ref[1:2, :] = as_row(1.0 / before_ref[...])
        rows_ref[2:3, :] = as_row(1.0 / total_ref[...])

    kernel = kernel_ref[...]
    row_scale = 1.0 / (K * jnp.sum(kernel * rows_ref[0:1, :], axis=1, keepdims=True))
    targets = kernel * row_scale * rows_ref[1:2, :]
    probs = jnp.exp(logits_ref[...]) * rows_ref[2:3, :]
    grad = ((probs - targets) * SHARE).astype(bf16)
    shared = (targets * SHARE).astype(bf16)

    @pl.when(pl.program_id(0) < HALF)
    def _():
        near_ref[...] = shared

    @pl.when(pl.program_id(0) >= HALF)
    def _():
        far_ref[...] = shared

    units = unit_ref[pl.ds(pl.multiple_of(lax.axis_index("smp") * 64, 64), 64), :]
    slice_ref[...] = units
    out_ref[...] = lax.dot_general(units, grad, (((1,), (1,)), ((), ())), preferred_element_type=f32)


def final_kernel(
    got_ref, features_ref, scale_ref, total_ref, before_ref, unit_ref, near_ref, held_ref, targets_far,
    features_out, loss_out, weight_out, change_ref, targets_ref, sem_ref,
):
    def copy_in(i):
        rows = pl.ds(i * TILE, TILE)
        return pltpu.make_async_copy(targets_far.at[rows], targets_ref.at[rows], sem_ref.at[i])

    for i in range(ROWS // TILE - HALF):
        copy_in(i).start()
    me = lax.axis_index("smp")
    got = received(got_ref)
    before = before_ref[...]
    change_ref[...] = got[:8] / (before + got[:8])
    own = change_ref[pl.ds(me, 1), :]
    unit_grad = got[8:16] + own * got[16:24]
    inner = (got[24:25] + got[25:26]) + own * (got[26:27] + got[27:28])
    scale = scale_ref[pl.ds(me, 1), :]
    features_out[...] = scale * unit_grad - (scale * scale * scale * inner) * features_ref[...].astype(f32)
    loss_out[...] = jnp.log(total_ref[pl.ds(me, 1), :]) - (1.0 - own) * (got[28:29] + got[29:30])
    moved = (unit_ref[...].astype(f32) * as_row(change_ref[...])).astype(bf16)

    def correct(start, targets):
        rows = pl.ds(start, targets.shape[0])
        weight_out[:, rows] = near_ref[:, rows] + lax.dot_general(
            moved, targets, (((1,), (1,)), ((), ())), preferred_element_type=f32
        )

    for i in range(HALF):
        correct(i * TILE, held_ref[pl.ds(i * TILE, TILE), :])
    for i in range(ROWS // TILE - HALF):
        copy_in(i).wait()
        correct((HALF + i) * TILE, targets_ref[pl.ds(i * TILE, TILE), :])


def shape(dims, dtype=f32):
    return jax.ShapeDtypeStruct(dims, dtype)


def on_device(teacher_features, student_features, teacher_weight, student_weight):
    raw = jnp.concatenate([teacher_features.T, student_features.T], axis=0)
    first = gathered(raw, ("yh", "yl", "z"))
    second = gathered(first, ("x",))
    second, teacher_weight = lax.optimization_barrier((second, teacher_weight))
    other = lax.ppermute(second, "proto", [(i, i ^ 1) for i in range(64)])

    stage = pltpu.VMEM((ROWS, B), f32)
    wide_sems, near_sems = pltpu.SemaphoreType.DMA((ROWS // WIDE,)), pltpu.SemaphoreType.DMA((ROWS // TILE,))
    row, rows8 = pltpu.VMEM((1, B), f32), pltpu.VMEM((8, B), f32)
    rows8_small = pltpu.VMEM((8, 128), f32)
    matmul = dict(flops=2 * ROWS * B * D, moved=12 * 2**20, exps=ROWS * B)
    (weight_near,) = call(
        fetch_kernel, [pltpu.VMEM((ROWS, D), bf16)], [ANY], None, [wide_sems], moved=4 * 2**20
    )(far(teacher_weight))
    kernel, kernel_end, student_unit, sent_1, student_scale, features_own = call(
        first_kernel,
        [pltpu.HBM((ROWS, B), f32), pltpu.VMEM((ROWS - FAR, B), f32), shape((D, B), bf16),
         pltpu.HBM((64, 8, 128), bf16), shape((8, 128)),
         shape((D, 128))],
        [VMEM, VMEM, VMEM],
        [ANY, VMEM, VMEM, ANY, VMEM, VMEM],
        [pltpu.VMEM((D, B), bf16), pltpu.VMEM((FAR, B), f32), pltpu.VMEM((64, 8, 128), bf16), rows8, wide_sems,
         pltpu.SemaphoreType.DMA],
        **matmul,
    )(second, other, weight_near)
    got_1 = sent_to_protos(sent_1)
    logits, logits_own, local_total, kernel = call(
        student_kernel,
        [pltpu.HBM((ROWS, B), f32), pltpu.HBM((ROWS, 128), f32), shape((8, 128)), pltpu.HBM((ROWS, B), f32)],
        [VMEM, ANY, VMEM, ANY],
        [ANY, ANY, VMEM, ANY],
        [pltpu.VMEM((ROWS, D), bf16), stage, pltpu.VMEM((ROWS, 128), f32), rows8, wide_sems, wide_sems, wide_sems,
         pltpu.SemaphoreType.DMA],
        {3: 3},
        **matmul,
    )(student_unit, far(student_weight), kernel_end, far(kernel))
    kernel_near, sent_2, kept = call(
        second_kernel,
        [pltpu.VMEM((ROWS, B), f32), shape((64, 16, 128), bf16), shape((8, 128))],
        [VMEM, ANY, VMEM, VMEM],
        None,
        [row, rows8, near_sems],
        flops=4 * ROWS * B,
        moved=8 * 2**20,
    )(got_1, far(kernel), kernel_end, local_total)
    got_2 = sent_to_protos(sent_2)
    sent_3, total, before = call(
        third_kernel,
        [shape((64, 32, 128), bf16), shape((8, 128)), shape((8, 128))],
        [VMEM] * 4 + [ANY] * 2,
        None,
        [row, rows8, pltpu.VMEM((ROWS, 128), f32), pltpu.VMEM((ROWS, 256), bf16), pltpu.VMEM((ROWS, 128), f32),
         pltpu.VMEM((ROWS, D), bf16), pltpu.SemaphoreType.DMA((1 + ROWS // WIDE,))],
        flops=2 * ROWS * 256 * D,
        moved=12 * 2**20,
        exps=ROWS * 128,
    )(got_2, kernel_near, kept, features_own, far(logits_own), far(student_weight))
    got_3 = sent_to_protos(sent_3)
    partial, targets_near, targets_far, unit_slice = streamed(
        weight_kernel,
        [shape((64, ROWS)), pltpu.VMEM((HALF * TILE, B), bf16), pltpu.HBM((ROWS - HALF * TILE, B), bf16),
         shape((64, B), bf16)],
        [stripe(B), stripe(B), whole(8, 128), whole(8, 128), whole(D, B)],
        [pl.BlockSpec((64, TILE), lambda i: (0, i)),
         pl.BlockSpec((TILE, B), lambda i: (jnp.minimum(i, HALF - 1), 0)),
         pl.BlockSpec((TILE, B), lambda i: (jnp.maximum(i - HALF, 0), 0)), whole(64, B)],
        [rows8],
        flops=2 * ROWS * B * 64,
        moved=21 * 2**20,
        exps=ROWS * B,
    )(far(kernel), far(logits), total, before, far(student_unit))
    grad_features, loss, grad_weight = call(
        final_kernel,
        [shape((8, 128)), shape((1, 128)), shape((64, ROWS))],
        [VMEM] * 8 + [ANY],
        None,
        [rows8_small, pltpu.VMEM((ROWS - HALF * TILE, B), bf16), near_sems],
        flops=2 * ROWS * B * 64,
        moved=5 * 2**20,
    )(
        got_3, student_features.T, student_scale, total, before, unit_slice, partial, targets_near,
        far(targets_far),
    )
    return loss.reshape(128), grad_features.T, grad_weight.T


def solution(mesh):
    placed = (P("smp", "proto"), P("smp", "proto"), P("proto", None), P("proto", None))
    return jax.shard_map(
        on_device,
        mesh=mesh,
        in_specs=placed,
        out_specs=(P("smp"), P("smp", "proto"), P("proto", "smp")),
        check_vma=False,
    )
```

```python
import jax
import jax.numpy as jnp
import numpy as np
from jax import lax
from jax.experimental import pallas as pl
from jax.experimental.pallas import tpu as pltpu
from jax.sharding import PartitionSpec as P

ITERS = 3
TEACHER_TEMP = 0.07
STUDENT_TEMP = 0.1
BOTH = ("smp", "proto")
PARTS = {"x": 4, "yh": 2, "yl": 4, "z": 8, "c": 2}
B, K, D = 1024, 131072, 512
ROWS = 2048
SHARE = 1.0 / (1024 * 0.1)
TILE = 256
WIDE = 512
HALF = 4
FAR = 1536
BLOCKS = 8
f32, bf16 = jnp.float32, jnp.bfloat16
VMEM = pl.BlockSpec(memory_space=pltpu.VMEM)
ANY = pl.BlockSpec(memory_space=pl.ANY)


def groups(names):
    order = list(PARTS)
    index = np.arange(512).reshape(tuple(PARTS.values()))
    inner = [order.index(n) for n in names]
    outer = [i for i in range(len(order)) if i not in inner]
    size = int(np.prod([PARTS[n] for n in names]))
    return index.transpose(outer + inner).reshape(-1, size).tolist()


def gathered(x, names):
    group = groups(names)
    copies = jnp.broadcast_to(x[None], (len(group[0]), *x.shape))
    return lax.all_to_all(copies, BOTH, 0, 0, tiled=True, axis_index_groups=group)


def sent_to_protos(x):
    return lax.all_to_all(x, "proto", 0, 0, tiled=True)


def far(x):
    return pltpu.with_memory_space_constraint(x, pltpu.HBM)


def limits():
    return pltpu.CompilerParams(vmem_limit_bytes=24 * 2**20)


def cost(flops=0, moved=0, exps=0):
    return pl.CostEstimate(flops=flops, bytes_accessed=moved, transcendentals=exps)


def call(body, outs, ins, out_specs=None, scratch=(), aliases=None, **work):
    return pl.pallas_call(
        body,
        out_shape=outs,
        in_specs=ins,
        out_specs=out_specs or [VMEM] * len(outs),
        scratch_shapes=scratch,
        input_output_aliases=aliases or {},
        compiler_params=limits(),
        cost_estimate=cost(**work),
    )


def streamed(body, outs, ins, out_specs, scratch=(), **work):
    return pl.pallas_call(
        body,
        out_shape=outs,
        grid=(ROWS // TILE,),
        in_specs=ins,
        out_specs=out_specs,
        scratch_shapes=scratch,
        compiler_params=limits(),
        cost_estimate=cost(**work),
    )


def whole(*dims):
    return pl.BlockSpec(dims, lambda i: (0,) * len(dims))


def stripe(width):
    return pl.BlockSpec((TILE, width), lambda i: (i, 0))


def features_of(cores, x, yh, which):
    base = yh * 32 if isinstance(yh, int) else pl.multiple_of(yh * 32, 32)
    halves = [ref[x, pl.ds(base, 32)].astype(f32)[:, which * 8 : which * 8 + 8] for ref in cores]
    return jnp.stack(halves, axis=1).reshape(D, 128)


def unit_columns(values):
    scale = lax.rsqrt(jnp.sum(folded(values * values), axis=0, keepdims=True) + 1e-06)
    return (values * scale).astype(bf16), scale


def folded(total):
    return jnp.sum(total.reshape(-1, 8, total.shape[1]), axis=0)


def as_blocks(wide):
    row = jnp.sum(wide, axis=0, keepdims=True)
    return jnp.concatenate([row[:, s * 128 : (s + 1) * 128] for s in range(BLOCKS)], axis=0)


def as_row(blocks):
    return jnp.concatenate([blocks[s : s + 1, :] for s in range(BLOCKS)], axis=1)


def fetch_kernel(far_ref, near_ref, sem_ref):
    copies = []
    for i in range(ROWS // WIDE):
        rows = pl.ds(i * WIDE, WIDE)
        copies.append(pltpu.make_async_copy(far_ref.at[rows], near_ref.at[rows], sem_ref.at[i]))
    for copy in copies:
        copy.start()
    for copy in copies:
        copy.wait()


def first_kernel(
    own_ref, other_ref, weight_ref, kernel_out, near_ref, unit_ref, sent_out, scale_ref, features_ref,
    teacher_ref, stage_ref, sent_ref, mass_ref, sem_ref, sent_sem,
):
    me, core = lax.axis_index("smp"), lax.rem(lax.axis_index("proto"), 2)

    def by_core(body):
        @pl.when(core == 0)
        def _():
            body((own_ref, other_ref))

        @pl.when(core == 1)
        def _():
            body((other_ref, own_ref))

    def teacher_units(cores):
        for s in range(BLOCKS):
            values = features_of(cores, s // 2, s % 2, 0)
            teacher_ref[:, s * 128 : (s + 1) * 128] = unit_columns(values)[0]

    def student_units(cores):
        for s in range(BLOCKS):
            values = features_of(cores, s // 2, s % 2, 1)
            unit, scale = unit_columns(values)
            unit_ref[:, s * 128 : (s + 1) * 128] = unit
            scale_ref[s : s + 1, :] = scale
        features_ref[...] = features_of(cores, me // 2, lax.rem(me, 2), 1)

    def copy_out(i):
        rows = pl.ds(pl.multiple_of(i * WIDE, WIDE), WIDE)
        return pltpu.make_async_copy(stage_ref.at[rows], kernel_out.at[rows], sem_ref.at[i])

    by_core(teacher_units)
    mass_ref[...] = jnp.zeros_like(mass_ref)

    def tile(rows, kept_ref, kept_rows):
        kernel = jnp.exp(
            jnp.dot(weight_ref[rows, :], teacher_ref[...], preferred_element_type=f32) * (1.0 / TEACHER_TEMP)
        )
        kept_ref[kept_rows, :] = kernel
        row_scale = 1.0 / (K * jnp.sum(kernel, axis=1, keepdims=True))
        mass_ref[...] += folded(kernel * row_scale)

    @pl.loop(0, FAR // WIDE)
    def _(i):
        rows = pl.ds(pl.multiple_of(i * WIDE, WIDE), WIDE)
        tile(rows, stage_ref, rows)
        copy_out(i).start()

    tile(pl.ds(FAR, ROWS - FAR), near_ref, pl.ds(0, ROWS - FAR))
    sent_ref[...] = jnp.broadcast_to(as_blocks(mass_ref[...]).astype(bf16)[None], sent_ref.shape)
    sent_copy = pltpu.make_async_copy(sent_ref, sent_out, sent_sem)
    sent_copy.start()
    by_core(student_units)
    sent_copy.wait()
    for i in range(FAR // WIDE):
        copy_out(i).wait()


def student_kernel(
    unit_ref, weight_far, near_ref, kernel_ref, own_out, total_ref, kernel_out,
    weight_ref, stage_ref, own_ref, sum_ref, own_sem, weight_sem, near_sem,
):
    def copy_in(i):
        rows = pl.ds(pl.multiple_of(i * WIDE, WIDE), WIDE)
        return pltpu.make_async_copy(weight_far.at[rows], weight_ref.at[rows], weight_sem.at[i])

    for i in range(ROWS // WIDE):
        copy_in(i).start()
    near_copy = pltpu.make_async_copy(near_ref, kernel_out.at[pl.ds(FAR, ROWS - FAR)], near_sem)
    near_copy.start()
    sum_ref[...] = jnp.zeros_like(sum_ref)
    lanes = pl.ds(pl.multiple_of(lax.axis_index("smp") * 128, 128), 128)

    def copy_out(i):
        rows = pl.ds(pl.multiple_of(i * WIDE, WIDE), WIDE)
        return pltpu.make_async_copy(own_ref.at[rows], own_out.at[rows], own_sem.at[i])

    @pl.loop(0, ROWS // WIDE)
    def _(i):
        copy_in(i).wait()
        rows = pl.ds(pl.multiple_of(i * WIDE, WIDE), WIDE)
        logits = jnp.dot(weight_ref[rows, :], unit_ref[...], preferred_element_type=f32) * (1.0 / STUDENT_TEMP)
        stage_ref[...] = logits
        own_ref[rows, :] = stage_ref[:, lanes]
        copy_out(i).start()
        sum_ref[...] += folded(jnp.exp(logits))

    total_ref[...] = as_blocks(sum_ref[...])
    for i in range(ROWS // WIDE):
        copy_out(i).wait()
    near_copy.wait()


def received(got_ref):
    return jnp.sum(got_ref[...].astype(f32), axis=0)


def second_kernel(
    got_ref, far_ref, near_ref, total_ref, kernel_ref, sent_ref, kept_ref, col_ref, mass_ref, sem_ref
):
    def copy_in(i):
        rows = pl.ds(pl.multiple_of(i * TILE, TILE), TILE)
        return pltpu.make_async_copy(far_ref.at[rows], kernel_ref.at[rows], sem_ref.at[i])

    for i in range(FAR // TILE):
        copy_in(i).start()
    col_ref[...] = as_row(1.0 / (B * received(got_ref)))
    mass_ref[...] = jnp.zeros_like(mass_ref)

    def add(kernel):
        row_scale = 1.0 / (K * jnp.sum(kernel * col_ref[...], axis=1, keepdims=True))
        mass_ref[...] += folded(kernel * row_scale)

    @pl.loop(0, (ROWS - FAR) // TILE)
    def _(i):
        start = pl.multiple_of(i * TILE, TILE)
        kernel = near_ref[pl.ds(start, TILE), :]
        kernel_ref[pl.ds(FAR + start, TILE), :] = kernel
        add(kernel)

    @pl.loop(0, FAR // TILE)
    def _(i):
        copy_in(i).wait()
        add(kernel_ref[pl.ds(pl.multiple_of(i * TILE, TILE), TILE), :])

    mass = as_blocks(mass_ref[...]).astype(bf16).astype(f32)
    kept_ref[...] = mass
    total = total_ref[...]
    step = jnp.exp2(jnp.floor(jnp.log2(total)) - 7.0)
    place = lax.axis_index("proto").astype(f32)
    spread = total + step * ((place + 0.5) * (1.0 / 64) - 0.5)
    packed = jnp.concatenate([mass, spread], axis=0).astype(bf16)
    sent_ref[...] = jnp.broadcast_to(packed[None], sent_ref.shape)


def split_rows(value):
    high = value.astype(bf16).astype(f32)
    return [high, value - high]


def third_kernel(
    got_ref, kernel_ref, kept_ref, features_ref, logits_far, weight_far,
    sent_ref, total_ref, before_ref, col_ref, mass_ref, scaled_ref, pair_ref, logits_ref, weight_ref, sem_ref,
):
    copies = [pltpu.make_async_copy(logits_far, logits_ref, sem_ref.at[0])]
    for i in range(ROWS // WIDE):
        rows = pl.ds(i * WIDE, WIDE)
        copies.append(pltpu.make_async_copy(weight_far.at[rows], weight_ref.at[rows], sem_ref.at[1 + i]))
    for copy in copies:
        copy.start()
    me = lax.axis_index("smp")
    got = received(got_ref)
    before_ref[...] = got[:8, :]
    total_ref[...] = got[8:, :]
    col_ref[...] = as_row(1.0 / (B * got[:8, :]))
    mass_ref[...] = jnp.zeros_like(mass_ref)
    lanes = pl.ds(pl.multiple_of(me * 128, 128), 128)

    @pl.loop(0, ROWS // TILE)
    def _(i):
        rows = pl.ds(pl.multiple_of(i * TILE, TILE), TILE)
        kernel = kernel_ref[rows, :]
        row_scale = 1.0 / (K * jnp.sum(kernel * col_ref[...], axis=1, keepdims=True))
        scaled_ref[rows, :] = kernel_ref[rows, lanes] * row_scale
        mass_ref[...] += folded(kernel * row_scale)

    change = as_blocks(mass_ref[...]) - kept_ref[...]
    copies[0].wait()
    logits = logits_ref[...]
    own_col = 1.0 / before_ref[pl.ds(me, 1), :]
    own_total = 1.0 / total_ref[pl.ds(me, 1), :]
    targets = scaled_ref[...] * own_col
    weighted = jnp.sum(folded(targets * logits), axis=0, keepdims=True)
    pair_ref[:, :128] = ((jnp.exp(logits) * own_total - targets) * SHARE).astype(bf16)
    pair_ref[:, 128:] = (targets * SHARE).astype(bf16)
    for copy in copies[1:]:
        copy.wait()
    parts = lax.dot_general(
        pair_ref[...], weight_ref[...], (((0,), (0,)), ((), ())), preferred_element_type=f32
    )
    grad_part, target_part = parts[:128, :].T, parts[128:, :].T
    features = features_ref[...]
    inner_grad = jnp.sum(folded(features * grad_part), axis=0, keepdims=True)
    inner_target = jnp.sum(folded(features * target_part), axis=0, keepdims=True)
    extra = jnp.concatenate(
        split_rows(inner_grad) + split_rows(inner_target) + split_rows(weighted) + [jnp.zeros((2, 128), f32)],
        axis=0,
    )

    def everywhere(rows):
        return jnp.broadcast_to(rows[None], (64, 8, 128))

    sent_ref[...] = jnp.concatenate(
        [everywhere(change), grad_part.reshape(64, 8, 128), target_part.reshape(64, 8, 128), everywhere(extra)],
        axis=1,
    ).astype(bf16)


def weight_kernel(
    kernel_ref, weight_ref, total_ref, before_ref, unit_ref, out_ref, near_ref, far_ref, slice_ref, rows_ref
):
    @pl.when(pl.program_id(0) == 0)
    def _():
        rows_ref[0:1, :] = as_row(1.0 / (B * before_ref[...]))
        rows_ref[1:2, :] = as_row(1.0 / before_ref[...])
        rows_ref[2:3, :] = as_row(1.0 / total_ref[...])

    kernel = kernel_ref[...]
    row_scale = 1.0 / (K * jnp.sum(kernel * rows_ref[0:1, :], axis=1, keepdims=True))
    targets = kernel * row_scale * rows_ref[1:2, :]
    logits = jnp.dot(weight_ref[...], unit_ref[...], preferred_element_type=f32) * (1.0 / STUDENT_TEMP)
    probs = jnp.exp(logits) * rows_ref[2:3, :]
    grad = ((probs - targets) * SHARE).astype(bf16)
    shared = (targets * SHARE).astype(bf16)

    @pl.when(pl.program_id(0) < HALF)
    def _():
        near_ref[...] = shared

    @pl.when(pl.program_id(0) >= HALF)
    def _():
        far_ref[...] = shared

    units = unit_ref[pl.ds(pl.multiple_of(lax.axis_index("smp") * 64, 64), 64), :]
    slice_ref[...] = units
    out_ref[...] = lax.dot_general(units, grad, (((1,), (1,)), ((), ())), preferred_element_type=f32)


def final_kernel(
    got_ref, features_ref, scale_ref, total_ref, before_ref, unit_ref, near_ref, held_ref, targets_far,
    features_out, loss_out, weight_out, change_ref, targets_ref, sem_ref,
):
    def copy_in(i):
        rows = pl.ds(i * TILE, TILE)
        return pltpu.make_async_copy(targets_far.at[rows], targets_ref.at[rows], sem_ref.at[i])

    for i in range(ROWS // TILE - HALF):
        copy_in(i).start()
    me = lax.axis_index("smp")
    got = received(got_ref)
    before = before_ref[...]
    change_ref[...] = got[:8] / (before + got[:8])
    own = change_ref[pl.ds(me, 1), :]
    unit_grad = got[8:16] + own * got[16:24]
    inner = (got[24:25] + got[25:26]) + own * (got[26:27] + got[27:28])
    scale = scale_ref[pl.ds(me, 1), :]
    features_out[...] = scale * unit_grad - (scale * scale * scale * inner) * features_ref[...].astype(f32)
    loss_out[...] = jnp.log(total_ref[pl.ds(me, 1), :]) - (1.0 - own) * (got[28:29] + got[29:30])
    moved = (unit_ref[...].astype(f32) * as_row(change_ref[...])).astype(bf16)

    def correct(start, targets):
        rows = pl.ds(start, targets.shape[0])
        weight_out[:, rows] = near_ref[:, rows] + lax.dot_general(
            moved, targets, (((1,), (1,)), ((), ())), preferred_element_type=f32
        )

    for i in range(HALF):
        correct(i * TILE, held_ref[pl.ds(i * TILE, TILE), :])
    for i in range(ROWS // TILE - HALF):
        copy_in(i).wait()
        correct((HALF + i) * TILE, targets_ref[pl.ds(i * TILE, TILE), :])


def shape(dims, dtype=f32):
    return jax.ShapeDtypeStruct(dims, dtype)


def on_device(teacher_features, student_features, teacher_weight, student_weight):
    raw = jnp.concatenate([teacher_features.T, student_features.T], axis=0)
    first = gathered(raw, ("yh", "yl", "z"))
    second = gathered(first, ("x",))
    second, teacher_weight = lax.optimization_barrier((second, teacher_weight))
    other = lax.ppermute(second, "proto", [(i, i ^ 1) for i in range(64)])

    wide_sems, near_sems = pltpu.SemaphoreType.DMA((ROWS // WIDE,)), pltpu.SemaphoreType.DMA((ROWS // TILE,))
    row, rows8 = pltpu.VMEM((1, B), f32), pltpu.VMEM((8, B), f32)
    rows8_small = pltpu.VMEM((8, 128), f32)
    matmul = dict(flops=2 * ROWS * B * D, moved=12 * 2**20, exps=ROWS * B)
    (weight_near,) = call(
        fetch_kernel, [pltpu.VMEM((ROWS, D), bf16)], [ANY], None, [wide_sems], moved=4 * 2**20
    )(far(teacher_weight))
    kernel, kernel_end, student_unit, sent_1, student_scale, features_own = call(
        first_kernel,
        [pltpu.HBM((ROWS, B), f32), pltpu.VMEM((ROWS - FAR, B), f32), shape((D, B), bf16),
         pltpu.HBM((64, 8, 128), bf16), shape((8, 128)),
         shape((D, 128))],
        [VMEM, VMEM, VMEM],
        [ANY, VMEM, VMEM, ANY, VMEM, VMEM],
        [pltpu.VMEM((D, B), bf16), pltpu.VMEM((FAR, B), f32), pltpu.VMEM((64, 8, 128), bf16), rows8, wide_sems,
         pltpu.SemaphoreType.DMA],
        **matmul,
    )(second, other, weight_near)
    got_1 = sent_to_protos(sent_1)
    logits_own, local_total, kernel = call(
        student_kernel,
        [pltpu.HBM((ROWS, 128), f32), shape((8, 128)), pltpu.HBM((ROWS, B), f32)],
        [VMEM, ANY, VMEM, ANY],
        [ANY, VMEM, ANY],
        [pltpu.VMEM((ROWS, D), bf16), pltpu.VMEM((WIDE, B), f32), pltpu.VMEM((ROWS, 128), f32), rows8, wide_sems,
         wide_sems, pltpu.SemaphoreType.DMA],
        {3: 2},
        **matmul,
    )(student_unit, far(student_weight), kernel_end, far(kernel))
    kernel_near, sent_2, kept = call(
        second_kernel,
        [pltpu.VMEM((ROWS, B), f32), shape((64, 16, 128), bf16), shape((8, 128))],
        [VMEM, ANY, VMEM, VMEM],
        None,
        [row, rows8, near_sems],
        flops=4 * ROWS * B,
        moved=8 * 2**20,
    )(got_1, far(kernel), kernel_end, local_total)
    got_2 = sent_to_protos(sent_2)
    sent_3, total, before = call(
        third_kernel,
        [shape((64, 32, 128), bf16), shape((8, 128)), shape((8, 128))],
        [VMEM] * 4 + [ANY] * 2,
        None,
        [row, rows8, pltpu.VMEM((ROWS, 128), f32), pltpu.VMEM((ROWS, 256), bf16), pltpu.VMEM((ROWS, 128), f32),
         pltpu.VMEM((ROWS, D), bf16), pltpu.SemaphoreType.DMA((1 + ROWS // WIDE,))],
        flops=2 * ROWS * 256 * D,
        moved=12 * 2**20,
        exps=ROWS * 128,
    )(got_2, kernel_near, kept, features_own, far(logits_own), far(student_weight))
    got_3 = sent_to_protos(sent_3)
    partial, targets_near, targets_far, unit_slice = streamed(
        weight_kernel,
        [shape((64, ROWS)), pltpu.VMEM((HALF * TILE, B), bf16), pltpu.HBM((ROWS - HALF * TILE, B), bf16),
         shape((64, B), bf16)],
        [stripe(B), stripe(D), whole(8, 128), whole(8, 128), whole(D, B)],
        [pl.BlockSpec((64, TILE), lambda i: (0, i)),
         pl.BlockSpec((TILE, B), lambda i: (jnp.minimum(i, HALF - 1), 0)),
         pl.BlockSpec((TILE, B), lambda i: (jnp.maximum(i - HALF, 0), 0)), whole(64, B)],
        [rows8],
        flops=2 * ROWS * B * (64 + D),
        moved=15 * 2**20,
        exps=ROWS * B,
    )(far(kernel), far(student_weight), total, before, far(student_unit))
    grad_features, loss, grad_weight = call(
        final_kernel,
        [shape((8, 128)), shape((1, 128)), shape((64, ROWS))],
        [VMEM] * 8 + [ANY],
        None,
        [rows8_small, pltpu.VMEM((ROWS - HALF * TILE, B), bf16), near_sems],
        flops=2 * ROWS * B * 64,
        moved=5 * 2**20,
    )(
        got_3, student_features.T, student_scale, total, before, unit_slice, partial, targets_near,
        far(targets_far),
    )
    return loss.reshape(128), grad_features.T, grad_weight.T


def solution(mesh):
    placed = (P("smp", "proto"), P("smp", "proto"), P("proto", None), P("proto", None))
    return jax.shard_map(
        on_device,
        mesh=mesh,
        in_specs=placed,
        out_specs=(P("smp"), P("smp", "proto"), P("proto", "smp")),
        check_vma=False,
    )
```

```python
import jax
import jax.numpy as jnp
import numpy as np
from jax import lax
from jax.experimental import pallas as pl
from jax.experimental.pallas import tpu as pltpu
from jax.sharding import PartitionSpec as P

ITERS = 3
TEACHER_TEMP = 0.07
STUDENT_TEMP = 0.1
BOTH = ("smp", "proto")
PARTS = {"x": 4, "yh": 2, "yl": 4, "z": 8, "c": 2}
B, K, D = 1024, 131072, 512
ROWS = 2048
SHARE = 1.0 / (1024 * 0.1)
TILE = 256
WIDE = 512
HALF = 4
FAR = 1536
BLOCKS = 8
f32, bf16 = jnp.float32, jnp.bfloat16
VMEM = pl.BlockSpec(memory_space=pltpu.VMEM)
ANY = pl.BlockSpec(memory_space=pl.ANY)


def groups(names):
    order = list(PARTS)
    index = np.arange(512).reshape(tuple(PARTS.values()))
    inner = [order.index(n) for n in names]
    outer = [i for i in range(len(order)) if i not in inner]
    size = int(np.prod([PARTS[n] for n in names]))
    return index.transpose(outer + inner).reshape(-1, size).tolist()


def gathered(x, names):
    group = groups(names)
    copies = jnp.broadcast_to(x[None], (len(group[0]), *x.shape))
    return lax.all_to_all(copies, BOTH, 0, 0, tiled=True, axis_index_groups=group)


def sent_to_protos(x):
    return lax.all_to_all(x, "proto", 0, 0, tiled=True)


def far(x):
    return pltpu.with_memory_space_constraint(x, pltpu.HBM)


def limits():
    return pltpu.CompilerParams(vmem_limit_bytes=24 * 2**20)


def cost(flops=0, moved=0, exps=0):
    return pl.CostEstimate(flops=flops, bytes_accessed=moved, transcendentals=exps)


def call(body, outs, ins, out_specs=None, scratch=(), aliases=None, **work):
    return pl.pallas_call(
        body,
        out_shape=outs,
        in_specs=ins,
        out_specs=out_specs or [VMEM] * len(outs),
        scratch_shapes=scratch,
        input_output_aliases=aliases or {},
        compiler_params=limits(),
        cost_estimate=cost(**work),
    )


def streamed(body, outs, ins, out_specs, scratch=(), **work):
    return pl.pallas_call(
        body,
        out_shape=outs,
        grid=(ROWS // TILE,),
        in_specs=ins,
        out_specs=out_specs,
        scratch_shapes=scratch,
        compiler_params=limits(),
        cost_estimate=cost(**work),
    )


def whole(*dims):
    return pl.BlockSpec(dims, lambda i: (0,) * len(dims))


def stripe(width):
    return pl.BlockSpec((TILE, width), lambda i: (i, 0))


def features_of(cores, x, yh, which):
    base = yh * 32 if isinstance(yh, int) else pl.multiple_of(yh * 32, 32)
    halves = [ref[x, pl.ds(base, 32)].astype(f32)[:, which * 8 : which * 8 + 8] for ref in cores]
    return jnp.stack(halves, axis=1).reshape(D, 128)


def unit_columns(values):
    scale = lax.rsqrt(jnp.sum(folded(values * values), axis=0, keepdims=True) + 1e-06)
    return (values * scale).astype(bf16), scale


def folded(total):
    return jnp.sum(total.reshape(-1, 8, total.shape[1]), axis=0)


def as_blocks(wide):
    row = jnp.sum(wide, axis=0, keepdims=True)
    return jnp.concatenate([row[:, s * 128 : (s + 1) * 128] for s in range(BLOCKS)], axis=0)


def as_row(blocks):
    return jnp.concatenate([blocks[s : s + 1, :] for s in range(BLOCKS)], axis=1)


def fetch_kernel(far_ref, near_ref, sem_ref):
    copies = []
    for i in range(ROWS // WIDE):
        rows = pl.ds(i * WIDE, WIDE)
        copies.append(pltpu.make_async_copy(far_ref.at[rows], near_ref.at[rows], sem_ref.at[i]))
    for copy in copies:
        copy.start()
    for copy in copies:
        copy.wait()


def first_kernel(
    own_ref, other_ref, weight_ref, kernel_out, near_ref, unit_ref, sent_out, scale_ref, features_ref,
    teacher_ref, stage_ref, sent_ref, mass_ref, sem_ref, sent_sem,
):
    me, core = lax.axis_index("smp"), lax.rem(lax.axis_index("proto"), 2)

    def by_core(body):
        @pl.when(core == 0)
        def _():
            body((own_ref, other_ref))

        @pl.when(core == 1)
        def _():
            body((other_ref, own_ref))

    def teacher_units(cores):
        for s in range(BLOCKS):
            values = features_of(cores, s // 2, s % 2, 0)
            teacher_ref[:, s * 128 : (s + 1) * 128] = unit_columns(values)[0]

    def student_units(cores):
        for s in range(BLOCKS):
            values = features_of(cores, s // 2, s % 2, 1)
            unit, scale = unit_columns(values)
            unit_ref[:, s * 128 : (s + 1) * 128] = unit
            scale_ref[s : s + 1, :] = scale
        features_ref[...] = features_of(cores, me // 2, lax.rem(me, 2), 1)

    def copy_out(i):
        rows = pl.ds(pl.multiple_of(i * WIDE, WIDE), WIDE)
        return pltpu.make_async_copy(stage_ref.at[rows], kernel_out.at[rows], sem_ref.at[i])

    by_core(teacher_units)
    mass_ref[...] = jnp.zeros_like(mass_ref)

    def tile(rows, kept_ref, kept_rows):
        kernel = jnp.exp(
            jnp.dot(weight_ref[rows, :], teacher_ref[...], preferred_element_type=f32) * (1.0 / TEACHER_TEMP)
        )
        kept_ref[kept_rows, :] = kernel
        row_scale = 1.0 / (K * jnp.sum(kernel, axis=1, keepdims=True))
        mass_ref[...] += folded(kernel * row_scale)

    @pl.loop(0, FAR // WIDE)
    def _(i):
        rows = pl.ds(pl.multiple_of(i * WIDE, WIDE), WIDE)
        tile(rows, stage_ref, rows)
        copy_out(i).start()

    tile(pl.ds(FAR, ROWS - FAR), near_ref, pl.ds(0, ROWS - FAR))
    sent_ref[...] = jnp.broadcast_to(as_blocks(mass_ref[...]).astype(bf16)[None], sent_ref.shape)
    sent_copy = pltpu.make_async_copy(sent_ref, sent_out, sent_sem)
    sent_copy.start()
    by_core(student_units)
    sent_copy.wait()
    for i in range(FAR // WIDE):
        copy_out(i).wait()


def student_kernel(
    unit_ref, weight_far, near_ref, kernel_ref, own_out, total_ref, kernel_out,
    weight_ref, stage_ref, own_ref, sum_ref, own_sem, weight_sem, near_sem,
):
    def copy_in(i):
        rows = pl.ds(pl.multiple_of(i * WIDE, WIDE), WIDE)
        return pltpu.make_async_copy(weight_far.at[rows], weight_ref.at[rows], weight_sem.at[i])

    copy_in(0).start()
    near_copy = pltpu.make_async_copy(near_ref, kernel_out.at[pl.ds(FAR, ROWS - FAR)], near_sem)
    sum_ref[...] = jnp.zeros_like(sum_ref)
    lanes = pl.ds(pl.multiple_of(lax.axis_index("smp") * 128, 128), 128)

    def copy_out(i):
        rows = pl.ds(pl.multiple_of(i * WIDE, WIDE), WIDE)
        return pltpu.make_async_copy(own_ref.at[rows], own_out.at[rows], own_sem.at[i])

    @pl.loop(0, ROWS // WIDE)
    def _(i):
        copy_in(i).wait()

        @pl.when(i == 0)
        def _():
            for later in range(1, ROWS // WIDE):
                copy_in(later).start()

        @pl.when(i == 1)
        def _():
            near_copy.start()

        rows = pl.ds(pl.multiple_of(i * WIDE, WIDE), WIDE)
        logits = jnp.dot(weight_ref[rows, :], unit_ref[...], preferred_element_type=f32) * (1.0 / STUDENT_TEMP)
        stage_ref[...] = logits
        own_ref[rows, :] = stage_ref[:, lanes]
        copy_out(i).start()
        sum_ref[...] += folded(jnp.exp(logits))

    total_ref[...] = as_blocks(sum_ref[...])
    for i in range(ROWS // WIDE):
        copy_out(i).wait()
    near_copy.wait()


def received(got_ref):
    return jnp.sum(got_ref[...].astype(f32), axis=0)


def second_kernel(
    got_ref, far_ref, near_ref, total_ref, kernel_ref, sent_ref, kept_ref, col_ref, mass_ref, sem_ref
):
    def copy_in(i):
        rows = pl.ds(pl.multiple_of(i * TILE, TILE), TILE)
        return pltpu.make_async_copy(far_ref.at[rows], kernel_ref.at[rows], sem_ref.at[i])

    for i in range(FAR // TILE):
        copy_in(i).start()
    col_ref[...] = as_row(1.0 / (B * received(got_ref)))
    mass_ref[...] = jnp.zeros_like(mass_ref)

    def add(kernel):
        row_scale = 1.0 / (K * jnp.sum(kernel * col_ref[...], axis=1, keepdims=True))
        mass_ref[...] += folded(kernel * row_scale)

    @pl.loop(0, (ROWS - FAR) // TILE)
    def _(i):
        start = pl.multiple_of(i * TILE, TILE)
        kernel = near_ref[pl.ds(start, TILE), :]
        kernel_ref[pl.ds(FAR + start, TILE), :] = kernel
        add(kernel)

    @pl.loop(0, FAR // TILE)
    def _(i):
        copy_in(i).wait()
        add(kernel_ref[pl.ds(pl.multiple_of(i * TILE, TILE), TILE), :])

    mass = as_blocks(mass_ref[...]).astype(bf16).astype(f32)
    kept_ref[...] = mass
    total = total_ref[...]
    step = jnp.exp2(jnp.floor(jnp.log2(total)) - 7.0)
    place = lax.axis_index("proto").astype(f32)
    spread = total + step * ((place + 0.5) * (1.0 / 64) - 0.5)
    packed = jnp.concatenate([mass, spread], axis=0).astype(bf16)
    sent_ref[...] = jnp.broadcast_to(packed[None], sent_ref.shape)


def split_rows(value):
    high = value.astype(bf16).astype(f32)
    return [high, value - high]


def third_kernel(
    got_ref, kernel_ref, kept_ref, features_ref, logits_far, weight_far,
    sent_ref, total_ref, before_ref, col_ref, mass_ref, scaled_ref, pair_ref, logits_ref, weight_ref, sem_ref,
):
    copies = [pltpu.make_async_copy(logits_far, logits_ref, sem_ref.at[0])]
    for i in range(ROWS // WIDE):
        rows = pl.ds(i * WIDE, WIDE)
        copies.append(pltpu.make_async_copy(weight_far.at[rows], weight_ref.at[rows], sem_ref.at[1 + i]))
    for copy in copies:
        copy.start()
    me = lax.axis_index("smp")
    got = received(got_ref)
    before_ref[...] = got[:8, :]
    total_ref[...] = got[8:, :]
    col_ref[...] = as_row(1.0 / (B * got[:8, :]))
    mass_ref[...] = jnp.zeros_like(mass_ref)
    lanes = pl.ds(pl.multiple_of(me * 128, 128), 128)

    @pl.loop(0, ROWS // TILE)
    def _(i):
        rows = pl.ds(pl.multiple_of(i * TILE, TILE), TILE)
        kernel = kernel_ref[rows, :]
        row_scale = 1.0 / (K * jnp.sum(kernel * col_ref[...], axis=1, keepdims=True))
        scaled_ref[rows, :] = kernel_ref[rows, lanes] * row_scale
        mass_ref[...] += folded(kernel * row_scale)

    change = as_blocks(mass_ref[...]) - kept_ref[...]
    copies[0].wait()
    logits = logits_ref[...]
    own_col = 1.0 / before_ref[pl.ds(me, 1), :]
    own_total = 1.0 / total_ref[pl.ds(me, 1), :]
    targets = scaled_ref[...] * own_col
    weighted = jnp.sum(folded(targets * logits), axis=0, keepdims=True)
    pair_ref[:, :128] = ((jnp.exp(logits) * own_total - targets) * SHARE).astype(bf16)
    pair_ref[:, 128:] = (targets * SHARE).astype(bf16)
    for copy in copies[1:]:
        copy.wait()
    parts = lax.dot_general(
        pair_ref[...], weight_ref[...], (((0,), (0,)), ((), ())), preferred_element_type=f32
    )
    grad_part, target_part = parts[:128, :].T, parts[128:, :].T
    features = features_ref[...]
    inner_grad = jnp.sum(folded(features * grad_part), axis=0, keepdims=True)
    inner_target = jnp.sum(folded(features * target_part), axis=0, keepdims=True)
    extra = jnp.concatenate(
        split_rows(inner_grad) + split_rows(inner_target) + split_rows(weighted) + [jnp.zeros((2, 128), f32)],
        axis=0,
    )

    def everywhere(rows):
        return jnp.broadcast_to(rows[None], (64, 8, 128))

    sent_ref[...] = jnp.concatenate(
        [everywhere(change), grad_part.reshape(64, 8, 128), target_part.reshape(64, 8, 128), everywhere(extra)],
        axis=1,
    ).astype(bf16)


def weight_kernel(
    kernel_ref, weight_ref, total_ref, before_ref, unit_ref, out_ref, near_ref, far_ref, slice_ref, rows_ref
):
    @pl.when(pl.program_id(0) == 0)
    def _():
        rows_ref[0:1, :] = as_row(1.0 / (B * before_ref[...]))
        rows_ref[1:2, :] = as_row(1.0 / before_ref[...])
        rows_ref[2:3, :] = as_row(1.0 / total_ref[...])

    kernel = kernel_ref[...]
    row_scale = 1.0 / (K * jnp.sum(kernel * rows_ref[0:1, :], axis=1, keepdims=True))
    targets = kernel * row_scale * rows_ref[1:2, :]
    logits = jnp.dot(weight_ref[...], unit_ref[...], preferred_element_type=f32) * (1.0 / STUDENT_TEMP)
    probs = jnp.exp(logits) * rows_ref[2:3, :]
    grad = ((probs - targets) * SHARE).astype(bf16)
    shared = (targets * SHARE).astype(bf16)

    @pl.when(pl.program_id(0) < HALF)
    def _():
        near_ref[...] = shared

    @pl.when(pl.program_id(0) >= HALF)
    def _():
        far_ref[...] = shared

    units = unit_ref[pl.ds(pl.multiple_of(lax.axis_index("smp") * 64, 64), 64), :]
    slice_ref[...] = units
    out_ref[...] = lax.dot_general(units, grad, (((1,), (1,)), ((), ())), preferred_element_type=f32)


def final_kernel(
    got_ref, features_ref, scale_ref, total_ref, before_ref, unit_ref, near_ref, held_ref, targets_far,
    features_out, loss_out, weight_out, change_ref, targets_ref, sem_ref,
):
    def copy_in(i):
        rows = pl.ds(i * TILE, TILE)
        return pltpu.make_async_copy(targets_far.at[rows], targets_ref.at[rows], sem_ref.at[i])

    for i in range(ROWS // TILE - HALF):
        copy_in(i).start()
    me = lax.axis_index("smp")
    got = received(got_ref)
    before = before_ref[...]
    change_ref[...] = got[:8] / (before + got[:8])
    own = change_ref[pl.ds(me, 1), :]
    unit_grad = got[8:16] + own * got[16:24]
    inner = (got[24:25] + got[25:26]) + own * (got[26:27] + got[27:28])
    scale = scale_ref[pl.ds(me, 1), :]
    features_out[...] = scale * unit_grad - (scale * scale * scale * inner) * features_ref[...].astype(f32)
    loss_out[...] = jnp.log(total_ref[pl.ds(me, 1), :]) - (1.0 - own) * (got[28:29] + got[29:30])
    moved = (unit_ref[...].astype(f32) * as_row(change_ref[...])).astype(bf16)

    def correct(start, targets):
        rows = pl.ds(start, targets.shape[0])
        weight_out[:, rows] = near_ref[:, rows] + lax.dot_general(
            moved, targets, (((1,), (1,)), ((), ())), preferred_element_type=f32
        )

    for i in range(HALF):
        correct(i * TILE, held_ref[pl.ds(i * TILE, TILE), :])
    for i in range(ROWS // TILE - HALF):
        copy_in(i).wait()
        correct((HALF + i) * TILE, targets_ref[pl.ds(i * TILE, TILE), :])


def shape(dims, dtype=f32):
    return jax.ShapeDtypeStruct(dims, dtype)


def on_device(teacher_features, student_features, teacher_weight, student_weight):
    raw = jnp.concatenate([teacher_features.T, student_features.T], axis=0)
    first = gathered(raw, ("yh", "yl", "z"))
    second = gathered(first, ("x",))
    second, teacher_weight = lax.optimization_barrier((second, teacher_weight))
    other = lax.ppermute(second, "proto", [(i, i ^ 1) for i in range(64)])

    wide_sems, near_sems = pltpu.SemaphoreType.DMA((ROWS // WIDE,)), pltpu.SemaphoreType.DMA((ROWS // TILE,))
    row, rows8 = pltpu.VMEM((1, B), f32), pltpu.VMEM((8, B), f32)
    rows8_small = pltpu.VMEM((8, 128), f32)
    matmul = dict(flops=2 * ROWS * B * D, moved=12 * 2**20, exps=ROWS * B)
    (weight_near,) = call(
        fetch_kernel, [pltpu.VMEM((ROWS, D), bf16)], [ANY], None, [wide_sems], moved=4 * 2**20
    )(far(teacher_weight))
    kernel, kernel_end, student_unit, sent_1, student_scale, features_own = call(
        first_kernel,
        [pltpu.HBM((ROWS, B), f32), pltpu.VMEM((ROWS - FAR, B), f32), shape((D, B), bf16),
         pltpu.HBM((64, 8, 128), bf16), shape((8, 128)),
         shape((D, 128))],
        [VMEM, VMEM, VMEM],
        [ANY, VMEM, VMEM, ANY, VMEM, VMEM],
        [pltpu.VMEM((D, B), bf16), pltpu.VMEM((FAR, B), f32), pltpu.VMEM((64, 8, 128), bf16), rows8, wide_sems,
         pltpu.SemaphoreType.DMA],
        **matmul,
    )(second, other, weight_near)
    got_1 = sent_to_protos(sent_1)
    logits_own, local_total, kernel = call(
        student_kernel,
        [pltpu.HBM((ROWS, 128), f32), shape((8, 128)), pltpu.HBM((ROWS, B), f32)],
        [VMEM, ANY, VMEM, ANY],
        [ANY, VMEM, ANY],
        [pltpu.VMEM((ROWS, D), bf16), pltpu.VMEM((WIDE, B), f32), pltpu.VMEM((ROWS, 128), f32), rows8, wide_sems,
         wide_sems, pltpu.SemaphoreType.DMA],
        {3: 2},
        **matmul,
    )(student_unit, far(student_weight), kernel_end, far(kernel))
    kernel_near, sent_2, kept = call(
        second_kernel,
        [pltpu.VMEM((ROWS, B), f32), shape((64, 16, 128), bf16), shape((8, 128))],
        [VMEM, ANY, VMEM, VMEM],
        None,
        [row, rows8, near_sems],
        flops=4 * ROWS * B,
        moved=8 * 2**20,
    )(got_1, far(kernel), kernel_end, local_total)
    got_2 = sent_to_protos(sent_2)
    sent_3, total, before = call(
        third_kernel,
        [shape((64, 32, 128), bf16), shape((8, 128)), shape((8, 128))],
        [VMEM] * 4 + [ANY] * 2,
        None,
        [row, rows8, pltpu.VMEM((ROWS, 128), f32), pltpu.VMEM((ROWS, 256), bf16), pltpu.VMEM((ROWS, 128), f32),
         pltpu.VMEM((ROWS, D), bf16), pltpu.SemaphoreType.DMA((1 + ROWS // WIDE,))],
        flops=2 * ROWS * 256 * D,
        moved=12 * 2**20,
        exps=ROWS * 128,
    )(got_2, kernel_near, kept, features_own, far(logits_own), far(student_weight))
    got_3 = sent_to_protos(sent_3)
    partial, targets_near, targets_far, unit_slice = streamed(
        weight_kernel,
        [shape((64, ROWS)), pltpu.VMEM((HALF * TILE, B), bf16), pltpu.HBM((ROWS - HALF * TILE, B), bf16),
         shape((64, B), bf16)],
        [stripe(B), stripe(D), whole(8, 128), whole(8, 128), whole(D, B)],
        [pl.BlockSpec((64, TILE), lambda i: (0, i)),
         pl.BlockSpec((TILE, B), lambda i: (jnp.minimum(i, HALF - 1), 0)),
         pl.BlockSpec((TILE, B), lambda i: (jnp.maximum(i - HALF, 0), 0)), whole(64, B)],
        [rows8],
        flops=2 * ROWS * B * (64 + D),
        moved=15 * 2**20,
        exps=ROWS * B,
    )(far(kernel), far(student_weight), total, before, far(student_unit))
    grad_features, loss, grad_weight = call(
        final_kernel,
        [shape((8, 128)), shape((1, 128)), shape((64, ROWS))],
        [VMEM] * 8 + [ANY],
        None,
        [rows8_small, pltpu.VMEM((ROWS - HALF * TILE, B), bf16), near_sems],
        flops=2 * ROWS * B * 64,
        moved=5 * 2**20,
    )(
        got_3, student_features.T, student_scale, total, before, unit_slice, partial, targets_near,
        far(targets_far),
    )
    return loss.reshape(128), grad_features.T, grad_weight.T


def solution(mesh):
    placed = (P("smp", "proto"), P("smp", "proto"), P("proto", None), P("proto", None))
    return jax.shard_map(
        on_device,
        mesh=mesh,
        in_specs=placed,
        out_specs=(P("smp"), P("smp", "proto"), P("proto", "smp")),
        check_vma=False,
    )
```
